32 devices in a mesh: grp: 2 (over x), wide: 16 (over z, y, core).
Axes of the slice: x: 2, y: 2, z: 4, core: 2. Of those that a mesh axis runs over, the one named last changes fastest.
Arguments:
- residual_in: bfloat16 [6, 16, 5120], P('grp', None, 'wide'), parts along dimension 0, may hold values from -1.5 to 1.5
- norm_gain: bfloat16 [5120], replicated, may hold values from 0.099609375 to 1.8984375
- gate_weight: bfloat16 [5120, 16384], P('wide'), may hold values from -0.078125 to 0.078125
- up_weight: bfloat16 [5120, 16384], P('wide'), may hold values from -0.078125 to 0.078125
- down_weight: bfloat16 [16384, 5120], P(None, 'wide'), may hold values from -0.046875 to 0.046875
- out_weight: bfloat16 [8192, 5120], P('wide'), may hold values from -0.5 to 0.5
- queries: bfloat16 [6, 16, 8, 8, 128], P('grp', 'wide'), parts along dimension 0, may hold values from -6 to 6
- kv_cache: bfloat16 [2, 32, 8, 512, 128], P(None, ('grp', 'wide')), parts along dimension 1, may hold values from -6 to 6
- new_kv: bfloat16 [6, 2, 16, 8, 128], P('grp', None, 'wide'), parts along dimension 0, may hold values from -6 to 6
- cache_len: int32 [32], P('grp'), parts along dimension 0, may hold values from 1 to 512, 4096 in all
Outputs:
- ffn_out: bfloat16 [6, 16, 5120], P('grp', 'wide'), parts along dimension 0
- attn_out: bfloat16 [6, 16, 8, 8, 128], P('grp', 'wide'), parts along dimension 0
- hidden: bfloat16 [6, 16, 5120], P('grp', 'wide'), parts along dimension 0
The draws below stay inside these ranges and needn't reach their ends.
There are 2 independent parts, one for each index of `grp`. The reference program is written for one: setup_inputs(seed, part) draws one part's arguments, and reference() takes and returns one part's arrays. A program takes and returns all parts, laid end to end along the dimension named above; an argument that names none is the same for every part. Nothing has to cross between parts.
All inputs are finite; a program needn't handle non-finite values. Where the reference program divides by a largest or mean magnitude, that divisor is 1e-20 or more.
Results may differ from the reference program's by a relative error of at most 0.0095.
Values may be sent and summed in bfloat16 or wider, within the bound.
No kernel may reach another device: no remote copies, remote signals or barrier semaphores. Data moves between devices by JAX's collectives and lax.ppermute only.
A program may use at most 256 MiB of HBM per device.

```python
import math
import jax
import jax.numpy as jnp
import numpy as np
from jax import lax

D = 5120
FFW = 16384
BLOCK = 128
QMAX = 448
HD = 128
KVH = 8
QPK = 8
STEPS = 3
CACHE = 512
SEQS = 16
QDIM = 8192


def draw_queries(key, part):
    key = jax.random.fold_in(key, 1)
    base = jnp.clip(jax.random.normal(key, (STEPS, SEQS, KVH, QPK, HD), jnp.float32), -4.0, 4.0)
    return base.astype(jnp.bfloat16)


def draw_kv_cache(key, part):
    key = jax.random.fold_in(key, 2)
    base = jnp.clip(jax.random.normal(key, (2, SEQS, KVH, CACHE, HD), jnp.float32), -4.0, 4.0)
    return base.astype(jnp.bfloat16)


def level_of(rng, shape, split, low, high):
    loudness = 1.0
    for axis_at, shards_of in split:
        heights = jax.random.uniform(jax.random.fold_in(jax.random.fold_in(rng, 6), axis_at), (shards_of,), jnp.float32, low / len(split), high / len(split))
        loudness = loudness * jnp.repeat(jnp.exp(heights), shape[axis_at] // shards_of).reshape((-1,) + (1,) * (len(shape) - 1 - axis_at))
    return loudness


def length_profile(number_of, total, most, skew):
    loads = [(1 << 20) // math.isqrt(standing ** skew) + 1 for standing in range(2, number_of + 1)]
    surplus, given = total - most - (number_of - 1), [1] * (number_of - 1)
    while surplus > 0:
        candidates = [i for i in range(number_of - 1) if given[i] < most]
        mass, budget = sum([loads[i] for i in candidates]), surplus
        for i in candidates:
            more = min(most - given[i], max(1, budget * loads[i] // mass), surplus)
            given[i] = given[i] + more
            surplus = surplus - more
    return np.array([most] + given)


def ragged_sizes(key, count, total, reach, skew):
    if count == 2:
        one = jax.random.randint(key, (), max(1, total - reach), min(reach, total - 1) + 1)
        return jnp.stack([one, total - one])
    tallies = jnp.asarray(length_profile(count, total, reach, skew), jnp.int32)
    pairs = (count - 1) // 2
    source_of, taker = tallies[1:1 + 2 * pairs:2], tallies[2:2 + 2 * pairs:2]
    margin = jnp.minimum(source_of - 1, reach - taker)
    passed = jax.random.randint(jax.random.fold_in(key, 1), (pairs,), 0, 1 << 20) % (margin + 1)
    tallies = tallies.at[1:1 + 2 * pairs:2].set(source_of - passed).at[2:2 + 2 * pairs:2].set(taker + passed)
    return tallies[jax.random.permutation(jax.random.fold_in(key, 2), count)]


def centred(own_key, dims, scale, bound, cuts=(), kind=jnp.bfloat16):
    factor_of = level_of(own_key, dims, cuts, -0.22, 0.18) if cuts else 1.0
    result = jax.random.normal(own_key, dims, jnp.float32) * scale * factor_of
    return jnp.minimum(jnp.maximum(result, -bound), bound).astype(kind)


def setup_inputs(seed: int = 0, part: int = 0) -> dict:
    splits = jax.random.split(jax.random.key(seed), 11)
    part_keys = jax.random.split(jax.random.fold_in(splits[10], part), 11)
    return {
        "residual_in": centred(part_keys[0], (STEPS, SEQS, D), 0.25, 1.5, ((2, 16),)),
        "norm_gain": jnp.clip(1.0 + 0.18 * jax.random.normal(splits[1], (D,), jnp.float32), 0.099609375, 1.8984375).astype(jnp.bfloat16),
        "gate_weight": centred(splits[2], (D, FFW), D ** -0.5, 0.078125, ((0, 16),)),
        "up_weight": centred(splits[3], (D, FFW), D ** -0.5, 0.078125, ((0, 16),)),
        "down_weight": centred(splits[4], (FFW, D), FFW ** -0.5, 0.046875, ((1, 16),)),
        "out_weight": centred(splits[5], (QDIM, D), HD ** -0.5, 0.5, ((0, 16),)),
        "queries": draw_queries(jax.random.fold_in(jax.random.fold_in(splits[10], part), 71), part),
        "kv_cache": draw_kv_cache(jax.random.fold_in(jax.random.fold_in(splits[10], part), 71), part),
        "new_kv": centred(part_keys[8], (STEPS, 2, SEQS, KVH, HD), 1.0, 6.0, ((2, 16),)),
        "cache_len": ragged_sizes(part_keys[9], SEQS, SEQS * CACHE // 2, CACHE, 1).astype(jnp.int32),
    }


EPS_NORM = 1e-06
EPS_SCALE = 1e-06
NEG = -1e+30

def float_grid(values):
    magnitude = jnp.abs(values)
    spacing = jnp.full_like(values, 2.0 ** (-9))
    for exponent in range(-5, 9):
        spacing = jnp.where(magnitude >= 2.0 ** exponent, spacing * 2.0, spacing)
    return jnp.floor(values / spacing + 0.5) * spacing

def quantize(weight):
    rows, cols = weight.shape
    blocks = weight.astype(jnp.float32).reshape(rows // BLOCK, BLOCK, cols // BLOCK, BLOCK)
    largest = lax.optimization_barrier(jnp.max(jnp.abs(blocks), axis=(1, 3))) + EPS_SCALE
    levels = float_grid(blocks * QMAX / largest[:, None, :, None])
    return (levels.reshape(rows, cols).astype(jnp.bfloat16), largest / QMAX)

def block_product(left, levels, scale):
    count = left.shape[0]
    inner = levels.shape[0] // BLOCK
    lhs = left.astype(jnp.float32).reshape(count, inner, BLOCK)

    def column_block(index):
        cols = lax.dynamic_slice_in_dim(levels, index * BLOCK, BLOCK, 1)
        cols = cols.astype(jnp.float32).reshape(inner, BLOCK, BLOCK)
        part = jnp.einsum('rki,kic->rkc', lhs, cols)
        return jnp.einsum('rkc,k->rc', part, scale[:, index])
    out = lax.map(column_block, jnp.arange(levels.shape[1] // BLOCK, dtype=jnp.int32))
    return jnp.transpose(out, (1, 0, 2)).reshape(count, levels.shape[1])

def attention(queries, kv_cache, new_kv, live):
    factor = HD ** (-0.5)
    keys = kv_cache[0].astype(jnp.float32)
    values = kv_cache[1].astype(jnp.float32)
    new_keys = new_kv[:, 0].astype(jnp.float32)
    new_values = new_kv[:, 1].astype(jnp.float32)
    position = jnp.arange(keys.shape[2], dtype=jnp.int32)
    valid = position[None, None, None, :] < live[:, None, None, None]
    results = []
    for step in range(STEPS):
        query = queries[step].astype(jnp.float32)
        cached = jnp.einsum('shqd,shcd->shqc', query, keys) * factor
        recent = jnp.einsum('shqd,tshd->shqt', query, new_keys) * factor
        fresh = (jnp.arange(STEPS, dtype=jnp.int32) <= step)[None, None, None, :]
        top = jnp.maximum(lax.optimization_barrier(jnp.max(jnp.where(valid, cached, NEG), axis=-1)), lax.optimization_barrier(jnp.max(jnp.where(fresh, recent, NEG), axis=-1)))[..., None]
        e_cached = jnp.where(valid, jnp.exp(cached - top), 0.0)
        e_recent = jnp.where(fresh, jnp.exp(recent - top), 0.0)
        total = lax.optimization_barrier(jnp.sum(e_cached, axis=-1, keepdims=True)) + lax.optimization_barrier(jnp.sum(e_recent, axis=-1, keepdims=True))
        p_cached = (e_cached / total).astype(jnp.bfloat16).astype(jnp.float32)
        p_recent = (e_recent / total).astype(jnp.bfloat16).astype(jnp.float32)
        mixed = jnp.einsum('shqc,shcd->shqd', p_cached, values) + jnp.einsum('shqt,tshd->shqd', p_recent, new_values)
        results.append(mixed.astype(jnp.bfloat16))
    return jnp.stack(results)

def reference(residual_in, norm_gain, gate_weight, up_weight, down_weight, out_weight, queries, kv_cache, new_kv, cache_len):
    attn_out = attention(queries, kv_cache, new_kv, cache_len)
    out_levels, out_scale = quantize(out_weight)
    projected = block_product(attn_out.reshape(STEPS * SEQS, QDIM), out_levels, out_scale).reshape(STEPS, SEQS, D)
    hidden = (residual_in.astype(jnp.float32) + projected).astype(jnp.bfloat16)
    states = hidden.astype(jnp.float32)
    power = lax.optimization_barrier(jnp.mean(states * states, axis=-1, keepdims=True))
    normed = (states * lax.rsqrt(power + EPS_NORM) * norm_gain.astype(jnp.float32)).astype(jnp.bfloat16)
    rows_all = normed.reshape(STEPS * SEQS, D)
    gate_levels, gate_scale = quantize(gate_weight)
    up_levels, up_scale = quantize(up_weight)
    down_levels, down_scale = quantize(down_weight)
    gate = block_product(rows_all, gate_levels, gate_scale)
    up = block_product(rows_all, up_levels, up_scale)
    act = (jax.nn.silu(gate) * up).astype(jnp.bfloat16)
    ffn_out = block_product(act, down_levels, down_scale).astype(jnp.bfloat16).reshape(STEPS, SEQS, D)
    return (ffn_out, attn_out, hidden)
```

```python
import functools
import math

import jax
import jax.numpy as jnp
from jax import lax
from jax.experimental import pallas as pl
from jax.experimental.pallas import tpu as pltpu
from jax.sharding import PartitionSpec as P

BLOCK = 128
QMAX = 448.0
EPS_NORM = 1e-06
EPS_SCALE = 1e-06
NEG = -1e30
LANES = 128
VMEM = 56 * 2**20

f32 = jnp.float32
bf16 = jnp.bfloat16
f8 = jnp.float8_e4m3fn


def params(**more):
    return pltpu.CompilerParams(vmem_limit_bytes=VMEM, **more)


def cost(flops, read):
    return pl.CostEstimate(flops=int(flops), bytes_accessed=int(read), transcendentals=0)


def row_chunk_max(weight, chunk, tile):
    rows, cols = weight.shape
    parts = rows // chunk

    def kernel(w_ref, o_ref):
        for j in range(parts):
            o_ref[pl.ds(j, 1), :] = jnp.max(
                jnp.abs(w_ref[pl.ds(j * chunk, chunk), :]), axis=0, keepdims=True
            ).astype(f32)
        for g in range(tile // LANES):
            at = pl.ds(g * LANES, LANES)
            top = jnp.max(o_ref[:, at], axis=1, keepdims=True)
            o_ref[:, at] = jnp.broadcast_to(top, (parts, LANES))

    return pl.pallas_call(
        kernel,
        grid=(cols // tile,),
        in_specs=[pl.BlockSpec((rows, tile), lambda i: (0, i))],
        out_specs=pl.BlockSpec((parts, tile), lambda i: (0, i)),
        out_shape=jax.ShapeDtypeStruct((parts, cols), f32),
        compiler_params=params(),
        cost_estimate=cost(2 * rows * cols, 2 * rows * cols),
        name="row_chunk_max",
    )(weight)


def col_chunk_max(weight, chunk, tile):
    rows, cols = weight.shape
    per = tile // BLOCK

    def kernel(w_ref, o_ref):
        for j in range(per):
            o_ref[pl.ds(j, 1), :] = jnp.max(
                jnp.abs(w_ref[pl.ds(j * BLOCK, BLOCK), :]), axis=0, keepdims=True
            ).astype(f32)
        tops = o_ref[...]
        column = lax.broadcasted_iota(jnp.int32, (per, cols), 1) // chunk
        spread = jnp.zeros((per, cols), f32)
        for q in range(cols // chunk):
            here = column == q
            top = jnp.max(jnp.where(here, tops, 0.0), axis=1, keepdims=True)
            spread = jnp.where(here, top, spread)
        o_ref[...] = spread

    return pl.pallas_call(
        kernel,
        grid=(rows // tile,),
        in_specs=[pl.BlockSpec((tile, cols), lambda i: (i, 0))],
        out_specs=pl.BlockSpec((per, cols), lambda i: (i, 0)),
        out_shape=jax.ShapeDtypeStruct((rows // BLOCK, cols), f32),
        compiler_params=params(),
        cost_estimate=cost(2 * rows * cols, 2 * rows * cols),
        name="col_chunk_max",
    )(weight)


def join_group(parts, size, dim):
    count = lax.axis_size("wide")
    me = lax.axis_index("wide")
    share = parts.shape[dim]
    shape = list(parts.shape)
    shape[dim] = share * size
    out = jnp.zeros(shape, parts.dtype)
    out = lax.dynamic_update_slice_in_dim(out, parts, (me % size) * share, dim)
    for step in range(1, size):
        perm = [(i // size * size + (i + step) % size, i) for i in range(count)]
        got = lax.ppermute(parts, "wide", perm)
        out = lax.dynamic_update_slice_in_dim(out, got, ((me + step) % size) * share, dim)
    return out


def row_scales(tops, chunk, rows):
    size = math.lcm(rows, BLOCK) // rows
    per = BLOCK // chunk
    own = tops.shape[0]
    if size > 1:
        joined = join_group(tops, size, 0)
    else:
        joined = tops
    blocks = joined.reshape(size * own // per, per, -1)
    joined = jnp.broadcast_to(jnp.max(blocks, axis=1, keepdims=True), blocks.shape)
    joined = joined.reshape(size * own, -1)
    if size > 1:
        joined = lax.dynamic_slice_in_dim(
            joined, (lax.axis_index("wide") % size) * own, own, 0
        )
    largest = joined + EPS_SCALE
    return QMAX / largest, largest / QMAX


def col_scales(tops, cols):
    size = math.lcm(cols, BLOCK) // cols
    joined = join_group(tops, size, 1) if size > 1 else tops
    blocks = joined.reshape(joined.shape[0], -1, BLOCK)
    joined = jnp.broadcast_to(jnp.max(blocks, axis=2, keepdims=True), blocks.shape)
    joined = joined.reshape(joined.shape[0], -1)
    if size > 1:
        joined = lax.dynamic_slice_in_dim(
            joined, (lax.axis_index("wide") % size) * cols, cols, 1
        )
    largest = joined + EPS_SCALE
    return QMAX / largest, largest / QMAX


def row_levels(weight, factor, chunk, tile):
    rows, cols = weight.shape
    parts = rows // chunk

    def kernel(w_ref, f_ref, o_ref):
        for j in range(parts):
            at = pl.ds(j * chunk, chunk)
            o_ref[at, :] = (w_ref[at, :].astype(f32) * f_ref[pl.ds(j, 1), :]).astype(f8)

    return pl.pallas_call(
        kernel,
        grid=(cols // tile,),
        in_specs=[
            pl.BlockSpec((rows, tile), lambda i: (0, i)),
            pl.BlockSpec((parts, tile), lambda i: (0, i)),
        ],
        out_specs=pl.BlockSpec((rows, tile), lambda i: (0, i)),
        out_shape=jax.ShapeDtypeStruct((rows, cols), f8),
        compiler_params=params(),
        cost_estimate=cost(4 * rows * cols, 3 * rows * cols),
        name="row_levels",
    )(weight, factor)


def col_levels(weight, factor, tile):
    rows, cols = weight.shape
    per = tile // BLOCK

    def kernel(w_ref, f_ref, o_ref):
        for j in range(per):
            at = pl.ds(j * BLOCK, BLOCK)
            o_ref[at, :] = (w_ref[at, :].astype(f32) * f_ref[pl.ds(j, 1), :]).astype(f8)

    return pl.pallas_call(
        kernel,
        grid=(rows // tile,),
        in_specs=[
            pl.BlockSpec((tile, cols), lambda i: (i, 0)),
            pl.BlockSpec((per, cols), lambda i: (i, 0)),
        ],
        out_specs=pl.BlockSpec((tile, cols), lambda i: (i, 0)),
        out_shape=jax.ShapeDtypeStruct((rows, cols), f8),
        compiler_params=params(),
        cost_estimate=cost(4 * rows * cols, 3 * rows * cols),
        name="col_levels",
    )(weight, factor)


def scaled_rows(x_ref, l_ref, s_ref, chunk, parts):
    total = None
    for j in range(parts):
        at = pl.ds(j * chunk, chunk)
        part = jnp.dot(x_ref[:, at], l_ref[at, :].astype(bf16), preferred_element_type=f32)
        part = part * s_ref[pl.ds(j, 1), :]
        total = part if total is None else total + part
    return total


def out_product(left, levels, scale, chunk, owners):
    count, rows = left.shape
    cols = levels.shape[1]
    parts = rows // chunk
    share = cols // owners
    tile = math.lcm(share, LANES)
    per = tile // share

    def kernel(x_ref, l_ref, s_ref, o_ref):
        total = scaled_rows(x_ref, l_ref, s_ref, chunk, parts).astype(bf16)
        for q in range(per):
            o_ref[q] = total[:, q * share : (q + 1) * share]

    return pl.pallas_call(
        kernel,
        grid=(cols // tile,),
        in_specs=[
            pl.BlockSpec((count, rows), lambda i: (0, 0)),
            pl.BlockSpec((rows, tile), lambda i: (0, i)),
            pl.BlockSpec((parts, tile), lambda i: (0, i)),
        ],
        out_specs=pl.BlockSpec((per, count, share), lambda i: (i, 0, 0)),
        out_shape=jax.ShapeDtypeStruct((owners, count, share), bf16),
        compiler_params=params(),
        cost_estimate=cost(2 * count * rows * cols, rows * cols),
        name="out_product",
    )(left, levels, scale)


def gate_up_product(core, left, gate, gate_scale, up, up_scale, power, chunk, owners):
    count, rows = left.shape
    parts = rows // chunk
    share = gate.shape[1] // owners
    chips = owners // 2

    def kernel(core_ref, x_ref, g_ref, gs_ref, u_ref, us_ref, p_ref, o_ref):
        o_ref[0, 0, :, pl.ds(0, share)] = scaled_rows(x_ref, g_ref, gs_ref, chunk, parts).astype(
            bf16
        )
        o_ref[0, 0, :, pl.ds(share, share)] = scaled_rows(
            x_ref, u_ref, us_ref, chunk, parts
        ).astype(bf16)
        o_ref[0, 0, :, pl.ds(2 * share, LANES)] = p_ref[...]

    def owner(i, core_ref):
        return (0, 2 * (i % chips) + (core_ref[0] + i // chips) % 2)

    fixed = lambda i, core_ref: (0, 0)
    return pl.pallas_call(
        kernel,
        grid_spec=pltpu.PrefetchScalarGridSpec(
            num_scalar_prefetch=1,
            grid=(owners,),
            in_specs=[
                pl.BlockSpec((count, rows), fixed),
                pl.BlockSpec((rows, share), owner),
                pl.BlockSpec((parts, share), owner),
                pl.BlockSpec((rows, share), owner),
                pl.BlockSpec((parts, share), owner),
                pl.BlockSpec((count, LANES), fixed),
            ],
            out_specs=pl.BlockSpec(
                (1, 1, count, 2 * share + LANES),
                lambda i, core_ref: (i // chips, i % chips, 0, 0),
            ),
        ),
        out_shape=jax.ShapeDtypeStruct((2, chips, count, 2 * share + LANES), bf16),
        compiler_params=params(),
        cost_estimate=cost(4 * count * rows * share * owners, 2 * rows * share * owners),
        name="gate_up_product",
    )(core, left, gate, gate_scale, up, up_scale, power)


def down_product(core, same, other, levels, scale):
    chips, count, share = same.shape
    rows, cols = levels.shape
    blocks = share // BLOCK
    group = max(1, 8 * BLOCK // (2 * share))

    def kernel(core_ref, a_ref, b_ref, l_ref, s_ref, o_ref, acc_ref):
        i = pl.program_id(0)

        @pl.when(i == 0)
        def _():
            acc_ref[...] = jnp.zeros_like(acc_ref)

        core_at = core_ref[0]
        total = acc_ref[...]
        for n in range(group):
            for side, ref in ((core_at, a_ref), (1 - core_at, b_ref)):
                for j in range(blocks):
                    block = (2 * n + side) * blocks + j
                    at = pl.ds(pl.multiple_of(block * BLOCK, BLOCK), BLOCK)
                    part = jnp.dot(
                        ref[n, :, pl.ds(j * BLOCK, BLOCK)],
                        l_ref[at, :].astype(bf16),
                        preferred_element_type=f32,
                    )
                    total = total + part * s_ref[pl.ds(block, 1), :]
        acc_ref[...] = total

        @pl.when(i == chips // group - 1)
        def _():
            o_ref[...] = acc_ref[...].astype(bf16)

    return pl.pallas_call(
        kernel,
        grid_spec=pltpu.PrefetchScalarGridSpec(
            num_scalar_prefetch=1,
            grid=(chips // group,),
            in_specs=[
                pl.BlockSpec((group, count, share), lambda i, c: (i, 0, 0)),
                pl.BlockSpec((group, count, share), lambda i, c: (i, 0, 0)),
                pl.BlockSpec((2 * group * share, cols), lambda i, c: (i, 0)),
                pl.BlockSpec((2 * group * blocks, cols), lambda i, c: (i, 0)),
            ],
            out_specs=pl.BlockSpec((count, cols), lambda i, c: (0, 0)),
            scratch_shapes=[pltpu.VMEM((count, cols), f32)],
        ),
        out_shape=jax.ShapeDtypeStruct((count, cols), bf16),
        compiler_params=params(),
        cost_estimate=cost(2 * count * rows * cols, rows * cols),
        name="down_product",
    )(core, same, other, levels, scale)


def attention(queries, kv_cache, new_kv, live):
    steps = queries.shape[0]
    factor = queries.shape[-1] ** (-0.5)
    keys = kv_cache[0]
    values = kv_cache[1]
    new_keys = new_kv[:, 0]
    new_values = new_kv[:, 1]
    position = jnp.arange(keys.shape[2], dtype=jnp.int32)
    valid = position[None, None, None, None, :] < live[None, :, None, None, None]
    cached = (
        jnp.einsum("nshqd,shcd->nshqc", queries, keys, preferred_element_type=f32) * factor
    )
    recent = (
        jnp.einsum("nshqd,tshd->nshqt", queries, new_keys, preferred_element_type=f32) * factor
    )
    order = jnp.arange(steps, dtype=jnp.int32)
    fresh = (order[None, :] <= order[:, None])[:, None, None, None, :]
    top = jnp.maximum(
        jnp.max(jnp.where(valid, cached, NEG), axis=-1),
        jnp.max(jnp.where(fresh, recent, NEG), axis=-1),
    )[..., None]
    e_cached = jnp.where(valid, jnp.exp(cached - top), 0.0)
    e_recent = jnp.where(fresh, jnp.exp(recent - top), 0.0)
    total = jnp.sum(e_cached, axis=-1, keepdims=True) + jnp.sum(e_recent, axis=-1, keepdims=True)
    p_cached = (e_cached / total).astype(bf16)
    p_recent = (e_recent / total).astype(bf16)
    mixed = jnp.einsum("nshqc,shcd->nshqd", p_cached, values, preferred_element_type=f32)
    mixed = mixed + jnp.einsum(
        "nshqt,tshd->nshqd", p_recent, new_values, preferred_element_type=f32
    )
    return mixed.astype(bf16)


def swap_cores(value):
    count = lax.axis_size("wide")
    return lax.ppermute(value, "wide", [(i, i ^ 1) for i in range(count)])


def exchange(value):
    return lax.all_to_all(value, "wide", split_axis=0, concat_axis=0, tiled=True)


def exchange_chips(value):
    count = lax.axis_size("wide")
    groups = [list(range(core, count, 2)) for core in range(2)]
    return lax.all_to_all(
        value, "wide", split_axis=0, concat_axis=0, tiled=True, axis_index_groups=groups
    )


def on_device(
    residual_in,
    norm_gain,
    gate_weight,
    up_weight,
    down_weight,
    out_weight,
    queries,
    kv_cache,
    new_kv,
    cache_len,
):
    owners = lax.axis_size("wide")
    me = lax.axis_index("wide")
    core = (me % 2).astype(jnp.int32).reshape(1)
    steps, seqs, width_dev = residual_in.shape
    seq_dev = seqs // owners
    tokens = steps * seqs
    mine = steps * seq_dev
    width = width_dev * owners

    live = lax.dynamic_slice_in_dim(cache_len, me * seq_dev, seq_dev, 0)
    attn_out = attention(queries, kv_cache, new_kv, live)
    heads = attn_out.reshape(steps, seq_dev, owners, -1)
    heads = exchange(jnp.transpose(heads, (2, 1, 0, 3)))
    heads = heads.reshape(tokens, -1)

    out_rows = out_weight.shape[0]
    out_chunk = math.gcd(out_rows, BLOCK)
    out_tops = row_chunk_max(out_weight, out_chunk, math.lcm(width_dev, LANES))
    out_factor, out_scale = row_scales(out_tops, out_chunk, out_rows)
    out_levels = row_levels(out_weight, out_factor, out_chunk, math.lcm(width_dev, LANES))

    projected = out_product(heads, out_levels, out_scale, out_chunk, owners)
    projected = jnp.sum(exchange(projected).astype(f32), axis=0)
    residual = jnp.transpose(residual_in, (1, 0, 2)).reshape(tokens, width_dev)
    hidden = (residual.astype(f32) + projected).astype(bf16)

    hidden_out = exchange(hidden.reshape(owners, mine, width_dev))
    hidden_out = jnp.transpose(
        hidden_out.reshape(owners, seq_dev, steps, width_dev), (2, 1, 0, 3)
    ).reshape(steps, seq_dev, width)

    rows = gate_weight.shape[0]
    chunk = math.gcd(rows, BLOCK)
    tile = 1024
    gate_factor, gate_scale = row_scales(row_chunk_max(gate_weight, chunk, tile), chunk, rows)
    up_factor, up_scale = row_scales(row_chunk_max(up_weight, chunk, tile), chunk, rows)
    gate_levels = row_levels(gate_weight, gate_factor, chunk, tile)
    up_levels = row_levels(up_weight, up_factor, chunk, tile)

    states = hidden.astype(f32)
    gain = lax.dynamic_slice_in_dim(norm_gain, me * width_dev, width_dev, 0).astype(f32)
    scaled = (states * gain).astype(bf16)
    squares = jnp.sum(states * states, axis=1, keepdims=True)
    high = squares.astype(bf16)
    low = (squares - high.astype(f32)).astype(bf16)
    lane = lax.broadcasted_iota(jnp.int32, (tokens, LANES), 1)
    power = jnp.where(lane == 0, high, jnp.where(lane == 1, low, jnp.zeros_like(low)))

    partial = gate_up_product(
        core, scaled, gate_levels, gate_scale, up_levels, up_scale, power, chunk, owners
    )
    other = swap_cores(partial[1])
    chip_sum = (partial[0].astype(f32) + other.astype(f32)).astype(bf16)
    summed = jnp.sum(exchange_chips(chip_sum).astype(f32), axis=0)
    share = gate_weight.shape[1] // owners
    total = summed[:, 2 * share : 2 * share + 1] + summed[:, 2 * share + 1 : 2 * share + 2]
    scale = lax.rsqrt(total / width + EPS_NORM)
    gate = summed[:, :share] * scale
    up = summed[:, share : 2 * share] * scale
    act = (jax.nn.silu(gate) * up).astype(bf16)

    down_rows, down_cols = down_weight.shape
    down_chunk = math.gcd(down_cols, BLOCK)
    down_factor, down_scale = col_scales(col_chunk_max(down_weight, down_chunk, 1024), down_cols)
    down_levels = col_levels(down_weight, down_factor, 1024)
    same = exchange_chips(jnp.broadcast_to(act[None], (owners // 2,) + act.shape))
    other = swap_cores(same)
    ffn = down_product(core, same, other, down_levels, down_scale)
    ffn = exchange(ffn.reshape(owners, mine, width_dev))
    ffn_out = jnp.transpose(
        ffn.reshape(owners, seq_dev, steps, width_dev), (2, 1, 0, 3)
    ).reshape(steps, seq_dev, width)
    return (ffn_out, attn_out, hidden_out)


def solution(mesh):
    placed = (
        P("grp", None, "wide"),
        P(),
        P("wide", None),
        P("wide", None),
        P(None, "wide"),
        P("wide", None),
        P("grp", "wide", None, None, None),
        P(None, ("grp", "wide"), None, None, None),
        P("grp", None, "wide", None, None),
        P("grp"),
    )
    return jax.shard_map(
        on_device,
        mesh=mesh,
        in_specs=placed,
        out_specs=(
            P("grp", "wide", None),
            P("grp", "wide", None, None, None),
            P("grp", "wide", None),
        ),
        check_vma=False,
    )
```

```python
import functools
import math

import jax
import jax.numpy as jnp
from jax import lax
from jax.experimental import pallas as pl
from jax.experimental.pallas import tpu as pltpu
from jax.sharding import PartitionSpec as P

BLOCK = 128
QMAX = 448.0
EPS_NORM = 1e-06
EPS_SCALE = 1e-06
NEG = -1e30
LANES = 128
VMEM = 56 * 2**20

f32 = jnp.float32
bf16 = jnp.bfloat16
f8 = jnp.float8_e4m3fn


def params(**more):
    return pltpu.CompilerParams(vmem_limit_bytes=VMEM, **more)


def cost(flops, read):
    return pl.CostEstimate(flops=int(flops), bytes_accessed=int(read), transcendentals=0)


def pick_tile(cols, most):
    tile = most
    while cols % tile:
        tile -= LANES
    return tile


def chunk_max(weights, chunk, tile):
    rows, cols = weights[0].shape
    parts = rows // chunk
    count = len(weights)

    def kernel(*refs):
        o_ref = refs[count]
        for a in range(count):
            tops = [
                jnp.max(
                    jnp.abs(refs[a][pl.ds(j * chunk, chunk), :]), axis=0, keepdims=True
                ).astype(f32)
                for j in range(parts)
            ]
            tops = jnp.concatenate(tops + [tops[0]] * (8 - parts), axis=0)
            for g in range(tile // LANES):
                at = slice(g * LANES, (g + 1) * LANES)
                top = jnp.max(tops[:, at], axis=1, keepdims=True)
                o_ref[a, :, at] = jnp.broadcast_to(top, (8, LANES))

    return pl.pallas_call(
        kernel,
        grid=(cols // tile,),
        in_specs=[pl.BlockSpec((rows, tile), lambda i: (0, i))] * count,
        out_specs=pl.BlockSpec((count, 8, tile), lambda i: (0, 0, i)),
        out_shape=jax.ShapeDtypeStruct((count, 8, cols), f32),
        compiler_params=params(),
        cost_estimate=cost(2 * count * rows * cols, 2 * count * rows * cols),
        name="chunk_max",
    )(*weights)


def levels_of(weights, own, got, odd, chunk, tile):
    rows, cols = weights[0].shape
    parts = rows // chunk
    count = len(weights)
    extra = 1 if got is None else 2

    def kernel(odd_ref, *refs):
        w_refs = refs[:count]
        top_refs = refs[count : count + extra]
        o_refs = refs[count + extra : 2 * count + extra]
        s_ref = refs[2 * count + extra]
        factor = refs[2 * count + extra + 1]
        is_odd = odd_ref[0] == 1
        for a in range(count):
            if got is None:
                tops = top_refs[0][a]
            else:
                mine, other = top_refs[0], top_refs[1]
                joined = []
                for j in range(parts):
                    even = mine[a, pl.ds(j ^ 1, 1)] if j ^ 1 < parts else other[a, pl.ds(0, 1)]
                    back = j - 1 if j % 2 == 0 else j + 1
                    near = other[a, pl.ds(parts - 1, 1)] if back < 0 else mine[a, pl.ds(back, 1)]
                    joined.append(
                        jnp.maximum(mine[a, pl.ds(j, 1)], jnp.where(is_odd, near, even))
                    )
                tops = jnp.concatenate(joined + [joined[0]] * (8 - parts), axis=0)
            largest = tops + EPS_SCALE
            factor[a] = QMAX / largest
            s_ref[a] = largest * (1.0 / QMAX)
        for a in range(count):
            for j in range(parts):
                rows_at = pl.ds(j * chunk, chunk)
                value = w_refs[a][rows_at, :].astype(f32) * factor[a, pl.ds(j, 1), :]
                o_refs[a][rows_at, :] = value.astype(f8)

    tops = [own] if got is None else [own, got]
    return pl.pallas_call(
        kernel,
        grid_spec=pltpu.PrefetchScalarGridSpec(
            num_scalar_prefetch=1,
            grid=(cols // tile,),
            in_specs=[pl.BlockSpec((rows, tile), lambda i, c: (0, i))] * count
            + [pl.BlockSpec((count, 8, tile), lambda i, c: (0, 0, i))] * extra,
            out_specs=[pl.BlockSpec((rows, tile), lambda i, c: (0, i))] * count
            + [pl.BlockSpec((count, 8, tile), lambda i, c: (0, 0, i))],
            scratch_shapes=[pltpu.VMEM((count, 8, tile), f32)],
        ),
        out_shape=[jax.ShapeDtypeStruct((rows, cols), f8)] * count
        + [jax.ShapeDtypeStruct((count, 8, cols), f32)],
        compiler_params=params(),
        cost_estimate=cost(4 * count * rows * cols, 3 * count * rows * cols),
        name="levels_of",
    )(odd, *weights, *tops)


def join_group(parts, size, dim):
    count = lax.axis_size("wide")
    me = lax.axis_index("wide")
    share = parts.shape[dim]
    shape = list(parts.shape)
    shape[dim] = share * size
    out = jnp.zeros(shape, parts.dtype)
    out = lax.dynamic_update_slice_in_dim(out, parts, (me % size) * share, dim)
    for step in range(1, size):
        perm = [(i // size * size + (i + step) % size, i) for i in range(count)]
        got = lax.ppermute(parts, "wide", perm)
        out = lax.dynamic_update_slice_in_dim(out, got, ((me + step) % size) * share, dim)
    return out


def quantize(weights, tops, chunk, odd, tile):
    rows = weights[0].shape[0]
    size = math.lcm(rows, BLOCK) // rows
    per = BLOCK // chunk
    parts = rows // chunk
    if size == 1 and per == 1:
        return levels_of(weights, tops, None, odd, chunk, tile)
    if size == 2 and per == 2:
        return levels_of(weights, tops, swap_cores(tops), odd, chunk, tile)
    joined = join_group(tops[:, :parts], size, 1)
    blocks = joined.reshape(joined.shape[0], -1, per, joined.shape[2])
    joined = jnp.broadcast_to(jnp.max(blocks, axis=2, keepdims=True), blocks.shape)
    joined = joined.reshape(joined.shape[0], size * parts, -1)
    own = lax.dynamic_slice_in_dim(joined, (lax.axis_index("wide") % size) * parts, parts, 1)
    own = jnp.pad(own, ((0, 0), (0, 8 - parts), (0, 0)))
    return levels_of(weights, own, None, odd, chunk, tile)


def scaled_rows(x_ref, l_ref, scale_of, chunk, parts):
    total = None
    for j in range(parts):
        at = pl.ds(j * chunk, chunk)
        part = jnp.dot(x_ref[:, at], l_ref[at, :].astype(bf16), preferred_element_type=f32)
        part = part * scale_of(j)
        total = part if total is None else total + part
    return total


def out_product(left, levels, scale, chunk, owners):
    count, rows = left.shape
    cols = levels.shape[1]
    parts = rows // chunk
    share = cols // owners
    tile = pick_tile(cols, 2 * math.lcm(share, LANES))
    per = tile // share

    def kernel(x_ref, l_ref, s_ref, o_ref):
        total = scaled_rows(x_ref, l_ref, lambda j: s_ref[0, pl.ds(j, 1), :], chunk, parts)
        total = total.astype(bf16)
        for q in range(per):
            o_ref[q] = total[:, q * share : (q + 1) * share]

    return pl.pallas_call(
        kernel,
        grid=(cols // tile,),
        in_specs=[
            pl.BlockSpec((count, rows), lambda i: (0, 0)),
            pl.BlockSpec((rows, tile), lambda i: (0, i)),
            pl.BlockSpec((1, 8, tile), lambda i: (0, 0, i)),
        ],
        out_specs=pl.BlockSpec((per, count, share), lambda i: (i, 0, 0)),
        out_shape=jax.ShapeDtypeStruct((owners, count, share), bf16),
        compiler_params=params(),
        cost_estimate=cost(2 * count * rows * cols, rows * cols),
        name="out_product",
    )(left, levels, scale)


def gate_up_product(side, left, gate, up, scale, power, chunk, owners, out_type):
    count, rows = left.shape
    parts = rows // chunk
    share = gate.shape[1] // owners
    chips = owners // 2
    width = 2 * share + LANES
    per = max(1, min(chips, 2048 // share))
    tile = per * share
    steps = chips // per

    def kernel(side_ref, x_ref, g_ref, u_ref, s_ref, p_ref, o_ref):
        for a, ref in enumerate((g_ref, u_ref)):
            total = scaled_rows(
                x_ref, ref, lambda j, a=a: s_ref[a, pl.ds(j, 1), :], chunk, parts
            ).astype(out_type)
            for q in range(per):
                o_ref[q, :, pl.ds(a * share, share)] = total[:, q * share : (q + 1) * share]
        for q in range(per):
            o_ref[q, :, pl.ds(2 * share, LANES)] = p_ref[...].astype(out_type)

    def columns(i, side_ref):
        return (0, side_ref[0] * steps + i)

    def fixed(i, side_ref):
        return (0, 0)

    return pl.pallas_call(
        kernel,
        grid_spec=pltpu.PrefetchScalarGridSpec(
            num_scalar_prefetch=1,
            grid=(steps,),
            in_specs=[
                pl.BlockSpec((count, rows), fixed),
                pl.BlockSpec((rows, tile), columns),
                pl.BlockSpec((rows, tile), columns),
                pl.BlockSpec((2, 8, tile), lambda i, side_ref: (0, 0, side_ref[0] * steps + i)),
                pl.BlockSpec((count, LANES), fixed),
            ],
            out_specs=pl.BlockSpec((per, count, width), lambda i, side_ref: (i, 0, 0)),
        ),
        out_shape=jax.ShapeDtypeStruct((chips, count, width), out_type),
        compiler_params=params(),
        cost_estimate=cost(4 * count * rows * share * chips, 2 * rows * share * chips),
        name="gate_up_product",
    )(side, left, gate, up, scale, power)


def down_product(side, act, levels, scale):
    chips, count, share = act.shape
    width, hidden = levels.shape
    blocks = share // BLOCK
    per = max(1, min(chips, 4096 // share))
    tile = per * share
    steps = chips // per

    def kernel(side_ref, a_ref, l_ref, s_ref, o_ref):
        total = jnp.zeros((count, width), f32)
        for q in range(per):
            for j in range(blocks):
                block = q * blocks + j
                part = lax.dot_general(
                    a_ref[q, :, pl.ds(j * BLOCK, BLOCK)],
                    l_ref[:, pl.ds(block * BLOCK, BLOCK)].astype(bf16),
                    (((1,), (1,)), ((), ())),
                    preferred_element_type=f32,
                )
                total = total + part * s_ref[pl.ds(block, 1), :]

        @pl.when(pl.program_id(0) == 0)
        def _():
            o_ref[...] = total

        @pl.when(pl.program_id(0) > 0)
        def _():
            o_ref[...] += total

    return pl.pallas_call(
        kernel,
        grid_spec=pltpu.PrefetchScalarGridSpec(
            num_scalar_prefetch=1,
            grid=(steps,),
            in_specs=[
                pl.BlockSpec((per, count, share), lambda i, c: (i, 0, 0)),
                pl.BlockSpec((width, tile), lambda i, c: (0, c[0] * steps + i)),
                pl.BlockSpec((per * blocks, width), lambda i, c: (c[0] * steps + i, 0)),
            ],
            out_specs=pl.BlockSpec((count, width), lambda i, c: (0, 0)),
        ),
        out_shape=jax.ShapeDtypeStruct((count, width), f32),
        compiler_params=params(),
        cost_estimate=cost(2 * count * width * hidden // 2, width * hidden // 2),
        name="down_product",
    )(side, act, levels, scale)


def attention(queries, kv_cache, new_kv, live):
    steps = queries.shape[0]
    factor = queries.shape[-1] ** (-0.5)
    keys = kv_cache[0]
    values = kv_cache[1]
    new_keys = new_kv[:, 0]
    new_values = new_kv[:, 1]
    position = jnp.arange(keys.shape[2], dtype=jnp.int32)
    valid = position[None, None, None, None, :] < live[None, :, None, None, None]
    cached = (
        jnp.einsum("nshqd,shcd->nshqc", queries, keys, preferred_element_type=f32) * factor
    )
    recent = (
        jnp.einsum("nshqd,tshd->nshqt", queries, new_keys, preferred_element_type=f32) * factor
    )
    order = jnp.arange(steps, dtype=jnp.int32)
    fresh = (order[None, :] <= order[:, None])[:, None, None, None, :]
    top = jnp.maximum(
        jnp.max(jnp.where(valid, cached, NEG), axis=-1),
        jnp.max(jnp.where(fresh, recent, NEG), axis=-1),
    )[..., None]
    e_cached = jnp.where(valid, jnp.exp(cached - top), 0.0)
    e_recent = jnp.where(fresh, jnp.exp(recent - top), 0.0)
    total = jnp.sum(e_cached, axis=-1, keepdims=True) + jnp.sum(e_recent, axis=-1, keepdims=True)
    p_cached = (e_cached / total).astype(bf16)
    p_recent = (e_recent / total).astype(bf16)
    mixed = jnp.einsum("nshqc,shcd->nshqd", p_cached, values, preferred_element_type=f32)
    mixed = mixed + jnp.einsum(
        "nshqt,tshd->nshqd", p_recent, new_values, preferred_element_type=f32
    )
    return mixed.astype(bf16)


def swap_cores(value):
    count = lax.axis_size("wide")
    return lax.ppermute(value, "wide", [(i, i ^ 1) for i in range(count)])


def exchange(value):
    return lax.all_to_all(value, "wide", split_axis=0, concat_axis=0, tiled=True)


def exchange_chips(value):
    count = lax.axis_size("wide")
    groups = [list(range(core, count, 2)) for core in range(2)]
    return lax.all_to_all(
        value, "wide", split_axis=0, concat_axis=0, tiled=True, axis_index_groups=groups
    )


def on_device(
    residual_in,
    norm_gain,
    gate_weight,
    up_weight,
    down_weight,
    out_weight,
    queries,
    kv_cache,
    new_kv,
    cache_len,
):
    owners = lax.axis_size("wide")
    me = lax.axis_index("wide")
    core = (me % 2).astype(jnp.int32).reshape(1)
    steps, seqs, width_dev = residual_in.shape
    seq_dev = seqs // owners
    tokens = steps * seqs
    mine = steps * seq_dev
    width = width_dev * owners

    odd = core

    live = lax.dynamic_slice_in_dim(cache_len, me * seq_dev, seq_dev, 0)
    attn_out = attention(queries, kv_cache, new_kv, live)
    heads = attn_out.reshape(steps, seq_dev, owners, -1)
    heads = exchange(jnp.transpose(heads, (2, 1, 0, 3)))

    out_chunk = math.gcd(out_weight.shape[0], BLOCK)
    out_tile = pick_tile(out_weight.shape[1], 2560)
    out_tops = chunk_max([out_weight], out_chunk, out_tile)
    out_levels, out_scale = quantize([out_weight], out_tops, out_chunk, odd, out_tile)
    chunk = math.gcd(gate_weight.shape[0], BLOCK)
    tile = pick_tile(gate_weight.shape[1], 2048)
    down_tile = pick_tile(gate_weight.shape[1], 4096)
    gate_up_tops = chunk_max([gate_weight, up_weight], chunk, tile)
    heads, out_levels, out_scale, gate_up_tops = lax.optimization_barrier(
        (heads, out_levels, out_scale, gate_up_tops)
    )

    heads = heads.reshape(tokens, -1)
    projected = exchange(out_product(heads, out_levels, out_scale, out_chunk, owners))

    gate_levels, up_levels, gate_up_scale = quantize(
        [gate_weight, up_weight], gate_up_tops, chunk, odd, tile
    )
    projected, gate_levels, up_levels, gate_up_scale = lax.optimization_barrier(
        (projected, gate_levels, up_levels, gate_up_scale)
    )

    projected = jnp.sum(projected.astype(f32), axis=0)
    residual = jnp.transpose(residual_in, (1, 0, 2)).reshape(tokens, width_dev)
    hidden = (residual.astype(f32) + projected).astype(bf16)

    states = hidden.astype(f32)
    gain = lax.dynamic_slice_in_dim(norm_gain, me * width_dev, width_dev, 0).astype(f32)
    scaled = (states * gain).astype(bf16)
    squares = jnp.sum(states * states, axis=1, keepdims=True)
    high = squares.astype(bf16)
    low = (squares - high.astype(f32)).astype(bf16)
    lane = lax.broadcasted_iota(jnp.int32, (tokens, LANES), 1)
    power = jnp.where(lane == 0, high, jnp.where(lane == 1, low, jnp.zeros_like(low)))

    product = functools.partial(
        gate_up_product,
        left=scaled,
        gate=gate_levels,
        up=up_levels,
        scale=gate_up_scale,
        power=power,
        chunk=chunk,
        owners=owners,
    )
    sent = product(1 - core, out_type=bf16)
    got = swap_cores(sent)
    kept = product(core, out_type=f32)
    chip_sum = exchange_chips((kept + got.astype(f32)).astype(bf16))

    down = down_weight.T
    down_chunk = math.gcd(down.shape[0], BLOCK)
    down_tops = chunk_max([down], down_chunk, down_tile)
    down_levels, down_scale = quantize([down], down_tops, down_chunk, odd, down_tile)
    down_parts = down.shape[0] // down_chunk
    down_scale = jnp.repeat(down_scale[0, :down_parts, ::LANES].T, down_chunk, axis=1)
    hidden_out = exchange(hidden.reshape(owners, mine, width_dev))
    hidden_out = jnp.transpose(
        hidden_out.reshape(owners, seq_dev, steps, width_dev), (2, 1, 0, 3)
    ).reshape(steps, seq_dev, width)
    chip_sum, down_levels, down_scale, hidden_out = lax.optimization_barrier(
        (chip_sum, down_levels, down_scale, hidden_out)
    )

    summed = jnp.sum(chip_sum.astype(f32), axis=0)
    share = gate_weight.shape[1] // owners
    total = summed[:, 2 * share : 2 * share + 1] + summed[:, 2 * share + 1 : 2 * share + 2]
    scale = lax.rsqrt(total / width + EPS_NORM)
    gate = summed[:, :share] * scale
    up = summed[:, share : 2 * share] * scale
    act = (jax.nn.silu(gate) * up).astype(bf16)

    same = exchange_chips(jnp.broadcast_to(act[None], (owners // 2,) + act.shape))
    other = swap_cores(same)
    ffn = down_product(core, same, down_levels, down_scale)
    ffn = ffn + down_product(1 - core, other, down_levels, down_scale)
    ffn = exchange(ffn.astype(bf16).reshape(owners, mine, width_dev))
    ffn_out = jnp.transpose(
        ffn.reshape(owners, seq_dev, steps, width_dev), (2, 1, 0, 3)
    ).reshape(steps, seq_dev, width)
    return (ffn_out, attn_out, hidden_out)


def solution(mesh):
    placed = (
        P("grp", None, "wide"),
        P(),
        P("wide", None),
        P("wide", None),
        P(None, "wide"),
        P("wide", None),
        P("grp", "wide", None, None, None),
        P(None, ("grp", "wide"), None, None, None),
        P("grp", None, "wide", None, None),
        P("grp"),
    )
    return jax.shard_map(
        on_device,
        mesh=mesh,
        in_specs=placed,
        out_specs=(
            P("grp", "wide", None),
            P("grp", "wide", None, None, None),
            P("grp", "wide", None),
        ),
        check_vma=False,
    )
```

```python
import functools
import math

import jax
import jax.numpy as jnp
from jax import lax
from jax.experimental import pallas as pl
from jax.experimental.pallas import tpu as pltpu
from jax.sharding import PartitionSpec as P

BLOCK = 128
QMAX = 448.0
EPS_NORM = 1e-06
EPS_SCALE = 1e-06
NEG = -1e30
LANES = 128
VMEM = 56 * 2**20

f32 = jnp.float32
bf16 = jnp.bfloat16
f8 = jnp.float8_e4m3fn


def params(**more):
    return pltpu.CompilerParams(vmem_limit_bytes=VMEM, **more)


def cost(flops, read):
    return pl.CostEstimate(flops=int(flops), bytes_accessed=int(read), transcendentals=0)


def pick_tile(cols, most):
    tile = most
    while cols % tile:
        tile -= LANES
    return tile


def spread_lanes(tops):
    out = []
    for g in range(tops.shape[1] // LANES):
        top = jnp.max(tops[:, g * LANES : (g + 1) * LANES], axis=1, keepdims=True)
        out.append(jnp.broadcast_to(top, (tops.shape[0], LANES)))
    return jnp.concatenate(out, axis=1)


def rows_max(ref, start, size):
    return jnp.max(jnp.abs(ref[pl.ds(start, size), :]), axis=0, keepdims=True).astype(f32)


def fill_rows(rows):
    return jnp.concatenate(rows + [rows[0]] * (8 - len(rows)), axis=0)


def chunk_max(place, weights, cols, chunk, tile):
    rows = weights[0].shape[0]
    parts = rows // chunk
    count = len(weights)
    steps = cols // tile

    def kernel(place_ref, *refs):
        for a in range(count):
            tops = [rows_max(refs[a], j * chunk, chunk) for j in range(parts)]
            refs[count][a] = spread_lanes(fill_rows(tops))

    return pl.pallas_call(
        kernel,
        grid_spec=pltpu.PrefetchScalarGridSpec(
            num_scalar_prefetch=1,
            grid=(steps,),
            in_specs=[pl.BlockSpec((rows, tile), lambda i, p: (0, p[1] * steps + i))] * count,
            out_specs=pl.BlockSpec((count, 8, tile), lambda i, p: (0, 0, i)),
        ),
        out_shape=jax.ShapeDtypeStruct((count, 8, cols), f32),
        compiler_params=params(),
        cost_estimate=cost(2 * count * rows * cols, 2 * count * rows * cols),
        name="chunk_max",
    )(place, *weights)


def edge_max(place, weights, cols, chunk, tile):
    parts = weights[0].shape[0] // chunk
    count = len(weights)
    steps = cols // tile

    def kernel(place_ref, *refs):
        refs[count][...] = spread_lanes(
            fill_rows([rows_max(refs[a], 0, chunk) for a in range(count)])
        )

    return pl.pallas_call(
        kernel,
        grid_spec=pltpu.PrefetchScalarGridSpec(
            num_scalar_prefetch=1,
            grid=(steps,),
            in_specs=[
                pl.BlockSpec(
                    (chunk, tile), lambda i, p: ((1 - p[0]) * (parts - 1), p[1] * steps + i)
                )
            ]
            * count,
            out_specs=pl.BlockSpec((8, tile), lambda i, p: (0, i)),
        ),
        out_shape=jax.ShapeDtypeStruct((8, cols), f32),
        compiler_params=params(),
        cost_estimate=cost(2 * count * chunk * cols, 2 * count * chunk * cols),
        name="edge_max",
    )(place, *weights)


def levels_of(place, weights, edge, first, tops, cols, chunk, tile):
    rows = weights[0].shape[0]
    parts = rows // chunk
    count = len(weights)
    steps = cols // tile

    def kernel(place_ref, *refs):
        w_refs = refs[:count]
        top_ref = refs[count]
        o_refs = refs[count + 1 : 2 * count + 1]
        s_ref = refs[2 * count + 1]
        factor = refs[2 * count + 2]
        odd = place_ref[0] == 1
        for a in range(count):
            if edge is None:
                joined = top_ref[a]
            else:
                other = top_ref[pl.ds(first + a, 1), :]
                mine = [rows_max(w_refs[a], j * chunk, chunk) for j in range(parts)]
                joined = []
                for j in range(parts):
                    even = mine[j ^ 1] if j ^ 1 < parts else other
                    back = j - 1 if j % 2 == 0 else j + 1
                    near = other if back < 0 else mine[back]
                    joined.append(jnp.maximum(mine[j], jnp.where(odd, near, even)))
                joined = spread_lanes(fill_rows(joined))
            largest = joined + EPS_SCALE
            factor[a] = QMAX / largest
            s_ref[a] = largest * (1.0 / QMAX)
        for a in range(count):
            for j in range(parts):
                rows_at = pl.ds(j * chunk, chunk)
                value = w_refs[a][rows_at, :].astype(f32) * factor[a, pl.ds(j, 1), :]
                o_refs[a][rows_at, :] = value.astype(f8)

    if edge is None:
        top_spec = pl.BlockSpec((count, 8, tile), lambda i, p: (0, 0, i))
    else:
        top_spec = pl.BlockSpec((8, tile), lambda i, p: (0, i))
    return pl.pallas_call(
        kernel,
        grid_spec=pltpu.PrefetchScalarGridSpec(
            num_scalar_prefetch=1,
            grid=(steps,),
            in_specs=[pl.BlockSpec((rows, tile), lambda i, p: (0, p[1] * steps + i))] * count
            + [top_spec],
            out_specs=[pl.BlockSpec((rows, tile), lambda i, p: (0, i))] * count
            + [pl.BlockSpec((count, 8, tile), lambda i, p: (0, 0, i))],
            scratch_shapes=[pltpu.VMEM((count, 8, tile), f32)],
        ),
        out_shape=[jax.ShapeDtypeStruct((rows, cols), f8)] * count
        + [jax.ShapeDtypeStruct((count, 8, cols), f32)],
        compiler_params=params(),
        cost_estimate=cost(4 * count * rows * cols, 3 * count * rows * cols),
        name="levels_of",
    )(place, *weights, tops if edge is None else edge)


def join_group(parts, size, dim):
    count = lax.axis_size("wide")
    me = lax.axis_index("wide")
    share = parts.shape[dim]
    shape = list(parts.shape)
    shape[dim] = share * size
    out = jnp.zeros(shape, parts.dtype)
    out = lax.dynamic_update_slice_in_dim(out, parts, (me % size) * share, dim)
    for step in range(1, size):
        perm = [(i // size * size + (i + step) % size, i) for i in range(count)]
        got = lax.ppermute(parts, "wide", perm)
        out = lax.dynamic_update_slice_in_dim(out, got, ((me + step) % size) * share, dim)
    return out


def pair_shares_blocks(rows):
    return math.lcm(rows, BLOCK) == 2 * rows and math.gcd(rows, BLOCK) == BLOCK // 2


def joined_max(place, weights, cols, chunk, tile):
    rows = weights[0].shape[0]
    size = math.lcm(rows, BLOCK) // rows
    per = BLOCK // chunk
    parts = rows // chunk
    tops = chunk_max(place, weights, cols, chunk, tile)
    if size == 1:
        return tops
    joined = join_group(tops[:, :parts], size, 1)
    blocks = joined.reshape(joined.shape[0], -1, per, joined.shape[2])
    joined = jnp.broadcast_to(jnp.max(blocks, axis=2, keepdims=True), blocks.shape)
    joined = joined.reshape(joined.shape[0], size * parts, -1)
    own = lax.dynamic_slice_in_dim(joined, (lax.axis_index("wide") % size) * parts, parts, 1)
    return jnp.pad(own, ((0, 0), (0, 8 - parts), (0, 0)))


def out_product(left, weight, owners):
    count, rows = left.shape
    cols = weight.shape[1]
    parts = rows // BLOCK
    share = cols // owners
    tile = pick_tile(cols, 2 * math.lcm(share, LANES))
    per = tile // share

    def kernel(x_ref, w_ref, o_ref):
        tops = spread_lanes(
            jnp.concatenate([rows_max(w_ref, j * BLOCK, BLOCK) for j in range(parts)], axis=0)
        )
        largest = tops + EPS_SCALE
        factor = QMAX / largest
        scale = largest * (1.0 / QMAX)
        total = None
        for j in range(parts):
            at = pl.ds(j * BLOCK, BLOCK)
            levels = (w_ref[at, :].astype(f32) * factor[j : j + 1]).astype(f8).astype(bf16)
            part = jnp.dot(x_ref[:, at], levels, preferred_element_type=f32)
            part = part * scale[j : j + 1]
            total = part if total is None else total + part
        total = total.astype(bf16)
        for q in range(per):
            o_ref[q] = total[:, q * share : (q + 1) * share]

    return pl.pallas_call(
        kernel,
        grid=(cols // tile,),
        in_specs=[
            pl.BlockSpec((count, rows), lambda i: (0, 0)),
            pl.BlockSpec((rows, tile), lambda i: (0, i)),
        ],
        out_specs=pl.BlockSpec((per, count, share), lambda i: (i, 0, 0)),
        out_shape=jax.ShapeDtypeStruct((owners, count, share), bf16),
        compiler_params=params(),
        cost_estimate=cost(8 * count * rows * cols, 2 * rows * cols),
        name="out_product",
    )(left, weight)


def gate_up_product(at, left, gate, up, scale, power, added, share, chips, chunk, staged):
    count, rows = left.shape
    parts = rows // chunk
    extra = 0 if power is None else power.shape[1]
    width = 2 * share + extra
    split = 2 if chips % 2 == 0 else 1
    tile, chips_at = chips * share // split, chips // split

    def kernel(at_ref, x_ref, g_ref, u_ref, s_ref, *refs):
        refs = list(refs)
        o_refs = [refs.pop()]
        if staged:
            o_refs = [refs.pop(), o_refs[0]]
        p_ref = None if power is None else refs.pop(0)
        add_ref = None if added is None else refs.pop(0)
        blocks = []
        for a, ref in enumerate((g_ref, u_ref)):
            total = None
            for j in range(parts):
                rows_at = pl.ds(j * chunk, chunk)
                part = jnp.dot(
                    x_ref[:, rows_at], ref[rows_at, :].astype(bf16), preferred_element_type=f32
                )
                part = part * s_ref[a, pl.ds(j, 1), :]
                total = part if total is None else total + part
            blocks.append(total)
        for q in range(chips_at):
            here = slice(q * share, (q + 1) * share)
            values = [total[:, here] for total in blocks]
            if power is not None:
                values.append(p_ref[...])
            starts = [0, share, 2 * share][: len(values)]

            def write(o_ref, position):
                for start, value in zip(starts, values):
                    lanes = pl.ds(start, value.shape[1])
                    if added is not None:
                        value = value + add_ref[q, :, lanes].astype(f32)
                    o_ref[position, :, lanes] = value.astype(bf16)

            if not staged:
                write(o_refs[0], q)
                continue
            away = (pl.program_id(0) * chips_at + q) ^ at_ref[1]
            position, rest = 0, away // 2
            for _ in range(chips.bit_length() - 2):
                position, rest = position * 2 + rest % 2, rest // 2
            for side in range(2):
                pl.when(away % 2 == side)(functools.partial(write, o_refs[side], position))

    def fixed(i, p):
        return (0, 0)

    owner_spec = pl.BlockSpec((chips_at, count, width), lambda i, p: (i, 0, 0))
    in_specs = [
        pl.BlockSpec((count, rows), fixed),
        pl.BlockSpec((rows, tile), lambda i, p: (0, p[0] * split + i)),
        pl.BlockSpec((rows, tile), lambda i, p: (0, p[0] * split + i)),
        pl.BlockSpec((2, 8, tile), lambda i, p: (0, 0, p[0] * split + i)),
    ]
    operands = [left, gate, up, scale]
    if power is not None:
        in_specs.append(pl.BlockSpec((count, extra), fixed))
        operands.append(power)
    if added is not None:
        in_specs.append(owner_spec)
        operands.append(added)
    out_spec, out_shape = owner_spec, jax.ShapeDtypeStruct((chips, count, width), bf16)
    if staged:
        out_spec = [pl.BlockSpec((chips // 2, count, width), lambda i, p: (0, 0, 0))] * 2
        out_shape = [jax.ShapeDtypeStruct((chips // 2, count, width), bf16)] * 2
    return pl.pallas_call(
        kernel,
        grid_spec=pltpu.PrefetchScalarGridSpec(
            num_scalar_prefetch=1, grid=(split,), in_specs=in_specs, out_specs=out_spec
        ),
        out_shape=out_shape,
        compiler_params=params(),
        cost_estimate=cost(4 * count * rows * share * chips, 2 * rows * share * chips),
        name="gate_up_product",
    )(at, *operands)


def down_product(at, act, levels, scale, added, staged):
    chips, count, share = act.shape
    width, hidden = levels.shape
    blocks = share // BLOCK
    tile = chips * share

    def kernel(at_ref, a_ref, l_ref, s_ref, *refs):
        total = refs[0][...] if added is not None else jnp.zeros((count, width), f32)
        for q in range(chips):
            chip = q
            if staged:
                chip, rest = 0, q
                for _ in range(chips.bit_length() - 1):
                    chip, rest = chip * 2 + rest % 2, rest // 2
                chip = chip ^ at_ref[1]
            for j in range(blocks):
                block = chip * blocks + j
                start = block * BLOCK
                if staged:
                    start = pl.multiple_of(start, BLOCK)
                part = lax.dot_general(
                    a_ref[q, :, pl.ds(j * BLOCK, BLOCK)],
                    l_ref[:, pl.ds(start, BLOCK)].astype(bf16),
                    (((1,), (1,)), ((), ())),
                    preferred_element_type=f32,
                )
                total = total + part * s_ref[pl.ds(block, 1), :]
        refs[-1][...] = total

    fixed = pl.BlockSpec((count, width), lambda i, p: (0, 0))
    return pl.pallas_call(
        kernel,
        grid_spec=pltpu.PrefetchScalarGridSpec(
            num_scalar_prefetch=1,
            grid=(1,),
            in_specs=[
                pl.BlockSpec((chips, count, share), lambda i, p: (0, 0, 0)),
                pl.BlockSpec((width, tile), lambda i, p: (0, p[0])),
                pl.BlockSpec((chips * blocks, width), lambda i, p: (p[0], 0)),
            ]
            + ([] if added is None else [fixed]),
            out_specs=fixed,
        ),
        out_shape=jax.ShapeDtypeStruct((count, width), f32),
        compiler_params=params(),
        cost_estimate=cost(2 * count * width * tile, width * tile),
        name="down_product",
    )(at, act, levels, scale, *([] if added is None else [added]))


def attention(queries, kv_cache, new_kv, live):
    steps = queries.shape[0]
    factor = queries.shape[-1] ** (-0.5)
    keys = kv_cache[0]
    values = kv_cache[1]
    new_keys = new_kv[:, 0]
    new_values = new_kv[:, 1]
    position = jnp.arange(keys.shape[2], dtype=jnp.int32)
    valid = position[None, None, None, None, :] < live[None, :, None, None, None]
    cached = (
        jnp.einsum("nshqd,shcd->nshqc", queries, keys, preferred_element_type=f32) * factor
    )
    recent = (
        jnp.einsum("nshqd,tshd->nshqt", queries, new_keys, preferred_element_type=f32) * factor
    )
    order = jnp.arange(steps, dtype=jnp.int32)
    fresh = (order[None, :] <= order[:, None])[:, None, None, None, :]
    top = jnp.maximum(
        jnp.max(jnp.where(valid, cached, NEG), axis=-1),
        jnp.max(jnp.where(fresh, recent, NEG), axis=-1),
    )[..., None]
    e_cached = jnp.where(valid, jnp.exp(cached - top), 0.0)
    e_recent = jnp.where(fresh, jnp.exp(recent - top), 0.0)
    total = jnp.sum(e_cached, axis=-1, keepdims=True) + jnp.sum(e_recent, axis=-1, keepdims=True)
    p_cached = (e_cached / total).astype(bf16)
    p_recent = (e_recent / total).astype(bf16)
    mixed = jnp.einsum("nshqc,shcd->nshqd", p_cached, values, preferred_element_type=f32)
    mixed = mixed + jnp.einsum(
        "nshqt,tshd->nshqd", p_recent, new_values, preferred_element_type=f32
    )
    return mixed.astype(bf16)


def swap_cores(value):
    count = lax.axis_size("wide")
    return lax.ppermute(value, "wide", [(i, i ^ 1) for i in range(count)])


def exchange(value):
    return lax.all_to_all(value, "wide", split_axis=0, concat_axis=0, tiled=True)


def exchange_chips(value):
    count = lax.axis_size("wide")
    groups = [list(range(core, count, 2)) for core in range(2)]
    return lax.all_to_all(
        value, "wide", split_axis=0, concat_axis=0, tiled=True, axis_index_groups=groups
    )


def exchange_halves(keep, send):
    count = lax.axis_size("wide")
    bit = 2
    while True:
        got = lax.ppermute(send, "wide", [(i, i ^ bit) for i in range(count)])
        total = keep.astype(f32) + got.astype(f32)
        bit *= 2
        if bit == count:
            return total[0]
        total = total.astype(bf16)
        half = total.shape[0] // 2
        keep, send = total[:half], total[half:]


def gather_halves(value):
    count = lax.axis_size("wide")
    value = value[None]
    bit = count // 2
    while bit > 1:
        got = lax.ppermute(value, "wide", [(i, i ^ bit) for i in range(count)])
        value = jnp.concatenate([value, got], axis=0)
        bit //= 2
    return value


def on_device(
    residual_in,
    norm_gain,
    gate_weight,
    up_weight,
    down_weight,
    out_weight,
    queries,
    kv_cache,
    new_kv,
    cache_len,
):
    owners = lax.axis_size("wide")
    groups = lax.axis_size("grp")
    me = lax.axis_index("wide")
    steps, seqs, width_dev = residual_in.shape
    seq_dev = seqs // owners
    tokens = steps * seqs
    mine = steps * seq_dev
    width = width_dev * owners
    chips = owners // 2
    hidden_units = gate_weight.shape[1]

    halves = 2
    parts = groups if hidden_units % (groups * owners * halves * BLOCK) == 0 else 1
    units = hidden_units // parts
    share = units // (owners * halves)
    part = lax.axis_index("grp") if parts > 1 else jnp.zeros((), jnp.int32)
    odd = me % 2
    place = jnp.stack([odd, part]).astype(jnp.int32)

    live = lax.dynamic_slice_in_dim(cache_len, me * seq_dev, seq_dev, 0)
    attn_out = attention(queries, kv_cache, new_kv, live)
    heads = attn_out.reshape(steps, seq_dev, owners, -1)
    heads = exchange(jnp.transpose(heads, (2, 1, 0, 3)))

    down = down_weight.T
    rows = gate_weight.shape[0]
    chunk = math.gcd(rows, BLOCK)
    tile = pick_tile(units, 2048)
    paired = pair_shares_blocks(rows) and down.shape[0] == rows
    if paired:
        edge = edge_max(place, [gate_weight, up_weight, down], units, chunk, pick_tile(units, 4096))
        heads, edge = lax.optimization_barrier((heads, edge))
        edge = swap_cores(edge)

    heads = heads.reshape(tokens, -1)
    projected = exchange(out_product(heads, out_weight, owners))

    if paired:
        gate_levels, up_levels, gate_up_scale = levels_of(
            place, [gate_weight, up_weight], edge, 0, None, units, chunk, tile
        )
    else:
        tops = joined_max(place, [gate_weight, up_weight], units, chunk, tile)
        gate_levels, up_levels, gate_up_scale = levels_of(
            place, [gate_weight, up_weight], None, 0, tops, units, chunk, tile
        )
    projected, gate_levels, up_levels, gate_up_scale = lax.optimization_barrier(
        (projected, gate_levels, up_levels, gate_up_scale)
    )

    projected = jnp.sum(projected.astype(f32), axis=0)
    residual = jnp.transpose(residual_in, (1, 0, 2)).reshape(tokens, width_dev)
    hidden = (residual.astype(f32) + projected).astype(bf16)

    states = hidden
    if parts > 1:
        if groups == 2:
            got = lax.ppermute(hidden, "grp", [(0, 1), (1, 0)])
            first = part == 0
            states = jnp.concatenate(
                [jnp.where(first, hidden, got), jnp.where(first, got, hidden)], axis=0
            )
        else:
            states = lax.all_gather(hidden, "grp", axis=0, tiled=True)
    states = states.astype(f32)
    gain = lax.dynamic_slice_in_dim(norm_gain, me * width_dev, width_dev, 0).astype(f32)
    scaled = (states * gain).astype(bf16)
    squares = jnp.sum(states * states, axis=1, keepdims=True)
    spread = -(-2 * owners // LANES) * LANES
    lane = lax.broadcasted_iota(jnp.int32, (states.shape[0], spread), 1)
    high = squares.astype(bf16).astype(f32)
    power = jnp.where(lane == 2 * me, high, jnp.where(lane == 2 * me + 1, squares - high, 0.0))

    def run_at(half, side):
        return jnp.stack([half * 2 + side, me // 2]).astype(jnp.int32)

    def product(half, side, added, staged):
        return gate_up_product(
            run_at(half, side),
            scaled,
            gate_levels,
            up_levels,
            gate_up_scale,
            power if half == 0 else None,
            added,
            share,
            chips,
            chunk,
            staged,
        )

    sent = [swap_cores(product(half, 1 - odd, None, False)) for half in range(halves)]
    keep, send = product(0, odd, sent[0], True)
    kept = product(1, odd, sent[1], False)
    kept, place = lax.optimization_barrier((kept, place))
    sums = [exchange_halves(keep, send), exchange_chips(kept)]

    down_chunk = math.gcd(down.shape[0], BLOCK)
    down_tile = pick_tile(units, 4096)
    if paired:
        down_levels, down_scale = levels_of(
            place, [down], edge, 2, None, units, down_chunk, down_tile
        )
    else:
        tops = joined_max(place, [down], units, down_chunk, down_tile)
        down_levels, down_scale = levels_of(
            place, [down], None, 0, tops, units, down_chunk, down_tile
        )
    down_scale = down_scale[0, : down.shape[0] // down_chunk, ::LANES].T
    down_scale = jnp.repeat(down_scale, down_chunk, axis=1)
    sums[0], down_levels, down_scale = lax.optimization_barrier((sums[0], down_levels, down_scale))

    squares = jnp.sum(sums[0][:, 2 * share :], axis=1, keepdims=True)
    scale = lax.rsqrt(squares / width + EPS_NORM)

    def act_of(summed):
        gate = summed[:, :share] * scale
        up = summed[:, share : 2 * share] * scale
        return (jax.nn.silu(gate) * up).astype(bf16)

    same = gather_halves(act_of(sums[0]))
    act = act_of(jnp.sum(sums[1].astype(f32), axis=0))
    last = exchange_chips(jnp.broadcast_to(act[None], (chips,) + act.shape))
    other = swap_cores(same)
    ffn = down_product(run_at(0, odd), same, down_levels, down_scale, None, True)
    ffn = down_product(run_at(0, 1 - odd), other, down_levels, down_scale, ffn, True)
    last, ffn = lax.optimization_barrier((last, ffn))
    other = swap_cores(last)
    ffn = down_product(run_at(1, odd), last, down_levels, down_scale, ffn, False)
    ffn = down_product(run_at(1, 1 - odd), other, down_levels, down_scale, ffn, False)

    axes = ("grp", "wide") if parts > 1 else "wide"
    blocks = (parts * owners, mine, width_dev)
    both = jnp.concatenate(
        [ffn.astype(bf16).reshape(blocks), states.astype(bf16).reshape(blocks)], axis=1
    )
    both = lax.all_to_all(both, axes, split_axis=0, concat_axis=0, tiled=True)
    both = both.reshape(parts, owners, 2, seq_dev, steps, width_dev)
    ffn = both[0, :, 0]
    if parts > 1:
        ffn = jnp.sum(both[:, :, 0].astype(f32), axis=0).astype(bf16)
    ffn_out = jnp.transpose(ffn, (2, 1, 0, 3)).reshape(steps, seq_dev, width)
    hidden_out = jnp.transpose(both[0, :, 1], (2, 1, 0, 3)).reshape(steps, seq_dev, width)
    return (ffn_out, attn_out, hidden_out)


def solution(mesh):
    placed = (
        P("grp", None, "wide"),
        P(),
        P("wide", None),
        P("wide", None),
        P(None, "wide"),
        P("wide", None),
        P("grp", "wide", None, None, None),
        P(None, ("grp", "wide"), None, None, None),
        P("grp", None, "wide", None, None),
        P("grp"),
    )
    return jax.shard_map(
        on_device,
        mesh=mesh,
        in_specs=placed,
        out_specs=(
            P("grp", "wide", None),
            P("grp", "wide", None, None, None),
            P("grp", "wide", None),
        ),
        check_vma=False,
    )
```

```python
import functools
import math

import jax
import jax.numpy as jnp
from jax import lax
from jax.experimental import pallas as pl
from jax.experimental.pallas import tpu as pltpu
from jax.sharding import PartitionSpec as P

BLOCK = 128
QMAX = 448.0
EPS_NORM = 1e-06
EPS_SCALE = 1e-06
NEG = -1e30
LANES = 128
VMEM = 56 * 2**20

f32 = jnp.float32
bf16 = jnp.bfloat16
f8 = jnp.float8_e4m3fn


def params(**more):
    return pltpu.CompilerParams(vmem_limit_bytes=VMEM, **more)


def in_hbm(*arrays):
    return [pltpu.with_memory_space_constraint(x, pltpu.HBM) for x in arrays]


def cost(flops, read):
    return pl.CostEstimate(flops=int(flops), bytes_accessed=int(read), transcendentals=0)


def pick_tile(cols, most):
    tile = most
    while cols % tile:
        tile -= LANES
    return tile


def spread_lanes(tops):
    out = []
    for g in range(tops.shape[1] // LANES):
        top = jnp.max(tops[:, g * LANES : (g + 1) * LANES], axis=1, keepdims=True)
        out.append(jnp.broadcast_to(top, (tops.shape[0], LANES)))
    return jnp.concatenate(out, axis=1)


def rows_max(ref, start, size):
    return jnp.max(jnp.abs(ref[pl.ds(start, size), :]), axis=0, keepdims=True).astype(f32)


def fill_rows(rows):
    return jnp.concatenate(rows + [rows[0]] * (8 - len(rows)), axis=0)


def chunk_max(place, weights, cols, chunk, tile):
    rows = weights[0].shape[0]
    parts = rows // chunk
    count = len(weights)
    steps = cols // tile

    def kernel(place_ref, *refs):
        for a in range(count):
            tops = [rows_max(refs[a], j * chunk, chunk) for j in range(parts)]
            refs[count][a] = spread_lanes(fill_rows(tops))

    return pl.pallas_call(
        kernel,
        grid_spec=pltpu.PrefetchScalarGridSpec(
            num_scalar_prefetch=1,
            grid=(steps,),
            in_specs=[pl.BlockSpec((rows, tile), lambda i, p: (0, p[1] * steps + i))] * count,
            out_specs=pl.BlockSpec((count, 8, tile), lambda i, p: (0, 0, i)),
        ),
        out_shape=jax.ShapeDtypeStruct((count, 8, cols), f32),
        compiler_params=params(),
        cost_estimate=cost(2 * count * rows * cols, 2 * count * rows * cols),
        name="chunk_max",
    )(place, *in_hbm(*weights))


def edge_max(place, weights, cols, chunk, tile):
    parts = weights[0].shape[0] // chunk
    count = len(weights)
    steps = cols // tile

    def kernel(place_ref, *refs):
        refs[count][...] = spread_lanes(
            fill_rows([rows_max(refs[a], 0, chunk) for a in range(count)])
        )

    return pl.pallas_call(
        kernel,
        grid_spec=pltpu.PrefetchScalarGridSpec(
            num_scalar_prefetch=1,
            grid=(steps,),
            in_specs=[
                pl.BlockSpec(
                    (chunk, tile), lambda i, p: ((1 - p[0]) * (parts - 1), p[1] * steps + i)
                )
            ]
            * count,
            out_specs=pl.BlockSpec((8, tile), lambda i, p: (0, i)),
        ),
        out_shape=jax.ShapeDtypeStruct((8, cols), f32),
        compiler_params=params(),
        cost_estimate=cost(2 * count * chunk * cols, 2 * count * chunk * cols),
        name="edge_max",
    )(place, *in_hbm(*weights))


def join_pair(w_ref, other, odd, chunk, parts):
    mine = [rows_max(w_ref, j * chunk, chunk) for j in range(parts)]
    joined = []
    for j in range(parts):
        even = mine[j ^ 1] if j ^ 1 < parts else other
        back = j - 1 if j % 2 == 0 else j + 1
        near = other if back < 0 else mine[back]
        joined.append(jnp.maximum(mine[j], jnp.where(odd, near, even)))
    return fill_rows(joined)


def levels_of(place, weights, edge, tops, flip, cols, chunk, tile):
    rows = weights[0].shape[0]
    parts = rows // chunk
    count = len(weights)
    steps = cols // (2 * tile)

    def columns(i, p):
        return 2 * i + (p[0] ^ flip)

    def kernel(place_ref, *refs):
        w_refs = refs[:count]
        top_ref = refs[count]
        o_refs = refs[count + 1 : 2 * count + 1]
        s_ref = refs[2 * count + 1]
        factor = refs[2 * count + 2]
        odd = place_ref[0] == 1
        for a in range(count):
            if edge is None:
                joined = top_ref[a]
            else:
                other = top_ref[pl.ds(a, 1), :]
                joined = spread_lanes(join_pair(w_refs[a], other, odd, chunk, parts))
            largest = joined + EPS_SCALE
            factor[a] = QMAX / largest
            s_ref[a] = largest * (1.0 / QMAX)
        for a in range(count):
            for j in range(parts):
                rows_at = pl.ds(j * chunk, chunk)
                value = w_refs[a][rows_at, :].astype(f32) * factor[a, pl.ds(j, 1), :]
                o_refs[a][rows_at, :] = value.astype(f8)

    if edge is None:
        top_spec = pl.BlockSpec((count, 8, tile), lambda i, p: (0, 0, columns(i, p)))
    else:
        top_spec = pl.BlockSpec((8, tile), lambda i, p: (0, columns(i, p)))
    return pl.pallas_call(
        kernel,
        grid_spec=pltpu.PrefetchScalarGridSpec(
            num_scalar_prefetch=1,
            grid=(steps,),
            in_specs=[
                pl.BlockSpec((rows, tile), lambda i, p: (0, 2 * p[1] * steps + columns(i, p)))
            ]
            * count
            + [top_spec],
            out_specs=[pl.BlockSpec((rows, tile), lambda i, p: (0, i))] * count
            + [pl.BlockSpec((count, 8, tile), lambda i, p: (0, 0, i))],
            scratch_shapes=[pltpu.VMEM((count, 8, tile), f32)],
        ),
        out_shape=[jax.ShapeDtypeStruct((rows, cols // 2), f8)] * count
        + [jax.ShapeDtypeStruct((count, 8, cols // 2), f32)],
        compiler_params=params(),
        cost_estimate=cost(2 * count * rows * cols, 2 * count * rows * cols),
        name="levels_of",
    )(place, *in_hbm(*weights), tops if edge is None else edge)


def down_levels_of(place, weight, edge, row, tops, cols, chunk, tile):
    rows = weight.shape[0]
    parts = rows // chunk
    steps = cols // tile

    def kernel(place_ref, w_ref, top_ref, o_ref, s_ref):
        odd = place_ref[0] == 1
        if edge is None:
            joined = top_ref[0]
        else:
            other = top_ref[pl.ds(row, 1), :]
            joined = spread_lanes(join_pair(w_ref, other, odd, chunk, parts))
        largest = joined + EPS_SCALE
        factor = QMAX / largest
        scale = largest * (1.0 / QMAX)
        for g in range(tile // LANES):
            at = slice(g * LANES, (g + 1) * LANES)
            value = jnp.concatenate(
                [
                    w_ref[pl.ds(j * chunk, chunk), pl.ds(g * LANES, LANES)].astype(f32)
                    * factor[j : j + 1, at]
                    for j in range(parts)
                ],
                axis=0,
            )
            o_ref[pl.ds(g * LANES, LANES), :] = value.T.astype(f8)
            s_ref[pl.ds(g, 1), :] = jnp.concatenate(
                [scale[j : j + 1, at][:, :chunk] for j in range(parts)], axis=1
            )

    if edge is None:
        top_spec = pl.BlockSpec((1, 8, tile), lambda i, p: (0, 0, i))
    else:
        top_spec = pl.BlockSpec((8, tile), lambda i, p: (0, i))
    return pl.pallas_call(
        kernel,
        grid_spec=pltpu.PrefetchScalarGridSpec(
            num_scalar_prefetch=1,
            grid=(steps,),
            in_specs=[
                pl.BlockSpec((rows, tile), lambda i, p: (0, p[1] * steps + i)),
                top_spec,
            ],
            out_specs=[
                pl.BlockSpec((tile, rows), lambda i, p: (i, 0)),
                pl.BlockSpec((tile // LANES, rows), lambda i, p: (i, 0)),
            ],
        ),
        out_shape=[
            jax.ShapeDtypeStruct((cols, rows), f8),
            jax.ShapeDtypeStruct((cols // LANES, rows), f32),
        ],
        compiler_params=params(),
        cost_estimate=cost(8 * rows * cols, 3 * rows * cols),
        name="down_levels_of",
    )(place, *in_hbm(weight), tops if edge is None else edge)


def join_group(parts, size, dim):
    count = lax.axis_size("wide")
    me = lax.axis_index("wide")
    share = parts.shape[dim]
    shape = list(parts.shape)
    shape[dim] = share * size
    out = jnp.zeros(shape, parts.dtype)
    out = lax.dynamic_update_slice_in_dim(out, parts, (me % size) * share, dim)
    for step in range(1, size):
        perm = [(i // size * size + (i + step) % size, i) for i in range(count)]
        got = lax.ppermute(parts, "wide", perm)
        out = lax.dynamic_update_slice_in_dim(out, got, ((me + step) % size) * share, dim)
    return out


def pair_shares_blocks(rows):
    return math.lcm(rows, BLOCK) == 2 * rows and math.gcd(rows, BLOCK) == BLOCK // 2


def joined_max(place, weights, cols, chunk, tile):
    rows = weights[0].shape[0]
    size = math.lcm(rows, BLOCK) // rows
    per = BLOCK // chunk
    parts = rows // chunk
    tops = chunk_max(place, weights, cols, chunk, tile)
    if size == 1:
        return tops
    joined = join_group(tops[:, :parts], size, 1)
    blocks = joined.reshape(joined.shape[0], -1, per, joined.shape[2])
    joined = jnp.broadcast_to(jnp.max(blocks, axis=2, keepdims=True), blocks.shape)
    joined = joined.reshape(joined.shape[0], size * parts, -1)
    own = lax.dynamic_slice_in_dim(joined, (lax.axis_index("wide") % size) * parts, parts, 1)
    return jnp.pad(own, ((0, 0), (0, 8 - parts), (0, 0)))


def out_levels_of(weight, tile):
    rows, cols = weight.shape
    parts = rows // BLOCK

    def kernel(w_ref, o_ref, s_ref):
        tops = spread_lanes(fill_rows([rows_max(w_ref, j * BLOCK, BLOCK) for j in range(parts)]))
        largest = tops + EPS_SCALE
        factor = QMAX / largest
        s_ref[...] = largest * (1.0 / QMAX)
        for j in range(parts):
            at = pl.ds(j * BLOCK, BLOCK)
            o_ref[at, :] = (w_ref[at, :].astype(f32) * factor[j : j + 1]).astype(f8)

    columns = lambda i: (0, i)
    return pl.pallas_call(
        kernel,
        grid=(cols // tile,),
        in_specs=[pl.BlockSpec((rows, tile), columns)],
        out_specs=[pl.BlockSpec((rows, tile), columns), pl.BlockSpec((8, tile), columns)],
        out_shape=[
            jax.ShapeDtypeStruct((rows, cols), f8),
            jax.ShapeDtypeStruct((8, cols), f32),
        ],
        compiler_params=params(),
        cost_estimate=cost(8 * rows * cols, 3 * rows * cols),
        name="out_levels_of",
    )(*in_hbm(weight))


def out_product(left, levels, scale, owners):
    count, rows = left.shape
    cols = levels.shape[1]
    parts = rows // BLOCK
    share = cols // owners
    tile = pick_tile(cols, 4 * math.lcm(share, LANES))
    per = tile // share

    def kernel(x_ref, l_ref, s_ref, o_ref):
        total = None
        for j in range(parts):
            at = pl.ds(j * BLOCK, BLOCK)
            part = jnp.dot(x_ref[:, at], l_ref[at, :].astype(bf16), preferred_element_type=f32)
            part = part * s_ref[pl.ds(j, 1), :]
            total = part if total is None else total + part
        total = total.astype(bf16)
        for q in range(per):
            o_ref[q] = total[:, q * share : (q + 1) * share]

    return pl.pallas_call(
        kernel,
        grid=(cols // tile,),
        in_specs=[
            pl.BlockSpec((count, rows), lambda i: (0, 0)),
            pl.BlockSpec((rows, tile), lambda i: (0, i)),
            pl.BlockSpec((8, tile), lambda i: (0, i)),
        ],
        out_specs=pl.BlockSpec((per, count, share), lambda i: (i, 0, 0)),
        out_shape=jax.ShapeDtypeStruct((owners, count, share), bf16),
        compiler_params=params(),
        cost_estimate=cost(2 * count * rows * cols, rows * cols),
        name="out_product",
    )(left, levels, scale)


def gate_up_product(place, hidden, gain, gate, up, scale, added, runs, chips, paired):
    groups = len(hidden)
    rows = gate.shape[0]
    count = groups * hidden[0].shape[0]
    chunk = math.gcd(rows, BLOCK)
    extra = -(-4 * chips // LANES) * LANES
    units = [run * BLOCK for run in runs]
    widths = (2 * units[0], 2 * units[1] + extra)
    tile = chips * BLOCK
    staged = added is not None

    def kernel(place_ref, *refs):
        refs = list(refs)
        h_refs, refs = refs[:groups], refs[groups:]
        gain_ref, g_ref, u_ref, s_ref = refs[:4]
        a_refs = refs[4:6] if staged else (None, None)
        o_refs = refs[6:-2] if staged else refs[4:-2]
        x_ref, p_ref = refs[-2:]
        step = pl.program_id(0)
        odd = place_ref[0]

        @pl.when(step == 0)
        def _():
            values = [ref[...].astype(f32) for ref in h_refs]
            if groups == 2:
                first = place_ref[1] == 0
                values = [
                    jnp.where(first, values[0], values[1]),
                    jnp.where(first, values[1], values[0]),
                ]
            states = jnp.concatenate(values, axis=0)
            left = (states * gain_ref[...]).astype(bf16)
            if paired:
                turned = jnp.concatenate([left[:, chunk:], left[:, :chunk]], axis=1)
                left = jnp.where(odd == 1, turned, left)
            x_ref[...] = left
            squares = jnp.sum(states * states, axis=1, keepdims=True)
            high = squares.astype(bf16).astype(f32)
            lane = lax.broadcasted_iota(jnp.int32, (count, extra), 1)
            at = 2 * place_ref[3]
            p_ref[...] = jnp.where(
                lane == at, high, jnp.where(lane == at + 1, squares - high, 0.0)
            )

        if paired:
            whole = rows // BLOCK
            blocks = [
                (odd * chunk + j * BLOCK, j * BLOCK, BLOCK, odd + 2 * j) for j in range(whole)
            ]
            blocks.append(
                ((1 - odd) * whole * BLOCK, whole * BLOCK, chunk, (1 - odd) * 2 * whole)
            )
        else:
            blocks = [(j * chunk, j * chunk, chunk, j) for j in range(rows // chunk)]
        totals = []
        for a, ref in enumerate((g_ref, u_ref)):
            total = None
            for start, x_at, size, s_at in blocks:
                if paired:
                    start = pl.multiple_of(start, chunk)
                part = jnp.dot(
                    x_ref[:, pl.ds(x_at, size)],
                    ref[pl.ds(start, size), :].astype(bf16),
                    preferred_element_type=f32,
                )
                part = part * s_ref[a, pl.ds(s_at, 1), :]
                total = part if total is None else total + part
            totals.append(total)

        def write(run, block, ref, position, q):
            values = [
                (a * units[run] + block * BLOCK, total[:, q * BLOCK : (q + 1) * BLOCK])
                for a, total in enumerate(totals)
            ]
            if run == 1 and block == 0:
                values.append((2 * units[1], p_ref[...]))
            for start, value in values:
                lanes = pl.ds(start, value.shape[1])
                if staged:
                    value = value + a_refs[run][q, :, lanes].astype(f32)
                ref[position, :, lanes] = value.astype(bf16)

        def write_first(block):
            for q in range(chips):
                if not staged:
                    write(0, block, o_refs[0], q, q)
                    continue
                away = q ^ place_ref[2]
                position, rest = 0, away // 2
                for _ in range(chips.bit_length() - 2):
                    position, rest = position * 2 + rest % 2, rest // 2
                for side in range(2):
                    pl.when(away % 2 == side)(
                        functools.partial(write, 0, block, o_refs[side], position, q)
                    )

        def write_second(block):
            for q in range(chips):
                write(1, block, o_refs[-1], q, q)

        for block in range(runs[0]):
            pl.when(step == block)(functools.partial(write_first, block))
        for block in range(runs[1]):
            pl.when(step == runs[0] + block)(functools.partial(write_second, block))

    fixed = lambda i, p: (0, 0)
    whole_of = lambda shape: pl.BlockSpec(shape, lambda i, p: (0, 0, 0))
    run_shapes = [(chips, count, width) for width in widths]
    out_shapes = list(run_shapes)
    if staged:
        out_shapes[:1] = [(chips // 2, count, widths[0])] * 2
    return pl.pallas_call(
        kernel,
        grid_spec=pltpu.PrefetchScalarGridSpec(
            num_scalar_prefetch=1,
            grid=(sum(runs),),
            in_specs=[pl.BlockSpec(x.shape, fixed) for x in hidden]
            + [
                pl.BlockSpec((1, rows), fixed),
                pl.BlockSpec((rows, tile), lambda i, p: (0, i)),
                pl.BlockSpec((rows, tile), lambda i, p: (0, i)),
                pl.BlockSpec((2, 8, tile), lambda i, p: (0, 0, i)),
            ]
            + ([whole_of(shape) for shape in run_shapes] if staged else []),
            out_specs=[whole_of(shape) for shape in out_shapes],
            scratch_shapes=[pltpu.VMEM((count, rows), bf16), pltpu.VMEM((count, extra), f32)],
        ),
        out_shape=[jax.ShapeDtypeStruct(shape, bf16) for shape in out_shapes],
        compiler_params=params(),
        cost_estimate=cost(4 * count * rows * gate.shape[1], 2 * rows * gate.shape[1]),
        name="gate_up_product",
    )(place, *hidden, gain, gate, up, scale, *(added if staged else []))


def down_product(place, act, levels, scale, added, flip, states, mine):
    chips, count, units = act.shape
    hidden, width = levels.shape
    tile = chips * BLOCK
    blocks = units // BLOCK
    last = added is not None

    def kernel(place_ref, a_ref, l_ref, s_ref, *refs):
        step = pl.program_id(0)
        o_ref, total_ref = refs[-2:]
        total = jnp.zeros((count, width), f32)
        for q in range(chips):
            part = jnp.dot(
                a_ref[q],
                l_ref[pl.ds(q * BLOCK, BLOCK), :].astype(bf16),
                preferred_element_type=f32,
            )
            total = total + part * s_ref[pl.ds(q, 1), :]

        @pl.when(step == 0)
        def _():
            total_ref[...] = refs[0][...] + total if last else total

        @pl.when(step > 0)
        def _():
            total_ref[...] += total

        @pl.when(step == blocks - 1)
        def _():
            if not last:
                o_ref[...] = total_ref[...]
                return
            values = [ref[...].astype(f32) for ref in refs[1 : 1 + len(states)]]
            if len(states) == 2:
                first = place_ref[1] == 0
                values = [
                    jnp.where(first, values[0], values[1]),
                    jnp.where(first, values[1], values[0]),
                ]
            sums, values = total_ref[...], jnp.concatenate(values, axis=0)
            for b in range(count // mine):
                at = slice(b * mine, (b + 1) * mine)
                o_ref[b] = jnp.concatenate([sums[at], values[at]], axis=0).astype(bf16)

    def at(i, p):
        return 2 * i + (p[0] ^ flip)

    fixed = lambda shape: pl.BlockSpec(shape, lambda i, p: (0,) * len(shape))
    more = [added, *states] if last else []
    shape = (count // mine, 2 * mine, width) if last else (count, width)
    return pl.pallas_call(
        kernel,
        grid_spec=pltpu.PrefetchScalarGridSpec(
            num_scalar_prefetch=1,
            grid=(blocks,),
            in_specs=[
                pl.BlockSpec((chips, count, BLOCK), lambda i, p: (0, 0, i)),
                pl.BlockSpec((tile, width), lambda i, p: (at(i, p), 0)),
                pl.BlockSpec((chips, width), lambda i, p: (at(i, p), 0)),
            ]
            + [fixed(x.shape) for x in more],
            out_specs=fixed(shape),
            scratch_shapes=[pltpu.VMEM((count, width), f32)],
        ),
        out_shape=jax.ShapeDtypeStruct(shape, bf16 if last else f32),
        compiler_params=params(),
        cost_estimate=cost(2 * count * width * tile * blocks, width * tile * blocks),
        name="down_product",
    )(place, act, levels, scale, *more)


def attention(queries, kv_cache, new_kv, live):
    steps = queries.shape[0]
    factor = queries.shape[-1] ** (-0.5)
    keys = kv_cache[0]
    values = kv_cache[1]
    new_keys = new_kv[:, 0]
    new_values = new_kv[:, 1]
    position = jnp.arange(keys.shape[2], dtype=jnp.int32)
    valid = position[None, None, None, None, :] < live[None, :, None, None, None]
    cached = (
        jnp.einsum("nshqd,shcd->nshqc", queries, keys, preferred_element_type=f32) * factor
    )
    recent = (
        jnp.einsum("nshqd,tshd->nshqt", queries, new_keys, preferred_element_type=f32) * factor
    )
    order = jnp.arange(steps, dtype=jnp.int32)
    fresh = (order[None, :] <= order[:, None])[:, None, None, None, :]
    top = jnp.maximum(
        jnp.max(jnp.where(valid, cached, NEG), axis=-1),
        jnp.max(jnp.where(fresh, recent, NEG), axis=-1),
    )[..., None]
    e_cached = jnp.where(valid, jnp.exp(cached - top), 0.0)
    e_recent = jnp.where(fresh, jnp.exp(recent - top), 0.0)
    total = jnp.sum(e_cached, axis=-1, keepdims=True) + jnp.sum(e_recent, axis=-1, keepdims=True)
    p_cached = (e_cached / total).astype(bf16)
    p_recent = (e_recent / total).astype(bf16)
    mixed = jnp.einsum("nshqc,shcd->nshqd", p_cached, values, preferred_element_type=f32)
    mixed = mixed + jnp.einsum(
        "nshqt,tshd->nshqd", p_recent, new_values, preferred_element_type=f32
    )
    return mixed.astype(bf16)


def swap_cores(value):
    count = lax.axis_size("wide")
    return lax.ppermute(value, "wide", [(i, i ^ 1) for i in range(count)])


def exchange(value):
    return lax.all_to_all(value, "wide", split_axis=0, concat_axis=0, tiled=True)


def exchange_chips(value):
    count = lax.axis_size("wide")
    groups = [list(range(core, count, 2)) for core in range(2)]
    return lax.all_to_all(
        value, "wide", split_axis=0, concat_axis=0, tiled=True, axis_index_groups=groups
    )


def exchange_halves(keep, send, beside):
    count = lax.axis_size("wide")
    bit = 2
    while True:
        got = lax.ppermute(send, "wide", [(i, i ^ bit) for i in range(count)])
        if bit == 2:
            got, beside = lax.optimization_barrier((got, beside))
        total = keep.astype(f32) + got.astype(f32)
        bit *= 2
        if bit == count:
            return total[0], beside
        total = total.astype(bf16)
        half = total.shape[0] // 2
        keep, send = total[:half], total[half:]


def on_device(
    residual_in,
    norm_gain,
    gate_weight,
    up_weight,
    down_weight,
    out_weight,
    queries,
    kv_cache,
    new_kv,
    cache_len,
):
    owners = lax.axis_size("wide")
    groups = lax.axis_size("grp")
    me = lax.axis_index("wide")
    steps, seqs, width_dev = residual_in.shape
    seq_dev = seqs // owners
    tokens = steps * seqs
    mine = steps * seq_dev
    width = width_dev * owners
    chips = owners // 2
    hidden_units = gate_weight.shape[1]

    parts = groups if hidden_units % (groups * owners * 2 * BLOCK) == 0 else 1
    units = hidden_units // parts
    per_owner = units // (owners * BLOCK)
    runs = (per_owner - max(1, per_owner // 4), max(1, per_owner // 4))
    part = lax.axis_index("grp") if parts > 1 else jnp.zeros((), jnp.int32)
    place = jnp.stack([me % 2, part, me // 2, me]).astype(jnp.int32)

    live = lax.dynamic_slice_in_dim(cache_len, me * seq_dev, seq_dev, 0)
    attn_out = attention(queries, kv_cache, new_kv, live)
    heads = attn_out.reshape(steps, seq_dev, owners, -1)
    heads = exchange(jnp.transpose(heads, (2, 1, 0, 3)))

    out_levels, out_scale = out_levels_of(out_weight, pick_tile(out_weight.shape[1], 2560))
    heads, out_levels, out_scale = lax.optimization_barrier((heads, out_levels, out_scale))
    heads = heads.reshape(tokens, -1)
    projected = exchange(out_product(heads, out_levels, out_scale, owners))

    down = down_weight.T
    rows = gate_weight.shape[0]
    chunk = math.gcd(rows, BLOCK)
    tile = pick_tile(units, 2048)
    paired = pair_shares_blocks(rows) and down.shape[0] == rows
    if paired:
        edge = edge_max(place, [gate_weight, up_weight, down], units, chunk, pick_tile(units, 4096))
        edge, tops = swap_cores(edge), None
    else:
        edge, tops = None, joined_max(place, [gate_weight, up_weight], units, chunk, tile)

    def levels(flip, place):
        weights = [gate_weight, up_weight]
        return levels_of(place, weights, edge, tops, flip, units, chunk, chips * BLOCK)

    away_levels = levels(1, place)
    gain = lax.dynamic_slice_in_dim(norm_gain, me * width_dev, width_dev, 0).astype(f32)[None]
    residual = jnp.transpose(residual_in, (1, 0, 2)).reshape(tokens, width_dev).astype(f32)
    projected, away_levels, gain, residual = lax.optimization_barrier(
        (projected, away_levels, gain, residual)
    )
    hidden = (residual + jnp.sum(projected.astype(f32), axis=0)).astype(bf16)

    states = [hidden]
    if parts == 2:
        states.append(lax.ppermute(hidden, "grp", [(0, 1), (1, 0)]))
    elif parts > 1:
        states = [lax.all_gather(hidden, "grp", axis=0, tiled=True)]

    def product(levels, added):
        return gate_up_product(place, states, gain, *levels, added, runs, chips, paired)

    sent = product(away_levels, None)
    *sent, place = lax.optimization_barrier((*sent, place))
    sent = [swap_cores(value) for value in sent]
    sent[0], home_levels = lax.optimization_barrier((sent[0], levels(0, place)))
    keep, send, kept = product(home_levels, sent)
    kept, place = lax.optimization_barrier((kept, place))

    down_chunk = math.gcd(down.shape[0], BLOCK)
    down_tile = pick_tile(units, 4096)
    tops = None if paired else joined_max(place, [down], units, down_chunk, down_tile)
    down_levels, down_scale = down_levels_of(
        place, down, edge if paired else None, 2, tops, units, down_chunk, down_tile
    )
    last = exchange_chips(kept)
    first, (down_levels, down_scale) = exchange_halves(keep, send, (down_levels, down_scale))

    last = jnp.sum(last.astype(f32), axis=0)
    squares = jnp.sum(last[:, 2 * runs[1] * BLOCK :], axis=1, keepdims=True)
    scale = lax.rsqrt(squares / width + EPS_NORM)

    def act_of(summed, run):
        size = run * BLOCK
        gate = summed[:, :size] * scale
        up = summed[:, size : 2 * size] * scale
        return (jax.nn.silu(gate) * up).astype(bf16)

    act = jnp.concatenate([act_of(first, runs[0]), act_of(last, runs[1])], axis=1)
    act = exchange_chips(jnp.broadcast_to(act[None], (chips,) + act.shape))
    other = swap_cores(act)
    ffn = down_product(place, act, down_levels, down_scale, None, 0, states, mine)
    both = down_product(place, other, down_levels, down_scale, ffn, 1, states, mine)

    axes = ("grp", "wide") if parts > 1 else "wide"
    both = lax.all_to_all(both, axes, split_axis=0, concat_axis=0, tiled=True)
    both = both.reshape(parts, owners, 2, seq_dev, steps, width_dev)
    ffn = both[0, :, 0]
    if parts > 1:
        ffn = jnp.sum(both[:, :, 0].astype(f32), axis=0).astype(bf16)
    ffn_out = jnp.transpose(ffn, (2, 1, 0, 3)).reshape(steps, seq_dev, width)
    hidden_out = jnp.transpose(both[0, :, 1], (2, 1, 0, 3)).reshape(steps, seq_dev, width)
    return (ffn_out, attn_out, hidden_out)


def solution(mesh):
    placed = (
        P("grp", None, "wide"),
        P(),
        P("wide", None),
        P("wide", None),
        P(None, "wide"),
        P("wide", None),
        P("grp", "wide", None, None, None),
        P(None, ("grp", "wide"), None, None, None),
        P("grp", None, "wide", None, None),
        P("grp"),
    )
    return jax.shard_map(
        on_device,
        mesh=mesh,
        in_specs=placed,
        out_specs=(
            P("grp", "wide", None),
            P("grp", "wide", None, None, None),
            P("grp", "wide", None),
        ),
        check_vma=False,
    )
```

```python
import functools
import math

import jax
import jax.numpy as jnp
from jax import lax
from jax.experimental import pallas as pl
from jax.experimental.pallas import tpu as pltpu
from jax.sharding import PartitionSpec as P

BLOCK = 128
QMAX = 448.0
EPS_NORM = 1e-06
EPS_SCALE = 1e-06
NEG = -1e30
LANES = 128
VMEM = 56 * 2**20

f32 = jnp.float32
bf16 = jnp.bfloat16
f8 = jnp.float8_e4m3fn


def params(limit=VMEM):
    return pltpu.CompilerParams(vmem_limit_bytes=limit)


def in_hbm(*arrays):
    return [pltpu.with_memory_space_constraint(x, pltpu.HBM) for x in arrays]


def cost(flops, read):
    return pl.CostEstimate(flops=int(flops), bytes_accessed=int(read), transcendentals=0)


def pick_tile(cols, most):
    tile = most
    while cols % tile:
        tile -= LANES
    return tile


def spread_lanes(tops):
    out = []
    for g in range(tops.shape[1] // LANES):
        top = jnp.max(tops[:, g * LANES : (g + 1) * LANES], axis=1, keepdims=True)
        out.append(jnp.broadcast_to(top, (tops.shape[0], LANES)))
    return jnp.concatenate(out, axis=1)


def rows_max(ref, start, size):
    return jnp.max(jnp.abs(ref[pl.ds(start, size), :]), axis=0, keepdims=True).astype(f32)


def fill_rows(rows):
    return jnp.concatenate(rows + [rows[0]] * (8 - len(rows)), axis=0)


def chunk_max(place, weights, cols, chunk, tile):
    rows = weights[0].shape[0]
    parts = rows // chunk
    count = len(weights)
    steps = cols // tile

    def kernel(place_ref, *refs):
        for a in range(count):
            tops = [rows_max(refs[a], j * chunk, chunk) for j in range(parts)]
            refs[count][a] = spread_lanes(fill_rows(tops))

    return pl.pallas_call(
        kernel,
        grid_spec=pltpu.PrefetchScalarGridSpec(
            num_scalar_prefetch=1,
            grid=(steps,),
            in_specs=[pl.BlockSpec((rows, tile), lambda i, p: (0, p[1] * steps + i))] * count,
            out_specs=pl.BlockSpec((count, 8, tile), lambda i, p: (0, 0, i)),
        ),
        out_shape=jax.ShapeDtypeStruct((count, 8, cols), f32),
        compiler_params=params(),
        cost_estimate=cost(2 * count * rows * cols, 2 * count * rows * cols),
        name="chunk_max",
    )(place, *in_hbm(*weights))


def edge_max(place, weights, cols, chunk, tile):
    parts = weights[0].shape[0] // chunk
    count = len(weights)
    steps = cols // tile

    def kernel(place_ref, *refs):
        refs[count][...] = spread_lanes(
            fill_rows([rows_max(refs[a], 0, chunk) for a in range(count)])
        )

    return pl.pallas_call(
        kernel,
        grid_spec=pltpu.PrefetchScalarGridSpec(
            num_scalar_prefetch=1,
            grid=(steps,),
            in_specs=[
                pl.BlockSpec(
                    (chunk, tile), lambda i, p: ((1 - p[0]) * (parts - 1), p[1] * steps + i)
                )
            ]
            * count,
            out_specs=pl.BlockSpec((8, tile), lambda i, p: (0, i)),
        ),
        out_shape=jax.ShapeDtypeStruct((8, cols), f32),
        compiler_params=params(),
        cost_estimate=cost(2 * count * chunk * cols, 2 * count * chunk * cols),
        name="edge_max",
    )(place, *in_hbm(*weights))


def join_pair(w_ref, other, odd, chunk, parts):
    mine = [rows_max(w_ref, j * chunk, chunk) for j in range(parts)]
    joined = []
    for j in range(parts):
        even = mine[j ^ 1] if j ^ 1 < parts else other
        back = j - 1 if j % 2 == 0 else j + 1
        near = other if back < 0 else mine[back]
        joined.append(jnp.maximum(mine[j], jnp.where(odd, near, even)))
    return fill_rows(joined)


def block_scales(w_ref, top_ref, place_ref, a, paired, chunk, parts):
    if paired:
        other = top_ref[pl.ds(a, 1), :]
        tops = spread_lanes(join_pair(w_ref, other, place_ref[0] == 1, chunk, parts))
    else:
        tops = top_ref[a]
    largest = tops + EPS_SCALE
    return QMAX / largest, largest * (1.0 / QMAX)


def rounded_chunk(w_ref, j, chunk, factor, scale):
    value = w_ref[pl.ds(j * chunk, chunk), :].astype(f32) * factor[j : j + 1]
    return (value.astype(f8).astype(f32) * scale[j : j + 1]).astype(bf16)


def top_spec_of(tops, paired, tile, at):
    if paired:
        return pl.BlockSpec((tops.shape[0], tile), lambda i, p: (0, at(i, p)))
    return pl.BlockSpec((tops.shape[0], 8, tile), lambda i, p: (0, 0, at(i, p)))


def rounded_weights(place, weights, tops, paired, first, flip, cols, chunk, tile):
    rows = weights[0].shape[0]
    parts = rows // chunk
    count = len(weights)
    taken = 1 if flip is None else 2
    steps = cols // (taken * tile)

    def columns(i, p):
        return i if flip is None else (p[0] ^ flip) * steps + i

    def kernel(place_ref, *refs):
        for a in range(count):
            factor, scale = block_scales(
                refs[a], refs[count], place_ref, first + a, paired, chunk, parts
            )
            for j in range(parts):
                refs[count + 1 + a][pl.ds(j * chunk, chunk), :] = rounded_chunk(
                    refs[a], j, chunk, factor, scale
                )

    return pl.pallas_call(
        kernel,
        grid_spec=pltpu.PrefetchScalarGridSpec(
            num_scalar_prefetch=1,
            grid=(steps,),
            in_specs=[
                pl.BlockSpec((rows, tile), lambda i, p: (0, taken * p[1] * steps + columns(i, p)))
            ]
            * count
            + [top_spec_of(tops, paired, tile, columns)],
            out_specs=[pl.BlockSpec((rows, tile), lambda i, p: (0, i))] * count,
        ),
        out_shape=[jax.ShapeDtypeStruct((rows, cols // taken), bf16)] * count,
        compiler_params=params(),
        cost_estimate=cost(
            6 * count * rows * cols // taken, 4 * count * rows * cols // taken
        ),
        name="rounded_weights",
    )(place, *in_hbm(*weights), tops)


def join_group(parts, size, dim):
    count = lax.axis_size("wide")
    me = lax.axis_index("wide")
    share = parts.shape[dim]
    shape = list(parts.shape)
    shape[dim] = share * size
    out = jnp.zeros(shape, parts.dtype)
    out = lax.dynamic_update_slice_in_dim(out, parts, (me % size) * share, dim)
    for step in range(1, size):
        perm = [(i // size * size + (i + step) % size, i) for i in range(count)]
        got = lax.ppermute(parts, "wide", perm)
        out = lax.dynamic_update_slice_in_dim(out, got, ((me + step) % size) * share, dim)
    return out


def pair_shares_blocks(rows):
    return math.lcm(rows, BLOCK) == 2 * rows and math.gcd(rows, BLOCK) == BLOCK // 2


def joined_max(place, weights, cols, chunk, tile):
    rows = weights[0].shape[0]
    size = math.lcm(rows, BLOCK) // rows
    per = BLOCK // chunk
    parts = rows // chunk
    tops = chunk_max(place, weights, cols, chunk, tile)
    if size == 1:
        return tops
    joined = join_group(tops[:, :parts], size, 1)
    blocks = joined.reshape(joined.shape[0], -1, per, joined.shape[2])
    joined = jnp.broadcast_to(jnp.max(blocks, axis=2, keepdims=True), blocks.shape)
    joined = joined.reshape(joined.shape[0], size * parts, -1)
    own = lax.dynamic_slice_in_dim(joined, (lax.axis_index("wide") % size) * parts, parts, 1)
    return jnp.pad(own, ((0, 0), (0, 8 - parts), (0, 0)))


def out_levels_of(weight, tile):
    rows, cols = weight.shape
    parts = rows // BLOCK

    def kernel(w_ref, o_ref, s_ref):
        tops = spread_lanes(fill_rows([rows_max(w_ref, j * BLOCK, BLOCK) for j in range(parts)]))
        largest = tops + EPS_SCALE
        factor = QMAX / largest
        s_ref[...] = largest * (1.0 / QMAX)
        for j in range(parts):
            at = pl.ds(j * BLOCK, BLOCK)
            o_ref[at, :] = (w_ref[at, :].astype(f32) * factor[j : j + 1]).astype(f8)

    columns = lambda i: (0, i)
    return pl.pallas_call(
        kernel,
        grid=(cols // tile,),
        in_specs=[pl.BlockSpec((rows, tile), columns)],
        out_specs=[pl.BlockSpec((rows, tile), columns), pl.BlockSpec((8, tile), columns)],
        out_shape=[
            jax.ShapeDtypeStruct((rows, cols), f8),
            jax.ShapeDtypeStruct((8, cols), f32),
        ],
        compiler_params=params(),
        cost_estimate=cost(8 * rows * cols, 3 * rows * cols),
        name="out_levels_of",
    )(*in_hbm(weight))


def out_product(left, levels, scale, owners):
    count, rows = left.shape
    cols = levels.shape[1]
    parts = rows // BLOCK
    share = cols // owners
    tile = pick_tile(cols, 4 * math.lcm(share, LANES))
    per = tile // share

    def kernel(x_ref, l_ref, s_ref, o_ref):
        total = None
        for j in range(parts):
            at = pl.ds(j * BLOCK, BLOCK)
            part = jnp.dot(x_ref[:, at], l_ref[at, :].astype(bf16), preferred_element_type=f32)
            part = part * s_ref[pl.ds(j, 1), :]
            total = part if total is None else total + part
        total = total.astype(bf16)
        for q in range(per):
            o_ref[q] = total[:, q * share : (q + 1) * share]

    return pl.pallas_call(
        kernel,
        grid=(cols // tile,),
        in_specs=[
            pl.BlockSpec((count, rows), lambda i: (0, 0)),
            pl.BlockSpec((rows, tile), lambda i: (0, i)),
            pl.BlockSpec((8, tile), lambda i: (0, i)),
        ],
        out_specs=pl.BlockSpec((per, count, share), lambda i: (i, 0, 0)),
        out_shape=jax.ShapeDtypeStruct((owners, count, share), bf16),
        compiler_params=params(),
        cost_estimate=cost(2 * count * rows * cols, rows * cols),
        name="out_product",
    )(left, levels, scale)


def gate_up_product(place, hidden, gain, gate, up, tops, runs, chips, paired, cols):
    groups = len(hidden)
    rows = gate.shape[0]
    count = groups * hidden[0].shape[0]
    chunk = math.gcd(rows, BLOCK)
    parts = rows // chunk
    extra = -(-4 * chips // LANES) * LANES
    units = [run * BLOCK for run in runs]
    widths = (2 * units[0], 2 * units[1] + extra)
    together = 2 if sum(runs) % 2 == 0 else 1
    tile = together * chips * BLOCK

    def kernel(place_ref, *refs):
        h_refs = refs[:groups]
        gain_ref, g_ref, u_ref = refs[groups : groups + 3]
        o_refs, x_ref, p_ref = refs[-4:-2], refs[-2], refs[-1]
        step = pl.program_id(0)

        @pl.when(step == 0)
        def _():
            values = [ref[...].astype(f32) for ref in h_refs]
            if groups == 2:
                first = place_ref[1] == 0
                values = [
                    jnp.where(first, values[0], values[1]),
                    jnp.where(first, values[1], values[0]),
                ]
            states = jnp.concatenate(values, axis=0)
            x_ref[...] = (states * gain_ref[...]).astype(bf16)
            squares = jnp.sum(states * states, axis=1, keepdims=True)
            high = squares.astype(bf16).astype(f32)
            lane = lax.broadcasted_iota(jnp.int32, (count, extra), 1)
            at = 2 * place_ref[3]
            p_ref[...] = jnp.where(
                lane == at, high, jnp.where(lane == at + 1, squares - high, 0.0)
            )

        totals = []
        for a, ref in enumerate((g_ref, u_ref)):
            if tops is None:
                weight = ref[...]
            else:
                factor, scale = block_scales(
                    ref, refs[groups + 3], place_ref, a, paired, chunk, parts
                )
                weight = jnp.concatenate(
                    [rounded_chunk(ref, j, chunk, factor, scale) for j in range(parts)], axis=0
                )
            totals.append(jnp.dot(x_ref[...], weight, preferred_element_type=f32))

        def write(run, block, position, q):
            ref = o_refs[run]
            at = ((runs[0] * run + block) % together * chips + q) * BLOCK
            for a, total in enumerate(totals):
                lanes = pl.ds(a * units[run] + block * BLOCK, BLOCK)
                ref[position, :, lanes] = total[:, at : at + BLOCK].astype(bf16)
            if run == 1 and block == 0:
                ref[position, :, pl.ds(2 * units[1], extra)] = p_ref[...].astype(bf16)

        def write_first(block):
            for q in range(chips):
                position, rest = 0, q ^ place_ref[2]
                for _ in range(chips.bit_length() - 1):
                    position, rest = position * 2 + rest % 2, rest // 2
                write(0, block, position, q)

        def write_second(block):
            for q in range(chips):
                write(1, block, q, q)

        for block in range(runs[0]):
            pl.when(step == block // together)(functools.partial(write_first, block))
        for block in range(runs[1]):
            pl.when(step == (runs[0] + block) // together)(
                functools.partial(write_second, block)
            )

    steps = sum(runs) // together
    home = lambda i, p: p[0] * steps + i
    fixed = lambda i, p: (0, 0)
    out_shapes = [(chips, count, width) for width in widths]
    if tops is None:
        weight_spec = pl.BlockSpec((rows, tile), lambda i, p: (0, i))
    else:
        weight_spec = pl.BlockSpec((rows, tile), lambda i, p: (0, 2 * p[1] * steps + home(i, p)))
    in_specs = [pl.BlockSpec(x.shape, fixed) for x in hidden]
    in_specs += [pl.BlockSpec((1, rows), fixed), weight_spec, weight_spec]
    if tops is not None:
        in_specs.append(top_spec_of(tops, paired, tile, home))
    return pl.pallas_call(
        kernel,
        grid_spec=pltpu.PrefetchScalarGridSpec(
            num_scalar_prefetch=1,
            grid=(steps,),
            in_specs=in_specs,
            out_specs=[pl.BlockSpec(shape, lambda i, p: (0, 0, 0)) for shape in out_shapes],
            scratch_shapes=[pltpu.VMEM((count, rows), bf16), pltpu.VMEM((count, extra), f32)],
        ),
        out_shape=[jax.ShapeDtypeStruct(shape, bf16) for shape in out_shapes],
        compiler_params=params(),
        cost_estimate=cost(4 * count * rows * cols // 2, 2 * rows * cols),
        name="gate_up_product",
    )(place, *hidden, gain, *in_hbm(gate, up), *([] if tops is None else [tops]))


def down_product(place, act, weight, added, states, mine):
    chips, count, units = act.shape
    width = weight.shape[0]
    together = 2 if units % (2 * BLOCK) == 0 else 1
    tile = together * chips * BLOCK
    steps = units // (together * BLOCK)
    last = added is not None

    def kernel(place_ref, a_ref, w_ref, *refs):
        step = pl.program_id(0)
        o_ref, total_ref = refs[-2:]
        total = lax.dot_general(
            jnp.concatenate(
                [
                    a_ref[q, :, pl.ds(t * BLOCK, BLOCK)]
                    for t in range(together)
                    for q in range(chips)
                ],
                axis=1,
            ),
            w_ref[...],
            (((1,), (1,)), ((), ())),
            preferred_element_type=f32,
        )

        @pl.when(step == 0)
        def _():
            total_ref[...] = refs[0][...] + total if last else total

        @pl.when(step > 0)
        def _():
            total_ref[...] += total

        @pl.when(step == steps - 1)
        def _():
            if not last:
                o_ref[...] = total_ref[...]
                return
            values = [ref[...].astype(f32) for ref in refs[1 : 1 + len(states)]]
            if len(states) == 2:
                first = place_ref[1] == 0
                values = [
                    jnp.where(first, values[0], values[1]),
                    jnp.where(first, values[1], values[0]),
                ]
            sums, values = total_ref[...], jnp.concatenate(values, axis=0)
            for b in range(count // mine):
                at = slice(b * mine, (b + 1) * mine)
                o_ref[b] = jnp.concatenate([sums[at], values[at]], axis=0).astype(bf16)

    fixed = lambda shape: pl.BlockSpec(shape, lambda i, p: (0,) * len(shape))
    more = [added, *states] if last else []
    shape = (count // mine, 2 * mine, width) if last else (count, width)
    return pl.pallas_call(
        kernel,
        grid_spec=pltpu.PrefetchScalarGridSpec(
            num_scalar_prefetch=1,
            grid=(steps,),
            in_specs=[
                pl.BlockSpec((chips, count, together * BLOCK), lambda i, p: (0, 0, i)),
                pl.BlockSpec((width, tile), lambda i, p: (0, i)),
            ]
            + [fixed(x.shape) for x in more],
            out_specs=fixed(shape),
            scratch_shapes=[pltpu.VMEM((count, width), f32)],
        ),
        out_shape=jax.ShapeDtypeStruct(shape, bf16 if last else f32),
        compiler_params=params(16 * 2**20),
        cost_estimate=cost(2 * count * width * tile * steps, 2 * width * tile * steps),
        name="down_product",
    )(place, act, weight, *more)


def attention(queries, kv_cache, new_kv, live):
    steps = queries.shape[0]
    factor = queries.shape[-1] ** (-0.5)
    keys = kv_cache[0]
    values = kv_cache[1]
    new_keys = new_kv[:, 0]
    new_values = new_kv[:, 1]
    position = jnp.arange(keys.shape[2], dtype=jnp.int32)
    valid = position[None, None, None, None, :] < live[None, :, None, None, None]
    cached = (
        jnp.einsum("nshqd,shcd->nshqc", queries, keys, preferred_element_type=f32) * factor
    )
    recent = (
        jnp.einsum("nshqd,tshd->nshqt", queries, new_keys, preferred_element_type=f32) * factor
    )
    order = jnp.arange(steps, dtype=jnp.int32)
    fresh = (order[None, :] <= order[:, None])[:, None, None, None, :]
    top = jnp.maximum(
        jnp.max(jnp.where(valid, cached, NEG), axis=-1),
        jnp.max(jnp.where(fresh, recent, NEG), axis=-1),
    )[..., None]
    e_cached = jnp.where(valid, jnp.exp(cached - top), 0.0)
    e_recent = jnp.where(fresh, jnp.exp(recent - top), 0.0)
    total = jnp.sum(e_cached, axis=-1, keepdims=True) + jnp.sum(e_recent, axis=-1, keepdims=True)
    p_cached = (e_cached / total).astype(bf16)
    p_recent = (e_recent / total).astype(bf16)
    mixed = jnp.einsum("nshqc,shcd->nshqd", p_cached, values, preferred_element_type=f32)
    mixed = mixed + jnp.einsum(
        "nshqt,tshd->nshqd", p_recent, new_values, preferred_element_type=f32
    )
    return mixed.astype(bf16)


def swap_cores(value):
    count = lax.axis_size("wide")
    return lax.ppermute(value, "wide", [(i, i ^ 1) for i in range(count)])


def exchange(value):
    return lax.all_to_all(value, "wide", split_axis=0, concat_axis=0, tiled=True)


def exchange_chips(value):
    count = lax.axis_size("wide")
    groups = [list(range(core, count, 2)) for core in range(2)]
    return lax.all_to_all(
        value, "wide", split_axis=0, concat_axis=0, tiled=True, axis_index_groups=groups
    )


def exchange_halves(kept, got, send, beside):
    count = lax.axis_size("wide")
    bit = 2
    while True:
        half = kept.shape[0] // 2
        received = lax.ppermute(send, "wide", [(i, i ^ bit) for i in range(count)])
        if bit == 2:
            received, beside = lax.optimization_barrier((received, beside))
        total = kept[:half].astype(f32) + received.astype(f32)
        if got is not None:
            total = total + got[:half].astype(f32)
        got = None
        bit *= 2
        if bit == count:
            return total[0], beside
        kept = total.astype(bf16)
        send = kept[half // 2 :]


def on_device(
    residual_in,
    norm_gain,
    gate_weight,
    up_weight,
    down_weight,
    out_weight,
    queries,
    kv_cache,
    new_kv,
    cache_len,
):
    owners = lax.axis_size("wide")
    groups = lax.axis_size("grp")
    me = lax.axis_index("wide")
    steps, seqs, width_dev = residual_in.shape
    seq_dev = seqs // owners
    tokens = steps * seqs
    mine = steps * seq_dev
    width = width_dev * owners
    chips = owners // 2
    hidden_units = gate_weight.shape[1]

    parts = groups if hidden_units % (groups * owners * 2 * BLOCK) == 0 else 1
    units = hidden_units // parts
    per_owner = units // (owners * BLOCK)
    runs = (per_owner - max(1, per_owner // 4), max(1, per_owner // 4))
    part = lax.axis_index("grp") if parts > 1 else jnp.zeros((), jnp.int32)
    place = jnp.stack([me % 2, part, me // 2, me]).astype(jnp.int32)

    live = lax.dynamic_slice_in_dim(cache_len, me * seq_dev, seq_dev, 0)
    attn_out = attention(queries, kv_cache, new_kv, live)
    heads = attn_out.reshape(steps, seq_dev, owners, -1)
    heads = exchange(jnp.transpose(heads, (2, 1, 0, 3)))

    out_levels, out_scale = out_levels_of(out_weight, pick_tile(out_weight.shape[1], 2560))
    heads, out_levels, out_scale = lax.optimization_barrier((heads, out_levels, out_scale))
    heads = heads.reshape(tokens, -1)
    projected = exchange(out_product(heads, out_levels, out_scale, owners))

    down = down_weight.T
    rows = gate_weight.shape[0]
    chunk = math.gcd(rows, BLOCK)
    tile = pick_tile(units, 2048)
    paired = pair_shares_blocks(rows) and down.shape[0] == rows
    weights = [gate_weight, up_weight]
    if paired:
        tops = edge_max(place, [*weights, down], units, chunk, pick_tile(units, 4096))
        tops = swap_cores(tops)
    else:
        tops = joined_max(place, weights, units, chunk, tile)
    away = rounded_weights(
        place, weights, tops, paired, 0, 1, units, chunk, pick_tile(units // 2, 2048)
    )
    gain = lax.dynamic_slice_in_dim(norm_gain, me * width_dev, width_dev, 0).astype(f32)[None]
    residual = jnp.transpose(residual_in, (1, 0, 2)).reshape(tokens, width_dev).astype(f32)
    projected, away, gain, residual = lax.optimization_barrier(
        (projected, away, gain, residual)
    )
    hidden = (residual + jnp.sum(projected.astype(f32), axis=0)).astype(bf16)

    states = [hidden]
    if parts == 2:
        states.append(lax.ppermute(hidden, "grp", [(0, 1), (1, 0)]))
    elif parts > 1:
        states = [lax.all_gather(hidden, "grp", axis=0, tiled=True)]

    def product(weights, tops):
        return gate_up_product(place, states, gain, *weights, tops, runs, chips, paired, units)

    got = [swap_cores(value) for value in product(away, None)]
    kept = list(product(weights, tops))
    half = chips // 2
    send = (kept[0][half:].astype(f32) + got[0][half:].astype(f32)).astype(bf16)
    send, kept[1], got[1] = lax.optimization_barrier((send, kept[1], got[1]))
    second = (kept[1].astype(f32) + got[1].astype(f32)).astype(bf16)
    second, place = lax.optimization_barrier((second, place))

    down_chunk = math.gcd(down.shape[0], BLOCK)
    row = 2
    if not paired:
        tops, row = joined_max(place, [down], units, down_chunk, pick_tile(units, 4096)), 0
    home, away = [
        rounded_weights(
            place, [down], tops, paired, row, flip, units, down_chunk, pick_tile(units // 2, 4096)
        )[0]
        for flip in range(2)
    ]
    last = exchange_chips(second)
    first, (home, away) = exchange_halves(kept[0], got[0], send, (home, away))

    last = jnp.sum(last.astype(f32), axis=0)
    squares = jnp.sum(last[:, 2 * runs[1] * BLOCK :], axis=1, keepdims=True)
    scale = lax.rsqrt(squares / width + EPS_NORM)

    def act_of(summed, run):
        size = run * BLOCK
        gate = summed[:, :size] * scale
        up = summed[:, size : 2 * size] * scale
        return (jax.nn.silu(gate) * up).astype(bf16)

    act = jnp.concatenate([act_of(first, runs[0]), act_of(last, runs[1])], axis=1)
    act = exchange_chips(jnp.broadcast_to(act[None], (chips,) + act.shape))
    other = swap_cores(act)
    ffn = down_product(place, act, home, None, states, mine)
    both = down_product(place, other, away, ffn, states, mine)

    axes = ("grp", "wide") if parts > 1 else "wide"
    both = lax.all_to_all(both, axes, split_axis=0, concat_axis=0, tiled=True)
    both = both.reshape(parts, owners, 2, seq_dev, steps, width_dev)
    ffn = both[0, :, 0]
    if parts > 1:
        ffn = jnp.sum(both[:, :, 0].astype(f32), axis=0).astype(bf16)
    ffn_out = jnp.transpose(ffn, (2, 1, 0, 3)).reshape(steps, seq_dev, width)
    hidden_out = jnp.transpose(both[0, :, 1], (2, 1, 0, 3)).reshape(steps, seq_dev, width)
    return (ffn_out, attn_out, hidden_out)


def solution(mesh):
    placed = (
        P("grp", None, "wide"),
        P(),
        P("wide", None),
        P("wide", None),
        P(None, "wide"),
        P("wide", None),
        P("grp", "wide", None, None, None),
        P(None, ("grp", "wide"), None, None, None),
        P("grp", None, "wide", None, None),
        P("grp"),
    )
    return jax.shard_map(
        on_device,
        mesh=mesh,
        in_specs=placed,
        out_specs=(
            P("grp", "wide", None),
            P("grp", "wide", None, None, None),
            P("grp", "wide", None),
        ),
        check_vma=False,
    )
```

```python
import functools
import math

import jax
import jax.numpy as jnp
from jax import lax
from jax.experimental import pallas as pl
from jax.experimental.pallas import tpu as pltpu
from jax.sharding import PartitionSpec as P

BLOCK = 128
QMAX = 448.0
EPS_NORM = 1e-06
EPS_SCALE = 1e-06
NEG = -1e30
LANES = 128
VMEM = 56 * 2**20

f32 = jnp.float32
bf16 = jnp.bfloat16
f8 = jnp.float8_e4m3fn


def params(limit=VMEM):
    return pltpu.CompilerParams(vmem_limit_bytes=limit)


def in_hbm(*arrays):
    return [pltpu.with_memory_space_constraint(x, pltpu.HBM) for x in arrays]


def in_vmem(*arrays):
    return [pltpu.with_memory_space_constraint(x, pltpu.VMEM) for x in arrays]


def cost(flops, read):
    return pl.CostEstimate(flops=int(flops), bytes_accessed=int(read), transcendentals=0)


def pick_tile(cols, most):
    tile = most
    while cols % tile:
        tile -= LANES
    return tile


def spread_lanes(tops):
    out = []
    for g in range(tops.shape[1] // LANES):
        top = jnp.max(tops[:, g * LANES : (g + 1) * LANES], axis=1, keepdims=True)
        out.append(jnp.broadcast_to(top, (tops.shape[0], LANES)))
    return jnp.concatenate(out, axis=1)


def rows_max(ref, start, size):
    return jnp.max(jnp.abs(ref[pl.ds(start, size), :]), axis=0, keepdims=True).astype(f32)


def fill_rows(rows):
    return jnp.concatenate(rows + [rows[0]] * (8 - len(rows)), axis=0)


def chunk_max(place, weights, cols, chunk, tile):
    rows = weights[0].shape[0]
    parts = rows // chunk
    count = len(weights)
    steps = cols // tile

    def kernel(place_ref, *refs):
        for a in range(count):
            tops = [rows_max(refs[a], j * chunk, chunk) for j in range(parts)]
            refs[count][a] = spread_lanes(fill_rows(tops))

    return pl.pallas_call(
        kernel,
        grid_spec=pltpu.PrefetchScalarGridSpec(
            num_scalar_prefetch=1,
            grid=(steps,),
            in_specs=[pl.BlockSpec((rows, tile), lambda i, p: (0, p[1] * steps + i))] * count,
            out_specs=pl.BlockSpec((count, 8, tile), lambda i, p: (0, 0, i)),
        ),
        out_shape=jax.ShapeDtypeStruct((count, 8, cols), f32),
        compiler_params=params(),
        cost_estimate=cost(2 * count * rows * cols, 2 * count * rows * cols),
        name="chunk_max",
    )(place, *in_hbm(*weights))


def edge_max(place, weights, cols, chunk, tile):
    parts = weights[0].shape[0] // chunk
    count = len(weights)
    steps = cols // tile

    def kernel(place_ref, *refs):
        refs[count][...] = spread_lanes(
            fill_rows([rows_max(refs[a], 0, chunk) for a in range(count)])
        )

    return pl.pallas_call(
        kernel,
        grid_spec=pltpu.PrefetchScalarGridSpec(
            num_scalar_prefetch=1,
            grid=(steps,),
            in_specs=[
                pl.BlockSpec(
                    (chunk, tile), lambda i, p: ((1 - p[0]) * (parts - 1), p[1] * steps + i)
                )
            ]
            * count,
            out_specs=pl.BlockSpec((8, tile), lambda i, p: (0, i)),
        ),
        out_shape=jax.ShapeDtypeStruct((8, cols), f32),
        compiler_params=params(),
        cost_estimate=cost(2 * count * chunk * cols, 2 * count * chunk * cols),
        name="edge_max",
    )(place, *in_hbm(*weights))


def join_pair(w_ref, other, odd, chunk, parts):
    mine = [rows_max(w_ref, j * chunk, chunk) for j in range(parts)]
    joined = []
    for j in range(parts):
        even = mine[j ^ 1] if j ^ 1 < parts else other
        back = j - 1 if j % 2 == 0 else j + 1
        near = other if back < 0 else mine[back]
        joined.append(jnp.maximum(mine[j], jnp.where(odd, near, even)))
    return fill_rows(joined)


def block_scales(w_ref, top_ref, place_ref, a, paired, chunk, parts):
    if paired:
        other = top_ref[pl.ds(a, 1), :]
        tops = spread_lanes(join_pair(w_ref, other, place_ref[0] == 1, chunk, parts))
    else:
        tops = top_ref[a]
    largest = tops + EPS_SCALE
    return QMAX / largest, largest * (1.0 / QMAX)


def rounded_chunk(w_ref, j, chunk, factor, scale):
    value = w_ref[pl.ds(j * chunk, chunk), :].astype(f32) * factor[j : j + 1]
    return (value.astype(f8).astype(f32) * scale[j : j + 1]).astype(bf16)


def top_spec_of(tops, paired, tile, at):
    if paired:
        return pl.BlockSpec((tops.shape[0], tile), lambda i, p: (0, at(i, p)))
    return pl.BlockSpec((tops.shape[0], 8, tile), lambda i, p: (0, 0, at(i, p)))


def rounded_weights(place, weights, tops, paired, first, flip, cols, chunk, tile):
    rows = weights[0].shape[0]
    parts = rows // chunk
    count = len(weights)
    taken = 1 if flip is None else 2
    steps = cols // (taken * tile)

    def columns(i, p):
        return i if flip is None else (p[0] ^ flip) * steps + i

    def kernel(place_ref, *refs):
        for a in range(count):
            factor, scale = block_scales(
                refs[a], refs[count], place_ref, first + a, paired, chunk, parts
            )
            for j in range(parts):
                refs[count + 1 + a][pl.ds(j * chunk, chunk), :] = rounded_chunk(
                    refs[a], j, chunk, factor, scale
                )

    return pl.pallas_call(
        kernel,
        grid_spec=pltpu.PrefetchScalarGridSpec(
            num_scalar_prefetch=1,
            grid=(steps,),
            in_specs=[
                pl.BlockSpec((rows, tile), lambda i, p: (0, taken * p[1] * steps + columns(i, p)))
            ]
            * count
            + [top_spec_of(tops, paired, tile, columns)],
            out_specs=[pl.BlockSpec((rows, tile), lambda i, p: (0, i))] * count,
        ),
        out_shape=[jax.ShapeDtypeStruct((rows, cols // taken), bf16)] * count,
        compiler_params=params(),
        cost_estimate=cost(
            6 * count * rows * cols // taken, 4 * count * rows * cols // taken
        ),
        name="rounded_weights",
    )(place, *in_hbm(*weights), *in_vmem(tops))


def join_group(parts, size, dim):
    count = lax.axis_size("wide")
    me = lax.axis_index("wide")
    share = parts.shape[dim]
    shape = list(parts.shape)
    shape[dim] = share * size
    out = jnp.zeros(shape, parts.dtype)
    out = lax.dynamic_update_slice_in_dim(out, parts, (me % size) * share, dim)
    for step in range(1, size):
        perm = [(i // size * size + (i + step) % size, i) for i in range(count)]
        got = lax.ppermute(parts, "wide", perm)
        out = lax.dynamic_update_slice_in_dim(out, got, ((me + step) % size) * share, dim)
    return out


def pair_shares_blocks(rows):
    return math.lcm(rows, BLOCK) == 2 * rows and math.gcd(rows, BLOCK) == BLOCK // 2


def joined_max(place, weights, cols, chunk, tile):
    rows = weights[0].shape[0]
    size = math.lcm(rows, BLOCK) // rows
    per = BLOCK // chunk
    parts = rows // chunk
    tops = chunk_max(place, weights, cols, chunk, tile)
    if size == 1:
        return tops
    joined = join_group(tops[:, :parts], size, 1)
    blocks = joined.reshape(joined.shape[0], -1, per, joined.shape[2])
    joined = jnp.broadcast_to(jnp.max(blocks, axis=2, keepdims=True), blocks.shape)
    joined = joined.reshape(joined.shape[0], size * parts, -1)
    own = lax.dynamic_slice_in_dim(joined, (lax.axis_index("wide") % size) * parts, parts, 1)
    return jnp.pad(own, ((0, 0), (0, 8 - parts), (0, 0)))


def out_levels_of(weight, tile):
    rows, cols = weight.shape
    parts = rows // BLOCK

    def kernel(w_ref, o_ref, s_ref):
        tops = spread_lanes(fill_rows([rows_max(w_ref, j * BLOCK, BLOCK) for j in range(parts)]))
        largest = tops + EPS_SCALE
        factor = QMAX / largest
        s_ref[...] = largest * (1.0 / QMAX)
        for j in range(parts):
            at = pl.ds(j * BLOCK, BLOCK)
            o_ref[at, :] = (w_ref[at, :].astype(f32) * factor[j : j + 1]).astype(f8)

    columns = lambda i: (0, i)
    return pl.pallas_call(
        kernel,
        grid=(cols // tile,),
        in_specs=[pl.BlockSpec((rows, tile), columns)],
        out_specs=[pl.BlockSpec((rows, tile), columns), pl.BlockSpec((8, tile), columns)],
        out_shape=[
            jax.ShapeDtypeStruct((rows, cols), f8),
            jax.ShapeDtypeStruct((8, cols), f32),
        ],
        compiler_params=params(),
        cost_estimate=cost(8 * rows * cols, 3 * rows * cols),
        name="out_levels_of",
    )(*in_hbm(weight))


def out_product(left, levels, scale, owners):
    count, rows = left.shape
    cols = levels.shape[1]
    parts = rows // BLOCK
    share = cols // owners
    tile = pick_tile(cols, 4 * math.lcm(share, LANES))
    per = tile // share

    def kernel(x_ref, l_ref, s_ref, o_ref):
        total = None
        for j in range(parts):
            at = pl.ds(j * BLOCK, BLOCK)
            part = jnp.dot(x_ref[:, at], l_ref[at, :].astype(bf16), preferred_element_type=f32)
            part = part * s_ref[pl.ds(j, 1), :]
            total = part if total is None else total + part
        total = total.astype(bf16)
        for q in range(per):
            o_ref[q] = total[:, q * share : (q + 1) * share]

    return pl.pallas_call(
        kernel,
        grid=(cols // tile,),
        in_specs=[
            pl.BlockSpec((count, rows), lambda i: (0, 0)),
            pl.BlockSpec((rows, tile), lambda i: (0, i)),
            pl.BlockSpec((8, tile), lambda i: (0, i)),
        ],
        out_specs=pl.BlockSpec((per, count, share), lambda i: (i, 0, 0)),
        out_shape=jax.ShapeDtypeStruct((owners, count, share), bf16),
        compiler_params=params(),
        cost_estimate=cost(2 * count * rows * cols, rows * cols),
        name="out_product",
    )(left, levels, scale)


def gate_up_product(place, hidden, gain, gate, up, tops, runs, chips, paired, cols):
    groups = len(hidden)
    rows = gate.shape[0]
    count = groups * hidden[0].shape[0]
    chunk = math.gcd(rows, BLOCK)
    parts = rows // chunk
    extra = -(-4 * chips // LANES) * LANES
    units = [run * BLOCK for run in runs]
    widths = (2 * units[0], 2 * units[1] + extra)
    together = 2 if sum(runs) % 2 == 0 else 1
    tile = together * chips * BLOCK

    def kernel(place_ref, *refs):
        h_refs = refs[:groups]
        gain_ref, g_ref, u_ref = refs[groups : groups + 3]
        o_refs, x_ref, p_ref = refs[-4:-2], refs[-2], refs[-1]
        step = pl.program_id(0)

        @pl.when(step == 0)
        def _():
            values = [ref[...].astype(f32) for ref in h_refs]
            if groups == 2:
                first = place_ref[1] == 0
                values = [
                    jnp.where(first, values[0], values[1]),
                    jnp.where(first, values[1], values[0]),
                ]
            states = jnp.concatenate(values, axis=0)
            x_ref[...] = (states * gain_ref[...]).astype(bf16)
            squares = jnp.sum(states * states, axis=1, keepdims=True)
            high = squares.astype(bf16).astype(f32)
            lane = lax.broadcasted_iota(jnp.int32, (count, extra), 1)
            at = 2 * place_ref[3]
            p_ref[...] = jnp.where(
                lane == at, high, jnp.where(lane == at + 1, squares - high, 0.0)
            )

        totals = []
        for a, ref in enumerate((g_ref, u_ref)):
            if tops is None:
                weight = ref[...]
            else:
                factor, scale = block_scales(
                    ref, refs[groups + 3], place_ref, a, paired, chunk, parts
                )
                weight = jnp.concatenate(
                    [rounded_chunk(ref, j, chunk, factor, scale) for j in range(parts)], axis=0
                )
            totals.append(jnp.dot(x_ref[...], weight, preferred_element_type=f32))

        def write(run, block, position, q):
            ref = o_refs[run]
            at = ((runs[0] * run + block) % together * chips + q) * BLOCK
            for a, total in enumerate(totals):
                lanes = pl.ds(a * units[run] + block * BLOCK, BLOCK)
                ref[position, :, lanes] = total[:, at : at + BLOCK].astype(bf16)
            if run == 1 and block == 0:
                ref[position, :, pl.ds(2 * units[1], extra)] = p_ref[...].astype(bf16)

        def write_first(block):
            for q in range(chips):
                position, rest = 0, q ^ place_ref[2]
                for _ in range(chips.bit_length() - 1):
                    position, rest = position * 2 + rest % 2, rest // 2
                write(0, block, position, q)

        def write_second(block):
            for q in range(chips):
                write(1, block, q, q)

        for block in range(runs[0]):
            pl.when(step == block // together)(functools.partial(write_first, block))
        for block in range(runs[1]):
            pl.when(step == (runs[0] + block) // together)(
                functools.partial(write_second, block)
            )

    steps = sum(runs) // together
    home = lambda i, p: p[0] * steps + i
    fixed = lambda i, p: (0, 0)
    out_shapes = [(chips, count, width) for width in widths]
    if tops is None:
        weight_spec = pl.BlockSpec((rows, tile), lambda i, p: (0, i))
    else:
        weight_spec = pl.BlockSpec((rows, tile), lambda i, p: (0, 2 * p[1] * steps + home(i, p)))
    in_specs = [pl.BlockSpec(x.shape, fixed) for x in hidden]
    in_specs += [pl.BlockSpec((1, rows), fixed), weight_spec, weight_spec]
    if tops is not None:
        in_specs.append(top_spec_of(tops, paired, tile, home))
    return pl.pallas_call(
        kernel,
        grid_spec=pltpu.PrefetchScalarGridSpec(
            num_scalar_prefetch=1,
            grid=(steps,),
            in_specs=in_specs,
            out_specs=[pl.BlockSpec(shape, lambda i, p: (0, 0, 0)) for shape in out_shapes],
            scratch_shapes=[pltpu.VMEM((count, rows), bf16), pltpu.VMEM((count, extra), f32)],
        ),
        out_shape=[jax.ShapeDtypeStruct(shape, bf16) for shape in out_shapes],
        compiler_params=params(),
        cost_estimate=cost(4 * count * rows * cols // 2, 2 * rows * cols),
        name="gate_up_product",
    )(place, *in_vmem(*hidden), gain, *in_hbm(gate, up), *([] if tops is None else in_vmem(tops)))


def down_product(place, act, weight, added, states, mine):
    chips, count, units = act.shape
    width = weight.shape[0]
    together = 2 if units % (2 * BLOCK) == 0 else 1
    tile = together * chips * BLOCK
    steps = units // (together * BLOCK)
    last = added is not None

    def kernel(place_ref, a_ref, w_ref, *refs):
        step = pl.program_id(0)
        o_ref, total_ref = refs[-2:]
        total = lax.dot_general(
            jnp.concatenate(
                [
                    a_ref[q, :, pl.ds(t * BLOCK, BLOCK)]
                    for t in range(together)
                    for q in range(chips)
                ],
                axis=1,
            ),
            w_ref[...],
            (((1,), (1,)), ((), ())),
            preferred_element_type=f32,
        )

        @pl.when(step == 0)
        def _():
            total_ref[...] = refs[0][...] + total if last else total

        @pl.when(step > 0)
        def _():
            total_ref[...] += total

        @pl.when(step == steps - 1)
        def _():
            if not last:
                o_ref[...] = total_ref[...]
                return
            values = [ref[...].astype(f32) for ref in refs[1 : 1 + len(states)]]
            if len(states) == 2:
                first = place_ref[1] == 0
                values = [
                    jnp.where(first, values[0], values[1]),
                    jnp.where(first, values[1], values[0]),
                ]
            sums, values = total_ref[...], jnp.concatenate(values, axis=0)
            for b in range(count // mine):
                at = slice(b * mine, (b + 1) * mine)
                o_ref[b] = jnp.concatenate([sums[at], values[at]], axis=0).astype(bf16)

    fixed = lambda shape: pl.BlockSpec(shape, lambda i, p: (0,) * len(shape))
    more = [added, *states] if last else []
    shape = (count // mine, 2 * mine, width) if last else (count, width)
    return pl.pallas_call(
        kernel,
        grid_spec=pltpu.PrefetchScalarGridSpec(
            num_scalar_prefetch=1,
            grid=(steps,),
            in_specs=[
                pl.BlockSpec((chips, count, together * BLOCK), lambda i, p: (0, 0, i)),
                pl.BlockSpec((width, tile), lambda i, p: (0, i)),
            ]
            + [fixed(x.shape) for x in more],
            out_specs=fixed(shape),
            scratch_shapes=[pltpu.VMEM((count, width), f32)],
        ),
        out_shape=jax.ShapeDtypeStruct(shape, bf16 if last else f32),
        compiler_params=params(16 * 2**20),
        cost_estimate=cost(2 * count * width * tile * steps, 2 * width * tile * steps),
        name="down_product",
    )(place, act, weight, *more)


def attention(cache_len, queries, kv_cache, new_kv, owners):
    steps, seqs, heads, per, size = queries.shape
    slots = kv_cache.shape[3]
    factor = size ** (-0.5)
    share = heads * per // owners
    splits = 2 if heads % 2 == 0 and owners % 2 == 0 else 1
    mine = heads // splits
    rows = steps * per
    pad = 8 - steps

    def kernel(len_ref, q_ref, kv_ref, new_ref, o_ref, h_ref):
        live = len_ref[lax.axis_index("wide") * seqs + pl.program_id(0)]
        valid = lax.broadcasted_iota(jnp.int32, (rows, slots), 1) < live
        step_of = lax.broadcasted_iota(jnp.int32, (rows, 8), 0) // per
        fresh = lax.broadcasted_iota(jnp.int32, (rows, 8), 1) <= step_of

        def product(left, right, dim):
            return lax.dot_general(
                left, right, (((1,), (dim,)), ((), ())), preferred_element_type=f32
            )

        new = []
        for n in range(2):
            value = new_ref[:, n, 0].astype(f32)
            if splits == 2:
                value = jnp.where(pl.program_id(1) == 0, value[:, :mine], value[:, mine:])
            new.append(value)
        at = range(mine)
        queries_of = [
            q_ref[:, 0, h].astype(f32).reshape(rows, size).astype(bf16) for h in at
        ]
        new_keys, new_values = [
            [
                jnp.concatenate([value[:, h], jnp.zeros((pad, size), f32)], axis=0).astype(bf16)
                for h in at
            ]
            for value in new
        ]
        cached = [product(queries_of[h], kv_ref[0, 0, h], 1) for h in at]
        recent = [product(queries_of[h], new_keys[h], 1) for h in at]
        cached = [jnp.where(valid, value * factor, NEG) for value in cached]
        recent = [jnp.where(fresh, value * factor, NEG) for value in recent]
        top = [
            jnp.maximum(
                jnp.max(cached[h], axis=1, keepdims=True), jnp.max(recent[h], axis=1, keepdims=True)
            )
            for h in at
        ]
        cached = [jnp.exp(cached[h] - top[h]) for h in at]
        recent = [jnp.exp(recent[h] - top[h]) for h in at]
        share_of = [
            1.0
            / (
                jnp.sum(cached[h], axis=1, keepdims=True)
                + jnp.sum(recent[h], axis=1, keepdims=True)
            )
            for h in at
        ]
        cached = [(cached[h] * share_of[h]).astype(bf16) for h in at]
        recent = [(recent[h] * share_of[h]).astype(bf16) for h in at]
        mixed = [
            product(cached[h], kv_ref[1, 0, h], 0) + product(recent[h], new_values[h], 0)
            for h in at
        ]
        for h in at:
            value = mixed[h].reshape(steps, per, size)
            o_ref[:, 0, h] = value.astype(bf16)
            for j in range(per):
                head = h * per + j
                h_ref[head // share, 0, :, pl.ds(head % share * size, size)] = value[:, j].astype(
                    bf16
                )

    return pl.pallas_call(
        kernel,
        grid_spec=pltpu.PrefetchScalarGridSpec(
            num_scalar_prefetch=1,
            grid=(seqs, splits),
            in_specs=[
                pl.BlockSpec((steps, 1, mine, per, size), lambda s, i, n: (0, s, i, 0, 0)),
                pl.BlockSpec((2, 1, mine, slots, size), lambda s, i, n: (0, s, i, 0, 0)),
                pl.BlockSpec((steps, 2, 1, heads, size), lambda s, i, n: (0, 0, s, 0, 0)),
            ],
            out_specs=[
                pl.BlockSpec((steps, 1, mine, per, size), lambda s, i, n: (0, s, i, 0, 0)),
                pl.BlockSpec(
                    (owners // splits, 1, steps, share * size), lambda s, i, n: (i, s, 0, 0)
                ),
            ],
        ),
        out_shape=[
            jax.ShapeDtypeStruct(queries.shape, bf16),
            jax.ShapeDtypeStruct((owners, seqs, steps, share * size), bf16),
        ],
        compiler_params=params(),
        cost_estimate=cost(4 * rows * heads * slots * size * seqs, 4 * heads * slots * size * seqs),
        name="attention",
    )(cache_len, queries, *in_hbm(kv_cache), new_kv)


def swap_cores(value):
    count = lax.axis_size("wide")
    return lax.ppermute(value, "wide", [(i, i ^ 1) for i in range(count)])


def exchange(value):
    return lax.all_to_all(value, "wide", split_axis=0, concat_axis=0, tiled=True)


def exchange_chips(value):
    count = lax.axis_size("wide")
    groups = [list(range(core, count, 2)) for core in range(2)]
    return lax.all_to_all(
        value, "wide", split_axis=0, concat_axis=0, tiled=True, axis_index_groups=groups
    )


def exchange_halves(kept, got, send, beside):
    count = lax.axis_size("wide")
    bit = 2
    while True:
        half = kept.shape[0] // 2
        received = lax.ppermute(send, "wide", [(i, i ^ bit) for i in range(count)])
        if bit == 2:
            received, beside = lax.optimization_barrier((received, beside))
        total = kept[:half].astype(f32) + received.astype(f32)
        if got is not None:
            total = total + got[:half].astype(f32)
        got = None
        bit *= 2
        if bit == count:
            return total[0], beside
        kept = total.astype(bf16)
        send = kept[half // 2 :]


def on_device(
    residual_in,
    norm_gain,
    gate_weight,
    up_weight,
    down_weight,
    out_weight,
    queries,
    kv_cache,
    new_kv,
    cache_len,
):
    owners = lax.axis_size("wide")
    groups = lax.axis_size("grp")
    me = lax.axis_index("wide")
    steps, seqs, width_dev = residual_in.shape
    seq_dev = seqs // owners
    tokens = steps * seqs
    mine = steps * seq_dev
    width = width_dev * owners
    chips = owners // 2
    hidden_units = gate_weight.shape[1]

    parts = groups if hidden_units % (groups * owners * 2 * BLOCK) == 0 else 1
    units = hidden_units // parts
    per_owner = units // (owners * BLOCK)
    runs = (per_owner - max(1, per_owner // 4), max(1, per_owner // 4))
    part = lax.axis_index("grp") if parts > 1 else jnp.zeros((), jnp.int32)
    place = jnp.stack([me % 2, part, me // 2, me]).astype(jnp.int32)

    attn_out, heads = attention(cache_len, queries, kv_cache, new_kv, owners)
    heads = exchange(heads)

    out_levels, out_scale = out_levels_of(out_weight, pick_tile(out_weight.shape[1], 2560))
    heads, out_levels, out_scale = lax.optimization_barrier((heads, out_levels, out_scale))
    heads = heads.reshape(tokens, -1)
    projected = exchange(out_product(heads, out_levels, out_scale, owners))

    down = down_weight.T
    rows = gate_weight.shape[0]
    chunk = math.gcd(rows, BLOCK)
    tile = pick_tile(units, 2048)
    paired = pair_shares_blocks(rows) and down.shape[0] == rows
    weights = [gate_weight, up_weight]
    if paired:
        tops = edge_max(place, [*weights, down], units, chunk, pick_tile(units, 4096))
        tops = swap_cores(tops)
    else:
        tops = joined_max(place, weights, units, chunk, tile)
    away = rounded_weights(
        place, weights, tops, paired, 0, 1, units, chunk, pick_tile(units // 2, 2048)
    )
    gain = lax.dynamic_slice_in_dim(norm_gain, me * width_dev, width_dev, 0).astype(f32)[None]
    residual = jnp.transpose(residual_in, (1, 0, 2)).reshape(tokens, width_dev).astype(f32)
    projected, away, gain, residual = lax.optimization_barrier(
        (projected, away, gain, residual)
    )
    hidden = (residual + jnp.sum(projected.astype(f32), axis=0)).astype(bf16)

    states = [hidden]
    if parts == 2:
        states.append(lax.ppermute(hidden, "grp", [(0, 1), (1, 0)]))
    elif parts > 1:
        states = [lax.all_gather(hidden, "grp", axis=0, tiled=True)]

    def product(weights, tops):
        return gate_up_product(place, states, gain, *weights, tops, runs, chips, paired, units)

    got = [swap_cores(value) for value in product(away, None)]
    kept = list(product(weights, tops))
    half = chips // 2
    send = (kept[0][half:].astype(f32) + got[0][half:].astype(f32)).astype(bf16)
    send, kept[1], got[1] = lax.optimization_barrier((send, kept[1], got[1]))
    second = (kept[1].astype(f32) + got[1].astype(f32)).astype(bf16)
    second, place = lax.optimization_barrier((second, place))

    down_chunk = math.gcd(down.shape[0], BLOCK)
    row = 2
    if not paired:
        tops, row = joined_max(place, [down], units, down_chunk, pick_tile(units, 4096)), 0
    home, away = [
        rounded_weights(
            place, [down], tops, paired, row, flip, units, down_chunk, pick_tile(units // 2, 4096)
        )[0]
        for flip in range(2)
    ]
    last = exchange_chips(second)
    first, (home, away) = exchange_halves(kept[0], got[0], send, (home, away))

    last = jnp.sum(last.astype(f32), axis=0)
    squares = jnp.sum(last[:, 2 * runs[1] * BLOCK :], axis=1, keepdims=True)
    scale = lax.rsqrt(squares / width + EPS_NORM)

    def act_of(summed, run):
        size = run * BLOCK
        gate = summed[:, :size] * scale
        up = summed[:, size : 2 * size] * scale
        return (jax.nn.silu(gate) * up).astype(bf16)

    act = jnp.concatenate([act_of(first, runs[0]), act_of(last, runs[1])], axis=1)
    act = exchange_chips(jnp.broadcast_to(act[None], (chips,) + act.shape))
    other = swap_cores(act)
    ffn = down_product(place, act, home, None, states, mine)
    both = down_product(place, other, away, ffn, states, mine)

    axes = ("grp", "wide") if parts > 1 else "wide"
    both = lax.all_to_all(both, axes, split_axis=0, concat_axis=0, tiled=True)
    both = both.reshape(parts, owners, 2, seq_dev, steps, width_dev)
    ffn = both[0, :, 0]
    if parts > 1:
        ffn = jnp.sum(both[:, :, 0].astype(f32), axis=0).astype(bf16)
    ffn_out = jnp.transpose(ffn, (2, 1, 0, 3)).reshape(steps, seq_dev, width)
    hidden_out = jnp.transpose(both[0, :, 1], (2, 1, 0, 3)).reshape(steps, seq_dev, width)
    return (ffn_out, attn_out, hidden_out)


def solution(mesh):
    placed = (
        P("grp", None, "wide"),
        P(),
        P("wide", None),
        P("wide", None),
        P(None, "wide"),
        P("wide", None),
        P("grp", "wide", None, None, None),
        P(None, ("grp", "wide"), None, None, None),
        P("grp", None, "wide", None, None),
        P("grp"),
    )
    return jax.shard_map(
        on_device,
        mesh=mesh,
        in_specs=placed,
        out_specs=(
            P("grp", "wide", None),
            P("grp", "wide", None, None, None),
            P("grp", "wide", None),
        ),
        check_vma=False,
    )
```

```python
import functools
import math

import jax
import jax.numpy as jnp
from jax import lax
from jax.experimental import pallas as pl
from jax.experimental.pallas import tpu as pltpu
from jax.sharding import PartitionSpec as P

BLOCK = 128
QMAX = 448.0
EPS_NORM = 1e-06
EPS_SCALE = 1e-06
NEG = -1e30
LANES = 128
VMEM = 56 * 2**20

f32 = jnp.float32
bf16 = jnp.bfloat16
f8 = jnp.float8_e4m3fn


def params(limit=VMEM):
    return pltpu.CompilerParams(vmem_limit_bytes=limit)


def in_hbm(*arrays):
    return [pltpu.with_memory_space_constraint(x, pltpu.HBM) for x in arrays]


def in_vmem(*arrays):
    return [pltpu.with_memory_space_constraint(x, pltpu.VMEM) for x in arrays]


def cost(flops, read):
    return pl.CostEstimate(flops=int(flops), bytes_accessed=int(read), transcendentals=0)


def pick_tile(cols, most):
    tile = most
    while cols % tile:
        tile -= LANES
    return tile


def spread_lanes(tops):
    out = []
    for g in range(tops.shape[1] // LANES):
        top = jnp.max(tops[:, g * LANES : (g + 1) * LANES], axis=1, keepdims=True)
        out.append(jnp.broadcast_to(top, (tops.shape[0], LANES)))
    return jnp.concatenate(out, axis=1)


def rows_max(ref, start, size):
    return jnp.max(jnp.abs(ref[pl.ds(start, size), :]), axis=0, keepdims=True).astype(f32)


def fill_rows(rows):
    return jnp.concatenate(rows + [rows[0]] * (8 - len(rows)), axis=0)


def chunk_max(place, weights, cols, chunk, tile):
    rows = weights[0].shape[0]
    parts = rows // chunk
    count = len(weights)
    steps = cols // tile

    def kernel(place_ref, *refs):
        for a in range(count):
            tops = [rows_max(refs[a], j * chunk, chunk) for j in range(parts)]
            refs[count][a] = spread_lanes(fill_rows(tops))

    return pl.pallas_call(
        kernel,
        grid_spec=pltpu.PrefetchScalarGridSpec(
            num_scalar_prefetch=1,
            grid=(steps,),
            in_specs=[pl.BlockSpec((rows, tile), lambda i, p: (0, p[1] * steps + i))] * count,
            out_specs=pl.BlockSpec((count, 8, tile), lambda i, p: (0, 0, i)),
        ),
        out_shape=jax.ShapeDtypeStruct((count, 8, cols), f32),
        compiler_params=params(),
        cost_estimate=cost(2 * count * rows * cols, 2 * count * rows * cols),
        name="chunk_max",
    )(place, *in_hbm(*weights))


def edge_max(place, weights, cols, chunk, tile):
    parts = weights[0].shape[0] // chunk
    count = len(weights)
    steps = cols // tile

    def kernel(place_ref, *refs):
        refs[count][...] = spread_lanes(
            fill_rows([rows_max(refs[a], 0, chunk) for a in range(count)])
        )

    return pl.pallas_call(
        kernel,
        grid_spec=pltpu.PrefetchScalarGridSpec(
            num_scalar_prefetch=1,
            grid=(steps,),
            in_specs=[
                pl.BlockSpec(
                    (chunk, tile), lambda i, p: ((1 - p[0]) * (parts - 1), p[1] * steps + i)
                )
            ]
            * count,
            out_specs=pl.BlockSpec((8, tile), lambda i, p: (0, i)),
        ),
        out_shape=jax.ShapeDtypeStruct((8, cols), f32),
        compiler_params=params(),
        cost_estimate=cost(2 * count * chunk * cols, 2 * count * chunk * cols),
        name="edge_max",
    )(place, *in_hbm(*weights))


def join_pair(w_ref, other, odd, chunk, parts):
    mine = [rows_max(w_ref, j * chunk, chunk) for j in range(parts)]
    joined = []
    for j in range(parts):
        even = mine[j ^ 1] if j ^ 1 < parts else other
        back = j - 1 if j % 2 == 0 else j + 1
        near = other if back < 0 else mine[back]
        joined.append(jnp.maximum(mine[j], jnp.where(odd, near, even)))
    return fill_rows(joined)


def block_scales(w_ref, top_ref, place_ref, a, paired, chunk, parts):
    if paired:
        other = top_ref[pl.ds(a, 1), :]
        tops = spread_lanes(join_pair(w_ref, other, place_ref[0] == 1, chunk, parts))
    else:
        tops = top_ref[a]
    largest = tops + EPS_SCALE
    return QMAX / largest, largest * (1.0 / QMAX)


def rounded_chunk(w_ref, j, chunk, factor, scale):
    value = w_ref[pl.ds(j * chunk, chunk), :].astype(f32) * factor[j : j + 1]
    return (value.astype(f8).astype(f32) * scale[j : j + 1]).astype(bf16)


def top_spec_of(tops, paired, tile, at):
    if paired:
        return pl.BlockSpec((tops.shape[0], tile), lambda i, p: (0, at(i, p)))
    return pl.BlockSpec((tops.shape[0], 8, tile), lambda i, p: (0, 0, at(i, p)))


def rounded_weights(place, weights, tops, paired, first, flip, cols, chunk, tile):
    rows = weights[0].shape[0]
    parts = rows // chunk
    count = len(weights)
    taken = 1 if flip is None else 2
    steps = cols // (taken * tile)

    def columns(i, p):
        return i if flip is None else (p[0] ^ flip) * steps + i

    def kernel(place_ref, *refs):
        for a in range(count):
            factor, scale = block_scales(
                refs[a], refs[count], place_ref, first + a, paired, chunk, parts
            )
            for j in range(parts):
                refs[count + 1 + a][pl.ds(j * chunk, chunk), :] = rounded_chunk(
                    refs[a], j, chunk, factor, scale
                )

    return pl.pallas_call(
        kernel,
        grid_spec=pltpu.PrefetchScalarGridSpec(
            num_scalar_prefetch=1,
            grid=(steps,),
            in_specs=[
                pl.BlockSpec((rows, tile), lambda i, p: (0, taken * p[1] * steps + columns(i, p)))
            ]
            * count
            + [top_spec_of(tops, paired, tile, columns)],
            out_specs=[pl.BlockSpec((rows, tile), lambda i, p: (0, i))] * count,
        ),
        out_shape=[jax.ShapeDtypeStruct((rows, cols // taken), bf16)] * count,
        compiler_params=params(),
        cost_estimate=cost(
            6 * count * rows * cols // taken, 4 * count * rows * cols // taken
        ),
        name="rounded_weights",
    )(place, *in_hbm(*weights), *in_vmem(tops))


def join_group(parts, size, dim):
    count = lax.axis_size("wide")
    me = lax.axis_index("wide")
    share = parts.shape[dim]
    shape = list(parts.shape)
    shape[dim] = share * size
    out = jnp.zeros(shape, parts.dtype)
    out = lax.dynamic_update_slice_in_dim(out, parts, (me % size) * share, dim)
    for step in range(1, size):
        perm = [(i // size * size + (i + step) % size, i) for i in range(count)]
        got = lax.ppermute(parts, "wide", perm)
        out = lax.dynamic_update_slice_in_dim(out, got, ((me + step) % size) * share, dim)
    return out


def pair_shares_blocks(rows):
    return math.lcm(rows, BLOCK) == 2 * rows and math.gcd(rows, BLOCK) == BLOCK // 2


def joined_max(place, weights, cols, chunk, tile):
    rows = weights[0].shape[0]
    size = math.lcm(rows, BLOCK) // rows
    per = BLOCK // chunk
    parts = rows // chunk
    tops = chunk_max(place, weights, cols, chunk, tile)
    if size == 1:
        return tops
    joined = join_group(tops[:, :parts], size, 1)
    blocks = joined.reshape(joined.shape[0], -1, per, joined.shape[2])
    joined = jnp.broadcast_to(jnp.max(blocks, axis=2, keepdims=True), blocks.shape)
    joined = joined.reshape(joined.shape[0], size * parts, -1)
    own = lax.dynamic_slice_in_dim(joined, (lax.axis_index("wide") % size) * parts, parts, 1)
    return jnp.pad(own, ((0, 0), (0, 8 - parts), (0, 0)))


def out_levels_of(weight, tile):
    rows, cols = weight.shape
    parts = rows // BLOCK

    def kernel(w_ref, o_ref, s_ref):
        tops = spread_lanes(fill_rows([rows_max(w_ref, j * BLOCK, BLOCK) for j in range(parts)]))
        largest = tops + EPS_SCALE
        factor = QMAX / largest
        s_ref[...] = largest * (1.0 / QMAX)
        for j in range(parts):
            at = pl.ds(j * BLOCK, BLOCK)
            o_ref[at, :] = (w_ref[at, :].astype(f32) * factor[j : j + 1]).astype(f8)

    columns = lambda i: (0, i)
    return pl.pallas_call(
        kernel,
        grid=(cols // tile,),
        in_specs=[pl.BlockSpec((rows, tile), columns)],
        out_specs=[pl.BlockSpec((rows, tile), columns), pl.BlockSpec((8, tile), columns)],
        out_shape=[
            jax.ShapeDtypeStruct((rows, cols), f8),
            jax.ShapeDtypeStruct((8, cols), f32),
        ],
        compiler_params=params(),
        cost_estimate=cost(8 * rows * cols, 3 * rows * cols),
        name="out_levels_of",
    )(*in_hbm(weight))


def out_product(left, levels, scale, owners):
    count, rows = left.shape
    cols = levels.shape[1]
    parts = rows // BLOCK
    share = cols // owners
    tile = pick_tile(cols, 4 * math.lcm(share, LANES))
    per = tile // share

    def kernel(x_ref, l_ref, s_ref, o_ref):
        total = None
        for j in range(parts):
            at = pl.ds(j * BLOCK, BLOCK)
            part = jnp.dot(x_ref[:, at], l_ref[at, :].astype(bf16), preferred_element_type=f32)
            part = part * s_ref[pl.ds(j, 1), :]
            total = part if total is None else total + part
        total = total.astype(bf16)
        for q in range(per):
            o_ref[q] = total[:, q * share : (q + 1) * share]

    return pl.pallas_call(
        kernel,
        grid=(cols // tile,),
        in_specs=[
            pl.BlockSpec((count, rows), lambda i: (0, 0)),
            pl.BlockSpec((rows, tile), lambda i: (0, i)),
            pl.BlockSpec((8, tile), lambda i: (0, i)),
        ],
        out_specs=pl.BlockSpec((per, count, share), lambda i: (i, 0, 0)),
        out_shape=jax.ShapeDtypeStruct((owners, count, share), bf16),
        compiler_params=params(),
        cost_estimate=cost(2 * count * rows * cols, rows * cols),
        name="out_product",
    )(left, levels, scale)


def gate_up_product(place, hidden, gain, gate, up, tops, runs, chips, paired, cols):
    groups = len(hidden)
    rows = gate.shape[0]
    count = groups * hidden[0].shape[0]
    chunk = math.gcd(rows, BLOCK)
    parts = rows // chunk
    extra = -(-4 * chips // LANES) * LANES
    units = [run * BLOCK for run in runs]
    widths = (2 * units[0], 2 * units[1] + extra)
    together = 2 if sum(runs) % 2 == 0 else 1
    tile = together * chips * BLOCK

    def kernel(place_ref, *refs):
        h_refs = refs[:groups]
        gain_ref, g_ref, u_ref = refs[groups : groups + 3]
        o_refs, x_ref, p_ref = refs[-4:-2], refs[-2], refs[-1]
        step = pl.program_id(0)

        @pl.when(step == 0)
        def _():
            values = [ref[...].astype(f32) for ref in h_refs]
            if groups == 2:
                first = place_ref[1] == 0
                values = [
                    jnp.where(first, values[0], values[1]),
                    jnp.where(first, values[1], values[0]),
                ]
            states = jnp.concatenate(values, axis=0)
            x_ref[...] = (states * gain_ref[...]).astype(bf16)
            squares = jnp.sum(states * states, axis=1, keepdims=True)
            high = squares.astype(bf16).astype(f32)
            lane = lax.broadcasted_iota(jnp.int32, (count, extra), 1)
            at = 2 * place_ref[3]
            p_ref[...] = jnp.where(
                lane == at, high, jnp.where(lane == at + 1, squares - high, 0.0)
            )

        totals = []
        for a, ref in enumerate((g_ref, u_ref)):
            if tops is None:
                weight = ref[...]
            else:
                factor, scale = block_scales(
                    ref, refs[groups + 3], place_ref, a, paired, chunk, parts
                )
                weight = jnp.concatenate(
                    [rounded_chunk(ref, j, chunk, factor, scale) for j in range(parts)], axis=0
                )
            totals.append(jnp.dot(x_ref[...], weight, preferred_element_type=f32))

        def write(run, block, position, q):
            ref = o_refs[run]
            at = ((runs[0] * run + block) % together * chips + q) * BLOCK
            for a, total in enumerate(totals):
                lanes = pl.ds(a * units[run] + block * BLOCK, BLOCK)
                ref[position, :, lanes] = total[:, at : at + BLOCK].astype(bf16)
            if run == 1 and block == 0:
                ref[position, :, pl.ds(2 * units[1], extra)] = p_ref[...].astype(bf16)

        def write_first(block):
            for q in range(chips):
                position, rest = 0, q ^ place_ref[2]
                for _ in range(chips.bit_length() - 1):
                    position, rest = position * 2 + rest % 2, rest // 2
                write(0, block, position, q)

        def write_second(block):
            for q in range(chips):
                write(1, block, q ^ (place_ref[2] % 2), q)

        for block in range(runs[0]):
            pl.when(step == block // together)(functools.partial(write_first, block))
        for block in range(runs[1]):
            pl.when(step == (runs[0] + block) // together)(
                functools.partial(write_second, block)
            )

    steps = sum(runs) // together
    home = lambda i, p: p[0] * steps + i
    fixed = lambda i, p: (0, 0)
    out_shapes = [(chips, count, width) for width in widths]
    if tops is None:
        weight_spec = pl.BlockSpec((rows, tile), lambda i, p: (0, i))
    else:
        weight_spec = pl.BlockSpec((rows, tile), lambda i, p: (0, 2 * p[1] * steps + home(i, p)))
    in_specs = [pl.BlockSpec(x.shape, fixed) for x in hidden]
    in_specs += [pl.BlockSpec((1, rows), fixed), weight_spec, weight_spec]
    if tops is not None:
        in_specs.append(top_spec_of(tops, paired, tile, home))
    return pl.pallas_call(
        kernel,
        grid_spec=pltpu.PrefetchScalarGridSpec(
            num_scalar_prefetch=1,
            grid=(steps,),
            in_specs=in_specs,
            out_specs=[pl.BlockSpec(shape, lambda i, p: (0, 0, 0)) for shape in out_shapes],
            scratch_shapes=[pltpu.VMEM((count, rows), bf16), pltpu.VMEM((count, extra), f32)],
        ),
        out_shape=[jax.ShapeDtypeStruct(shape, bf16) for shape in out_shapes],
        compiler_params=params(),
        cost_estimate=cost(4 * count * rows * cols // 2, 2 * rows * cols),
        name="gate_up_product",
    )(place, *in_vmem(*hidden), gain, *in_hbm(gate, up), *([] if tops is None else in_vmem(tops)))


def down_product(place, act, weight, added, states, mine):
    chips, count, units = act.shape
    width = weight.shape[0]
    together = 2 if units % (2 * BLOCK) == 0 else 1
    tile = together * chips * BLOCK
    steps = units // (together * BLOCK)
    last = added is not None

    def kernel(place_ref, a_ref, w_ref, *refs):
        step = pl.program_id(0)
        o_ref, total_ref = refs[-2:]
        total = lax.dot_general(
            jnp.concatenate(
                [
                    a_ref[q, :, pl.ds(t * BLOCK, BLOCK)]
                    for t in range(together)
                    for q in range(chips)
                ],
                axis=1,
            ),
            w_ref[...],
            (((1,), (1,)), ((), ())),
            preferred_element_type=f32,
        )

        @pl.when(step == 0)
        def _():
            total_ref[...] = refs[0][...] + total if last else total

        @pl.when(step > 0)
        def _():
            total_ref[...] += total

        @pl.when(step == steps - 1)
        def _():
            if not last:
                o_ref[...] = total_ref[...]
                return
            values = [ref[...].astype(f32) for ref in refs[1 : 1 + len(states)]]
            if len(states) == 2:
                first = place_ref[1] == 0
                values = [
                    jnp.where(first, values[0], values[1]),
                    jnp.where(first, values[1], values[0]),
                ]
            sums, values = total_ref[...], jnp.concatenate(values, axis=0)
            for b in range(count // mine):
                at = slice(b * mine, (b + 1) * mine)
                o_ref[b] = jnp.concatenate([sums[at], values[at]], axis=0).astype(bf16)

    fixed = lambda shape: pl.BlockSpec(shape, lambda i, p: (0,) * len(shape))
    more = [added, *states] if last else []
    shape = (count // mine, 2 * mine, width) if last else (count, width)
    return pl.pallas_call(
        kernel,
        grid_spec=pltpu.PrefetchScalarGridSpec(
            num_scalar_prefetch=1,
            grid=(steps,),
            in_specs=[
                pl.BlockSpec((chips, count, together * BLOCK), lambda i, p: (0, 0, i)),
                pl.BlockSpec((width, tile), lambda i, p: (0, i)),
            ]
            + [fixed(x.shape) for x in more],
            out_specs=fixed(shape),
            scratch_shapes=[pltpu.VMEM((count, width), f32)],
        ),
        out_shape=jax.ShapeDtypeStruct(shape, bf16 if last else f32),
        compiler_params=params(16 * 2**20),
        cost_estimate=cost(2 * count * width * tile * steps, 2 * width * tile * steps),
        name="down_product",
    )(place, act, weight, *more)


def attention(cache_len, queries, kv_cache, new_kv, owners):
    steps, seqs, heads, per, size = queries.shape
    slots = kv_cache.shape[3]
    factor = size ** (-0.5)
    share = heads * per // owners
    splits = 2 if heads % 2 == 0 and owners % 2 == 0 else 1
    mine = heads // splits
    rows = steps * per
    pad = 8 - steps

    def kernel(len_ref, q_ref, kv_ref, new_ref, o_ref, h_ref):
        live = len_ref[lax.axis_index("wide") * seqs + pl.program_id(0)]
        valid = lax.broadcasted_iota(jnp.int32, (rows, slots), 1) < live
        step_of = lax.broadcasted_iota(jnp.int32, (rows, 8), 0) // per
        fresh = lax.broadcasted_iota(jnp.int32, (rows, 8), 1) <= step_of

        def product(left, right, dim):
            return lax.dot_general(
                left, right, (((1,), (dim,)), ((), ())), preferred_element_type=f32
            )

        new = []
        for n in range(2):
            value = new_ref[:, n, 0].astype(f32)
            if splits == 2:
                value = jnp.where(pl.program_id(1) == 0, value[:, :mine], value[:, mine:])
            new.append(value)
        at = range(mine)
        queries_of = [
            q_ref[:, 0, h].astype(f32).reshape(rows, size).astype(bf16) for h in at
        ]
        new_keys, new_values = [
            [
                jnp.concatenate([value[:, h], jnp.zeros((pad, size), f32)], axis=0).astype(bf16)
                for h in at
            ]
            for value in new
        ]
        cached = [product(queries_of[h], kv_ref[0, 0, h], 1) for h in at]
        recent = [product(queries_of[h], new_keys[h], 1) for h in at]
        cached = [jnp.where(valid, value * factor, NEG) for value in cached]
        recent = [jnp.where(fresh, value * factor, NEG) for value in recent]
        top = [
            jnp.maximum(
                jnp.max(cached[h], axis=1, keepdims=True), jnp.max(recent[h], axis=1, keepdims=True)
            )
            for h in at
        ]
        cached = [jnp.exp(cached[h] - top[h]) for h in at]
        recent = [jnp.exp(recent[h] - top[h]) for h in at]
        share_of = [
            1.0
            / (
                jnp.sum(cached[h], axis=1, keepdims=True)
                + jnp.sum(recent[h], axis=1, keepdims=True)
            )
            for h in at
        ]
        cached = [(cached[h] * share_of[h]).astype(bf16) for h in at]
        recent = [(recent[h] * share_of[h]).astype(bf16) for h in at]
        mixed = [
            product(cached[h], kv_ref[1, 0, h], 0) + product(recent[h], new_values[h], 0)
            for h in at
        ]
        for h in at:
            value = mixed[h].reshape(steps, per, size)
            o_ref[:, 0, h] = value.astype(bf16)
            for j in range(per):
                head = h * per + j
                h_ref[head // share, 0, :, pl.ds(head % share * size, size)] = value[:, j].astype(
                    bf16
                )

    return pl.pallas_call(
        kernel,
        grid_spec=pltpu.PrefetchScalarGridSpec(
            num_scalar_prefetch=1,
            grid=(seqs, splits),
            in_specs=[
                pl.BlockSpec((steps, 1, mine, per, size), lambda s, i, n: (0, s, i, 0, 0)),
                pl.BlockSpec((2, 1, mine, slots, size), lambda s, i, n: (0, s, i, 0, 0)),
                pl.BlockSpec((steps, 2, 1, heads, size), lambda s, i, n: (0, 0, s, 0, 0)),
            ],
            out_specs=[
                pl.BlockSpec((steps, 1, mine, per, size), lambda s, i, n: (0, s, i, 0, 0)),
                pl.BlockSpec(
                    (owners // splits, 1, steps, share * size), lambda s, i, n: (i, s, 0, 0)
                ),
            ],
        ),
        out_shape=[
            jax.ShapeDtypeStruct(queries.shape, bf16),
            jax.ShapeDtypeStruct((owners, seqs, steps, share * size), bf16),
        ],
        compiler_params=params(),
        cost_estimate=cost(4 * rows * heads * slots * size * seqs, 4 * heads * slots * size * seqs),
        name="attention",
    )(cache_len, queries, *in_hbm(kv_cache), new_kv)


def swap_cores(value):
    count = lax.axis_size("wide")
    return lax.ppermute(value, "wide", [(i, i ^ 1) for i in range(count)])


def exchange(value):
    return lax.all_to_all(value, "wide", split_axis=0, concat_axis=0, tiled=True)


def exchange_chips(value):
    count = lax.axis_size("wide")
    groups = [list(range(core, count, 2)) for core in range(2)]
    return lax.all_to_all(
        value, "wide", split_axis=0, concat_axis=0, tiled=True, axis_index_groups=groups
    )


def exchange_halves(kept, got, send, beside):
    count = lax.axis_size("wide")
    bit = 2
    while True:
        half = kept.shape[0] // 2
        received = lax.ppermute(send, "wide", [(i, i ^ bit) for i in range(count)])
        if bit == 2:
            received, beside = lax.optimization_barrier((received, beside))
        total = kept[:half].astype(f32) + received.astype(f32)
        if got is not None:
            total = total + got[:half].astype(f32)
        got = None
        bit *= 2
        if bit == count:
            return total[0], beside
        kept = total.astype(bf16)
        send = kept[half // 2 :]


def exchange_pairs(value):
    count = lax.axis_size("wide")
    groups = [[rest + 4 * k for k in range(count // 4)] for rest in range(4)]
    value = value.reshape(count // 4, 2, *value.shape[1:])
    value = lax.all_to_all(
        value, "wide", split_axis=0, concat_axis=0, tiled=True, axis_index_groups=groups
    )
    value = jnp.sum(value.astype(f32), axis=0)
    received = lax.ppermute(value[1].astype(bf16), "wide", [(i, i ^ 2) for i in range(count)])
    return value[0] + received.astype(f32)


def on_device(
    residual_in,
    norm_gain,
    gate_weight,
    up_weight,
    down_weight,
    out_weight,
    queries,
    kv_cache,
    new_kv,
    cache_len,
):
    owners = lax.axis_size("wide")
    groups = lax.axis_size("grp")
    me = lax.axis_index("wide")
    steps, seqs, width_dev = residual_in.shape
    seq_dev = seqs // owners
    tokens = steps * seqs
    mine = steps * seq_dev
    width = width_dev * owners
    chips = owners // 2
    hidden_units = gate_weight.shape[1]

    parts = groups if hidden_units % (groups * owners * 2 * BLOCK) == 0 else 1
    units = hidden_units // parts
    per_owner = units // (owners * BLOCK)
    runs = (per_owner - max(1, per_owner // 4), max(1, per_owner // 4))
    part = lax.axis_index("grp") if parts > 1 else jnp.zeros((), jnp.int32)
    place = jnp.stack([me % 2, part, me // 2, me]).astype(jnp.int32)

    attn_out, heads = attention(cache_len, queries, kv_cache, new_kv, owners)
    heads = exchange(heads)

    out_levels, out_scale = out_levels_of(out_weight, pick_tile(out_weight.shape[1], 2560))
    heads, out_levels, out_scale = lax.optimization_barrier((heads, out_levels, out_scale))
    heads = heads.reshape(tokens, -1)
    projected = exchange(out_product(heads, out_levels, out_scale, owners))

    down = down_weight.T
    rows = gate_weight.shape[0]
    chunk = math.gcd(rows, BLOCK)
    tile = pick_tile(units, 2048)
    paired = pair_shares_blocks(rows) and down.shape[0] == rows
    weights = [gate_weight, up_weight]
    if paired:
        tops = edge_max(place, [*weights, down], units, chunk, pick_tile(units, 4096))
        tops = swap_cores(tops)
    else:
        tops = joined_max(place, weights, units, chunk, tile)
    away = rounded_weights(
        place, weights, tops, paired, 0, 1, units, chunk, pick_tile(units // 2, 2048)
    )
    gain = lax.dynamic_slice_in_dim(norm_gain, me * width_dev, width_dev, 0).astype(f32)[None]
    residual = jnp.transpose(residual_in, (1, 0, 2)).reshape(tokens, width_dev).astype(f32)
    projected, away, gain, residual = lax.optimization_barrier(
        (projected, away, gain, residual)
    )
    hidden = (residual + jnp.sum(projected.astype(f32), axis=0)).astype(bf16)

    states = [hidden]
    if parts == 2:
        states.append(lax.ppermute(hidden, "grp", [(0, 1), (1, 0)]))
    elif parts > 1:
        states = [lax.all_gather(hidden, "grp", axis=0, tiled=True)]

    def product(weights, tops):
        return gate_up_product(place, states, gain, *weights, tops, runs, chips, paired, units)

    got = [swap_cores(value) for value in product(away, None)]
    kept = list(product(weights, tops))
    half = chips // 2
    send = (kept[0][half:].astype(f32) + got[0][half:].astype(f32)).astype(bf16)
    send, kept[1], got[1] = lax.optimization_barrier((send, kept[1], got[1]))
    second = (kept[1].astype(f32) + got[1].astype(f32)).astype(bf16)
    second, place = lax.optimization_barrier((second, place))

    down_chunk = math.gcd(down.shape[0], BLOCK)
    row = 2
    if not paired:
        tops, row = joined_max(place, [down], units, down_chunk, pick_tile(units, 4096)), 0
    home, away = [
        rounded_weights(
            place, [down], tops, paired, row, flip, units, down_chunk, pick_tile(units // 2, 4096)
        )[0]
        for flip in range(2)
    ]
    last = exchange_pairs(second)
    first, (home, away) = exchange_halves(kept[0], got[0], send, (home, away))

    squares = jnp.sum(last[:, 2 * runs[1] * BLOCK :], axis=1, keepdims=True)
    scale = lax.rsqrt(squares / width + EPS_NORM)

    def act_of(summed, run):
        size = run * BLOCK
        gate = summed[:, :size] * scale
        up = summed[:, size : 2 * size] * scale
        return (jax.nn.silu(gate) * up).astype(bf16)

    act = jnp.concatenate([act_of(first, runs[0]), act_of(last, runs[1])], axis=1)
    act = exchange_chips(jnp.broadcast_to(act[None], (chips,) + act.shape))
    other = swap_cores(act)
    ffn = down_product(place, act, home, None, states, mine)
    both = down_product(place, other, away, ffn, states, mine)

    axes = ("grp", "wide") if parts > 1 else "wide"
    both = lax.all_to_all(both, axes, split_axis=0, concat_axis=0, tiled=True)
    both = both.reshape(parts, owners, 2, seq_dev, steps, width_dev)
    ffn = both[0, :, 0]
    if parts > 1:
        ffn = jnp.sum(both[:, :, 0].astype(f32), axis=0).astype(bf16)
    ffn_out = jnp.transpose(ffn, (2, 1, 0, 3)).reshape(steps, seq_dev, width)
    hidden_out = jnp.transpose(both[0, :, 1], (2, 1, 0, 3)).reshape(steps, seq_dev, width)
    return (ffn_out, attn_out, hidden_out)


def solution(mesh):
    placed = (
        P("grp", None, "wide"),
        P(),
        P("wide", None),
        P("wide", None),
        P(None, "wide"),
        P("wide", None),
        P("grp", "wide", None, None, None),
        P(None, ("grp", "wide"), None, None, None),
        P("grp", None, "wide", None, None),
        P("grp"),
    )
    return jax.shard_map(
        on_device,
        mesh=mesh,
        in_specs=placed,
        out_specs=(
            P("grp", "wide", None),
            P("grp", "wide", None, None, None),
            P("grp", "wide", None),
        ),
        check_vma=False,
    )
```

```python
import functools
import math

import jax
import jax.numpy as jnp
from jax import lax
from jax.experimental import pallas as pl
from jax.experimental.pallas import tpu as pltpu
from jax.sharding import PartitionSpec as P

BLOCK = 128
QMAX = 448.0
EPS_NORM = 1e-06
EPS_SCALE = 1e-06
NEG = -1e30
LANES = 128
VMEM = 56 * 2**20

f32 = jnp.float32
bf16 = jnp.bfloat16
f8 = jnp.float8_e4m3fn


def params(limit=VMEM):
    return pltpu.CompilerParams(vmem_limit_bytes=limit)


def in_hbm(*arrays):
    return [pltpu.with_memory_space_constraint(x, pltpu.HBM) for x in arrays]


def in_vmem(*arrays):
    return [pltpu.with_memory_space_constraint(x, pltpu.VMEM) for x in arrays]


def cost(flops, read):
    return pl.CostEstimate(flops=int(flops), bytes_accessed=int(read), transcendentals=0)


def pick_tile(cols, most):
    tile = most
    while cols % tile:
        tile -= LANES
    return tile


def spread_lanes(tops):
    out = []
    for g in range(tops.shape[1] // LANES):
        top = jnp.max(tops[:, g * LANES : (g + 1) * LANES], axis=1, keepdims=True)
        out.append(jnp.broadcast_to(top, (tops.shape[0], LANES)))
    return jnp.concatenate(out, axis=1)


def rows_max(ref, start, size):
    return jnp.max(jnp.abs(ref[pl.ds(start, size), :]), axis=0, keepdims=True).astype(f32)


def fill_rows(rows):
    return jnp.concatenate(rows + [rows[0]] * (8 - len(rows)), axis=0)


def chunk_max(place, weights, cols, chunk, tile):
    rows = weights[0].shape[0]
    parts = rows // chunk
    count = len(weights)
    steps = cols // tile

    def kernel(place_ref, *refs):
        for a in range(count):
            tops = [rows_max(refs[a], j * chunk, chunk) for j in range(parts)]
            refs[count][a] = spread_lanes(fill_rows(tops))

    return pl.pallas_call(
        kernel,
        grid_spec=pltpu.PrefetchScalarGridSpec(
            num_scalar_prefetch=1,
            grid=(steps,),
            in_specs=[pl.BlockSpec((rows, tile), lambda i, p: (0, p[1] * steps + i))] * count,
            out_specs=pl.BlockSpec((count, 8, tile), lambda i, p: (0, 0, i)),
        ),
        out_shape=jax.ShapeDtypeStruct((count, 8, cols), f32),
        compiler_params=params(),
        cost_estimate=cost(2 * count * rows * cols, 2 * count * rows * cols),
        name="chunk_max",
    )(place, *in_hbm(*weights))


def edge_max(place, weights, cols, chunk, tile):
    parts = weights[0].shape[0] // chunk
    count = len(weights)
    steps = cols // tile

    def kernel(place_ref, *refs):
        refs[count][...] = spread_lanes(
            fill_rows([rows_max(refs[a], 0, chunk) for a in range(count)])
        )

    return pl.pallas_call(
        kernel,
        grid_spec=pltpu.PrefetchScalarGridSpec(
            num_scalar_prefetch=1,
            grid=(steps,),
            in_specs=[
                pl.BlockSpec(
                    (chunk, tile), lambda i, p: ((1 - p[0]) * (parts - 1), p[1] * steps + i)
                )
            ]
            * count,
            out_specs=pl.BlockSpec((8, tile), lambda i, p: (0, i)),
        ),
        out_shape=jax.ShapeDtypeStruct((8, cols), f32),
        compiler_params=params(),
        cost_estimate=cost(2 * count * chunk * cols, 2 * count * chunk * cols),
        name="edge_max",
    )(place, *in_hbm(*weights))


def join_pair(w_ref, other, odd, chunk, parts):
    mine = [rows_max(w_ref, j * chunk, chunk) for j in range(parts)]
    joined = []
    for j in range(parts):
        even = mine[j ^ 1] if j ^ 1 < parts else other
        back = j - 1 if j % 2 == 0 else j + 1
        near = other if back < 0 else mine[back]
        joined.append(jnp.maximum(mine[j], jnp.where(odd, near, even)))
    return fill_rows(joined)


def block_scales(w_ref, top_ref, place_ref, a, paired, chunk, parts):
    if paired:
        other = top_ref[pl.ds(a, 1), :]
        tops = spread_lanes(join_pair(w_ref, other, place_ref[0] == 1, chunk, parts))
    else:
        tops = top_ref[a]
    largest = tops + EPS_SCALE
    return QMAX / largest, largest * (1.0 / QMAX)


def rounded_chunk(w_ref, j, chunk, factor, scale):
    value = w_ref[pl.ds(j * chunk, chunk), :].astype(f32) * factor[j : j + 1]
    return (value.astype(f8).astype(f32) * scale[j : j + 1]).astype(bf16)


def top_spec_of(tops, paired, tile, at):
    if paired:
        return pl.BlockSpec((tops.shape[0], tile), lambda i, p: (0, at(i, p)))
    return pl.BlockSpec((tops.shape[0], 8, tile), lambda i, p: (0, 0, at(i, p)))


def rounded_weights(place, weights, tops, paired, first, flip, cols, chunk, tile):
    rows = weights[0].shape[0]
    parts = rows // chunk
    count = len(weights)
    taken = 1 if flip is None else 2
    steps = cols // (taken * tile)

    def columns(i, p):
        return i if flip is None else (p[0] ^ flip) * steps + i

    def kernel(place_ref, *refs):
        for a in range(count):
            factor, scale = block_scales(
                refs[a], refs[count], place_ref, first + a, paired, chunk, parts
            )
            for j in range(parts):
                refs[count + 1 + a][pl.ds(j * chunk, chunk), :] = rounded_chunk(
                    refs[a], j, chunk, factor, scale
                )

    return pl.pallas_call(
        kernel,
        grid_spec=pltpu.PrefetchScalarGridSpec(
            num_scalar_prefetch=1,
            grid=(steps,),
            in_specs=[
                pl.BlockSpec((rows, tile), lambda i, p: (0, taken * p[1] * steps + columns(i, p)))
            ]
            * count
            + [top_spec_of(tops, paired, tile, columns)],
            out_specs=[pl.BlockSpec((rows, tile), lambda i, p: (0, i))] * count,
        ),
        out_shape=[jax.ShapeDtypeStruct((rows, cols // taken), bf16)] * count,
        compiler_params=params(),
        cost_estimate=cost(
            6 * count * rows * cols // taken, 4 * count * rows * cols // taken
        ),
        name="rounded_weights",
    )(place, *in_hbm(*weights), *in_vmem(tops))


def join_group(parts, size, dim):
    count = lax.axis_size("wide")
    me = lax.axis_index("wide")
    share = parts.shape[dim]
    shape = list(parts.shape)
    shape[dim] = share * size
    out = jnp.zeros(shape, parts.dtype)
    out = lax.dynamic_update_slice_in_dim(out, parts, (me % size) * share, dim)
    for step in range(1, size):
        perm = [(i // size * size + (i + step) % size, i) for i in range(count)]
        got = lax.ppermute(parts, "wide", perm)
        out = lax.dynamic_update_slice_in_dim(out, got, ((me + step) % size) * share, dim)
    return out


def pair_shares_blocks(rows):
    return math.lcm(rows, BLOCK) == 2 * rows and math.gcd(rows, BLOCK) == BLOCK // 2


def joined_max(place, weights, cols, chunk, tile):
    rows = weights[0].shape[0]
    size = math.lcm(rows, BLOCK) // rows
    per = BLOCK // chunk
    parts = rows // chunk
    tops = chunk_max(place, weights, cols, chunk, tile)
    if size == 1:
        return tops
    joined = join_group(tops[:, :parts], size, 1)
    blocks = joined.reshape(joined.shape[0], -1, per, joined.shape[2])
    joined = jnp.broadcast_to(jnp.max(blocks, axis=2, keepdims=True), blocks.shape)
    joined = joined.reshape(joined.shape[0], size * parts, -1)
    own = lax.dynamic_slice_in_dim(joined, (lax.axis_index("wide") % size) * parts, parts, 1)
    return jnp.pad(own, ((0, 0), (0, 8 - parts), (0, 0)))


def out_levels_of(weight, tile):
    rows, cols = weight.shape
    parts = rows // BLOCK

    def kernel(w_ref, o_ref, s_ref):
        tops = spread_lanes(fill_rows([rows_max(w_ref, j * BLOCK, BLOCK) for j in range(parts)]))
        largest = tops + EPS_SCALE
        factor = QMAX / largest
        s_ref[...] = largest * (1.0 / QMAX)
        for j in range(parts):
            at = pl.ds(j * BLOCK, BLOCK)
            o_ref[at, :] = (w_ref[at, :].astype(f32) * factor[j : j + 1]).astype(f8)

    columns = lambda i: (0, i)
    return pl.pallas_call(
        kernel,
        grid=(cols // tile,),
        in_specs=[pl.BlockSpec((rows, tile), columns)],
        out_specs=[pl.BlockSpec((rows, tile), columns), pl.BlockSpec((8, tile), columns)],
        out_shape=[
            jax.ShapeDtypeStruct((rows, cols), f8),
            jax.ShapeDtypeStruct((8, cols), f32),
        ],
        compiler_params=params(),
        cost_estimate=cost(8 * rows * cols, 3 * rows * cols),
        name="out_levels_of",
    )(*in_hbm(weight))


def out_product(left, levels, scale, owners):
    count, rows = left.shape
    cols = levels.shape[1]
    parts = rows // BLOCK
    share = cols // owners
    tile = pick_tile(cols, 4 * math.lcm(share, LANES))
    per = tile // share

    def kernel(x_ref, l_ref, s_ref, o_ref):
        total = None
        for j in range(parts):
            at = pl.ds(j * BLOCK, BLOCK)
            part = jnp.dot(x_ref[:, at], l_ref[at, :].astype(bf16), preferred_element_type=f32)
            part = part * s_ref[pl.ds(j, 1), :]
            total = part if total is None else total + part
        total = total.astype(bf16)
        for q in range(per):
            o_ref[q] = total[:, q * share : (q + 1) * share]

    return pl.pallas_call(
        kernel,
        grid=(cols // tile,),
        in_specs=[
            pl.BlockSpec((count, rows), lambda i: (0, 0)),
            pl.BlockSpec((rows, tile), lambda i: (0, i)),
            pl.BlockSpec((8, tile), lambda i: (0, i)),
        ],
        out_specs=pl.BlockSpec((per, count, share), lambda i: (i, 0, 0)),
        out_shape=jax.ShapeDtypeStruct((owners, count, share), bf16),
        compiler_params=params(),
        cost_estimate=cost(2 * count * rows * cols, rows * cols),
        name="out_product",
    )(left, levels, scale)


def gate_up_product(place, hidden, gain, gate, up, tops, runs, chips, paired, cols):
    groups = len(hidden)
    rows = gate.shape[0]
    count = groups * hidden[0].shape[0]
    chunk = math.gcd(rows, BLOCK)
    parts = rows // chunk
    extra = -(-4 * chips // LANES) * LANES
    units = [run * BLOCK for run in runs]
    widths = (2 * units[0], 2 * units[1] + extra)
    together = 2 if sum(runs) % 2 == 0 else 1
    tile = together * chips * BLOCK

    def kernel(place_ref, *refs):
        h_refs = refs[:groups]
        gain_ref, g_ref, u_ref = refs[groups : groups + 3]
        o_refs, x_ref, p_ref = refs[-4:-2], refs[-2], refs[-1]
        step = pl.program_id(0)

        @pl.when(step == 0)
        def _():
            values = [ref[...].astype(f32) for ref in h_refs]
            if groups == 2:
                first = place_ref[1] == 0
                values = [
                    jnp.where(first, values[0], values[1]),
                    jnp.where(first, values[1], values[0]),
                ]
            states = jnp.concatenate(values, axis=0)
            x_ref[...] = (states * gain_ref[...]).astype(bf16)
            squares = jnp.sum(states * states, axis=1, keepdims=True)
            high = squares.astype(bf16).astype(f32)
            lane = lax.broadcasted_iota(jnp.int32, (count, extra), 1)
            at = 2 * place_ref[3]
            p_ref[...] = jnp.where(
                lane == at, high, jnp.where(lane == at + 1, squares - high, 0.0)
            )

        totals = []
        for a, ref in enumerate((g_ref, u_ref)):
            if tops is None:
                weight = ref[...]
            else:
                factor, scale = block_scales(
                    ref, refs[groups + 3], place_ref, a, paired, chunk, parts
                )
                weight = jnp.concatenate(
                    [rounded_chunk(ref, j, chunk, factor, scale) for j in range(parts)], axis=0
                )
            totals.append(jnp.dot(x_ref[...], weight, preferred_element_type=f32))

        def write(run, block, position, q):
            ref = o_refs[run]
            at = ((runs[0] * run + block) % together * chips + q) * BLOCK
            for a, total in enumerate(totals):
                lanes = pl.ds(a * units[run] + block * BLOCK, BLOCK)
                ref[position, :, lanes] = total[:, at : at + BLOCK].astype(bf16)
            if run == 1 and block == 0:
                ref[position, :, pl.ds(2 * units[1], extra)] = p_ref[...].astype(bf16)

        def write_first(block):
            for q in range(chips):
                position, rest = 0, q ^ place_ref[2]
                for _ in range(chips.bit_length() - 1):
                    position, rest = position * 2 + rest % 2, rest // 2
                write(0, block, position, q)

        def write_second(block):
            for q in range(chips):
                write(1, block, q ^ (place_ref[2] % 2), q)

        for block in range(runs[0]):
            pl.when(step == block // together)(functools.partial(write_first, block))
        for block in range(runs[1]):
            pl.when(step == (runs[0] + block) // together)(
                functools.partial(write_second, block)
            )

    steps = sum(runs) // together
    home = lambda i, p: p[0] * steps + i
    fixed = lambda i, p: (0, 0)
    out_shapes = [(chips, count, width) for width in widths]
    if tops is None:
        weight_spec = pl.BlockSpec((rows, tile), lambda i, p: (0, i))
    else:
        weight_spec = pl.BlockSpec((rows, tile), lambda i, p: (0, 2 * p[1] * steps + home(i, p)))
    in_specs = [pl.BlockSpec(x.shape, fixed) for x in hidden]
    in_specs += [pl.BlockSpec((1, rows), fixed), weight_spec, weight_spec]
    if tops is not None:
        in_specs.append(top_spec_of(tops, paired, tile, home))
    return pl.pallas_call(
        kernel,
        grid_spec=pltpu.PrefetchScalarGridSpec(
            num_scalar_prefetch=1,
            grid=(steps,),
            in_specs=in_specs,
            out_specs=[pl.BlockSpec(shape, lambda i, p: (0, 0, 0)) for shape in out_shapes],
            scratch_shapes=[pltpu.VMEM((count, rows), bf16), pltpu.VMEM((count, extra), f32)],
        ),
        out_shape=[jax.ShapeDtypeStruct(shape, bf16) for shape in out_shapes],
        compiler_params=params(),
        cost_estimate=cost(4 * count * rows * cols // 2, 2 * rows * cols),
        name="gate_up_product",
    )(place, *in_vmem(*hidden), gain, *in_hbm(gate, up), *([] if tops is None else in_vmem(tops)))


def packed(width):
    return (2 * (width // LANES) + 1, LANES) if width % LANES == LANES // 2 else (2, width)


def pack(pair):
    width = pair[0].shape[1]
    if packed(width)[1] == width:
        return pair
    whole = width // LANES * LANES
    pieces = [x[:, at : at + LANES] for x in pair for at in range(0, whole, LANES)]
    return [*pieces, jnp.concatenate([x[:, whole:] for x in pair], axis=1)]


def unpack(pieces, width):
    if packed(width)[1] == width:
        return pieces
    each, rest = width // LANES, width % LANES
    last = pieces[-1]
    return [
        jnp.concatenate(
            [*pieces[n * each : (n + 1) * each], last[..., n * rest : (n + 1) * rest]], axis=-1
        )
        for n in range(2)
    ]


def down_product(place, act, weight, added, states, mine):
    chips, count, units = act.shape
    width = weight.shape[0]
    together = 2 if units % (2 * BLOCK) == 0 else 1
    tile = together * chips * BLOCK
    steps = units // (together * BLOCK)
    last = added is not None

    def kernel(place_ref, a_ref, w_ref, *refs):
        step = pl.program_id(0)
        o_ref, total_ref = refs[-2:]
        total = lax.dot_general(
            jnp.concatenate(
                [
                    a_ref[q, :, pl.ds(t * BLOCK, BLOCK)]
                    for t in range(together)
                    for q in range(chips)
                ],
                axis=1,
            ),
            w_ref[...],
            (((1,), (1,)), ((), ())),
            preferred_element_type=f32,
        )

        @pl.when(step == 0)
        def _():
            total_ref[...] = refs[0][...] + total if last else total

        @pl.when(step > 0)
        def _():
            total_ref[...] += total

        @pl.when(step == steps - 1)
        def _():
            if not last:
                o_ref[...] = total_ref[...]
                return
            values = [ref[...].astype(f32) for ref in refs[1 : 1 + len(states)]]
            if len(states) == 2:
                first = place_ref[1] == 0
                values = [
                    jnp.where(first, values[0], values[1]),
                    jnp.where(first, values[1], values[0]),
                ]
            pieces = pack([total_ref[...], jnp.concatenate(values, axis=0)])
            for b in range(count // mine):
                at = slice(b * mine, (b + 1) * mine)
                o_ref[b] = jnp.concatenate([piece[at] for piece in pieces], axis=0).astype(bf16)

    fixed = lambda shape: pl.BlockSpec(shape, lambda i, p: (0,) * len(shape))
    more = [added, *states] if last else []
    pieces, lanes = packed(width)
    shape = (count // mine, pieces * mine, lanes) if last else (count, width)
    return pl.pallas_call(
        kernel,
        grid_spec=pltpu.PrefetchScalarGridSpec(
            num_scalar_prefetch=1,
            grid=(steps,),
            in_specs=[
                pl.BlockSpec((chips, count, together * BLOCK), lambda i, p: (0, 0, i)),
                pl.BlockSpec((width, tile), lambda i, p: (0, i)),
            ]
            + [fixed(x.shape) for x in more],
            out_specs=fixed(shape),
            scratch_shapes=[pltpu.VMEM((count, width), f32)],
        ),
        out_shape=jax.ShapeDtypeStruct(shape, bf16 if last else f32),
        compiler_params=params(16 * 2**20),
        cost_estimate=cost(2 * count * width * tile * steps, 2 * width * tile * steps),
        name="down_product",
    )(place, act, weight, *more)


def attention(cache_len, queries, kv_cache, new_kv, owners):
    steps, seqs, heads, per, size = queries.shape
    slots = kv_cache.shape[3]
    factor = size ** (-0.5)
    share = heads * per // owners
    splits = 2 if heads % 2 == 0 and owners % 2 == 0 else 1
    mine = heads // splits
    rows = steps * per
    pad = 8 - steps

    def kernel(len_ref, q_ref, kv_ref, new_ref, o_ref, h_ref):
        live = len_ref[lax.axis_index("wide") * seqs + pl.program_id(0)]
        valid = lax.broadcasted_iota(jnp.int32, (rows, slots), 1) < live
        step_of = lax.broadcasted_iota(jnp.int32, (rows, 8), 0) // per
        fresh = lax.broadcasted_iota(jnp.int32, (rows, 8), 1) <= step_of

        def product(left, right, dim):
            return lax.dot_general(
                left, right, (((1,), (dim,)), ((), ())), preferred_element_type=f32
            )

        new = []
        for n in range(2):
            value = new_ref[:, n, 0].astype(f32)
            if splits == 2:
                value = jnp.where(pl.program_id(1) == 0, value[:, :mine], value[:, mine:])
            new.append(value)
        at = range(mine)
        queries_of = [
            q_ref[:, 0, h].astype(f32).reshape(rows, size).astype(bf16) for h in at
        ]
        new_keys, new_values = [
            [
                jnp.concatenate([value[:, h], jnp.zeros((pad, size), f32)], axis=0).astype(bf16)
                for h in at
            ]
            for value in new
        ]
        cached = [product(queries_of[h], kv_ref[0, 0, h], 1) for h in at]
        recent = [product(queries_of[h], new_keys[h], 1) for h in at]
        cached = [jnp.where(valid, value * factor, NEG) for value in cached]
        recent = [jnp.where(fresh, value * factor, NEG) for value in recent]
        top = [
            jnp.maximum(
                jnp.max(cached[h], axis=1, keepdims=True), jnp.max(recent[h], axis=1, keepdims=True)
            )
            for h in at
        ]
        cached = [jnp.exp(cached[h] - top[h]) for h in at]
        recent = [jnp.exp(recent[h] - top[h]) for h in at]
        share_of = [
            1.0
            / (
                jnp.sum(cached[h], axis=1, keepdims=True)
                + jnp.sum(recent[h], axis=1, keepdims=True)
            )
            for h in at
        ]
        cached = [(cached[h] * share_of[h]).astype(bf16) for h in at]
        recent = [(recent[h] * share_of[h]).astype(bf16) for h in at]
        mixed = [
            product(cached[h], kv_ref[1, 0, h], 0) + product(recent[h], new_values[h], 0)
            for h in at
        ]
        for h in at:
            value = mixed[h].reshape(steps, per, size)
            o_ref[:, 0, h] = value.astype(bf16)
            for j in range(per):
                head = h * per + j
                h_ref[head // share, 0, :, pl.ds(head % share * size, size)] = value[:, j].astype(
                    bf16
                )

    return pl.pallas_call(
        kernel,
        grid_spec=pltpu.PrefetchScalarGridSpec(
            num_scalar_prefetch=1,
            grid=(seqs, splits),
            in_specs=[
                pl.BlockSpec((steps, 1, mine, per, size), lambda s, i, n: (0, s, i, 0, 0)),
                pl.BlockSpec((2, 1, mine, slots, size), lambda s, i, n: (0, s, i, 0, 0)),
                pl.BlockSpec((steps, 2, 1, heads, size), lambda s, i, n: (0, 0, s, 0, 0)),
            ],
            out_specs=[
                pl.BlockSpec((steps, 1, mine, per, size), lambda s, i, n: (0, s, i, 0, 0)),
                pl.BlockSpec(
                    (owners // splits, 1, steps, share * size), lambda s, i, n: (i, s, 0, 0)
                ),
            ],
        ),
        out_shape=[
            jax.ShapeDtypeStruct(queries.shape, bf16),
            jax.ShapeDtypeStruct((owners, seqs, steps, share * size), bf16),
        ],
        compiler_params=params(),
        cost_estimate=cost(4 * rows * heads * slots * size * seqs, 4 * heads * slots * size * seqs),
        name="attention",
    )(cache_len, queries, *in_hbm(kv_cache), new_kv)


def swap_cores(value):
    count = lax.axis_size("wide")
    return lax.ppermute(value, "wide", [(i, i ^ 1) for i in range(count)])


def exchange(value):
    return lax.all_to_all(value, "wide", split_axis=0, concat_axis=0, tiled=True)


def exchange_chips(value):
    count = lax.axis_size("wide")
    groups = [list(range(core, count, 2)) for core in range(2)]
    return lax.all_to_all(
        value, "wide", split_axis=0, concat_axis=0, tiled=True, axis_index_groups=groups
    )


def exchange_halves(kept, got, send, beside):
    count = lax.axis_size("wide")
    bit = 2
    while True:
        half = kept.shape[0] // 2
        received = lax.ppermute(send, "wide", [(i, i ^ bit) for i in range(count)])
        if bit == 2:
            received, beside = lax.optimization_barrier((received, beside))
        total = kept[:half].astype(f32) + received.astype(f32)
        if got is not None:
            total = total + got[:half].astype(f32)
        got = None
        bit *= 2
        if bit == count:
            return total[0], beside
        kept = total.astype(bf16)
        send = kept[half // 2 :]


def exchange_pairs(value):
    count = lax.axis_size("wide")
    groups = [[rest + 4 * k for k in range(count // 4)] for rest in range(4)]
    value = value.reshape(count // 4, 2, *value.shape[1:])
    value = lax.all_to_all(
        value, "wide", split_axis=0, concat_axis=0, tiled=True, axis_index_groups=groups
    )
    value = jnp.sum(value.astype(f32), axis=0)
    received = lax.ppermute(value[1].astype(bf16), "wide", [(i, i ^ 2) for i in range(count)])
    return value[0] + received.astype(f32)


def on_device(
    residual_in,
    norm_gain,
    gate_weight,
    up_weight,
    down_weight,
    out_weight,
    queries,
    kv_cache,
    new_kv,
    cache_len,
):
    owners = lax.axis_size("wide")
    groups = lax.axis_size("grp")
    me = lax.axis_index("wide")
    steps, seqs, width_dev = residual_in.shape
    seq_dev = seqs // owners
    tokens = steps * seqs
    mine = steps * seq_dev
    width = width_dev * owners
    chips = owners // 2
    hidden_units = gate_weight.shape[1]

    parts = groups if hidden_units % (groups * owners * 2 * BLOCK) == 0 else 1
    units = hidden_units // parts
    per_owner = units // (owners * BLOCK)
    runs = (per_owner - max(1, per_owner // 4), max(1, per_owner // 4))
    part = lax.axis_index("grp") if parts > 1 else jnp.zeros((), jnp.int32)
    place = jnp.stack([me % 2, part, me // 2, me]).astype(jnp.int32)

    attn_out, heads = attention(cache_len, queries, kv_cache, new_kv, owners)
    heads = exchange(heads)

    out_levels, out_scale = out_levels_of(out_weight, pick_tile(out_weight.shape[1], 2560))
    heads, out_levels, out_scale = lax.optimization_barrier((heads, out_levels, out_scale))
    heads = heads.reshape(tokens, -1)
    projected = exchange(out_product(heads, out_levels, out_scale, owners))

    down = down_weight.T
    rows = gate_weight.shape[0]
    chunk = math.gcd(rows, BLOCK)
    tile = pick_tile(units, 2048)
    paired = pair_shares_blocks(rows) and down.shape[0] == rows
    weights = [gate_weight, up_weight]
    if paired:
        tops = edge_max(place, [*weights, down], units, chunk, pick_tile(units, 4096))
        tops = swap_cores(tops)
    else:
        tops = joined_max(place, weights, units, chunk, tile)
    away = rounded_weights(
        place, weights, tops, paired, 0, 1, units, chunk, pick_tile(units // 2, 2048)
    )
    gain = lax.dynamic_slice_in_dim(norm_gain, me * width_dev, width_dev, 0).astype(f32)[None]
    residual = jnp.transpose(residual_in, (1, 0, 2)).reshape(tokens, width_dev).astype(f32)
    projected, away, gain, residual = lax.optimization_barrier(
        (projected, away, gain, residual)
    )
    hidden = (residual + jnp.sum(projected.astype(f32), axis=0)).astype(bf16)

    states = [hidden]
    if parts == 2:
        states.append(lax.ppermute(hidden, "grp", [(0, 1), (1, 0)]))
    elif parts > 1:
        states = [lax.all_gather(hidden, "grp", axis=0, tiled=True)]

    def product(weights, tops):
        return gate_up_product(place, states, gain, *weights, tops, runs, chips, paired, units)

    got = [swap_cores(value) for value in product(away, None)]
    kept = list(product(weights, tops))
    half = chips // 2
    send = (kept[0][half:].astype(f32) + got[0][half:].astype(f32)).astype(bf16)
    send, kept[1], got[1] = lax.optimization_barrier((send, kept[1], got[1]))
    second = (kept[1].astype(f32) + got[1].astype(f32)).astype(bf16)
    second, place = lax.optimization_barrier((second, place))

    down_chunk = math.gcd(down.shape[0], BLOCK)
    row = 2
    if not paired:
        tops, row = joined_max(place, [down], units, down_chunk, pick_tile(units, 4096)), 0
    home, away = [
        rounded_weights(
            place, [down], tops, paired, row, flip, units, down_chunk, pick_tile(units // 2, 4096)
        )[0]
        for flip in range(2)
    ]
    last = exchange_pairs(second)
    first, (home, away) = exchange_halves(kept[0], got[0], send, (home, away))

    squares = jnp.sum(last[:, 2 * runs[1] * BLOCK :], axis=1, keepdims=True)
    scale = lax.rsqrt(squares / width + EPS_NORM)

    def act_of(summed, run):
        size = run * BLOCK
        gate = summed[:, :size] * scale
        up = summed[:, size : 2 * size] * scale
        return (jax.nn.silu(gate) * up).astype(bf16)

    act = jnp.concatenate([act_of(first, runs[0]), act_of(last, runs[1])], axis=1)
    act = exchange_chips(jnp.broadcast_to(act[None], (chips,) + act.shape))
    other = swap_cores(act)
    ffn = down_product(place, act, home, None, states, mine)
    both = down_product(place, other, away, ffn, states, mine)

    axes = ("grp", "wide") if parts > 1 else "wide"
    both = lax.all_to_all(both, axes, split_axis=0, concat_axis=0, tiled=True)
    pieces, lanes = packed(width_dev)
    both = both.reshape(parts, owners, pieces, seq_dev, steps, lanes)
    ffn, hidden_out = unpack([both[:, :, n] for n in range(pieces)], width_dev)
    if parts > 1:
        ffn = jnp.sum(ffn.astype(f32), axis=0, keepdims=True).astype(bf16)
    ffn_out = jnp.transpose(ffn[0], (2, 1, 0, 3)).reshape(steps, seq_dev, width)
    hidden_out = jnp.transpose(hidden_out[0], (2, 1, 0, 3)).reshape(steps, seq_dev, width)
    return (ffn_out, attn_out, hidden_out)


def solution(mesh):
    placed = (
        P("grp", None, "wide"),
        P(),
        P("wide", None),
        P("wide", None),
        P(None, "wide"),
        P("wide", None),
        P("grp", "wide", None, None, None),
        P(None, ("grp", "wide"), None, None, None),
        P("grp", None, "wide", None, None),
        P("grp"),
    )
    return jax.shard_map(
        on_device,
        mesh=mesh,
        in_specs=placed,
        out_specs=(
            P("grp", "wide", None),
            P("grp", "wide", None, None, None),
            P("grp", "wide", None),
        ),
        check_vma=False,
    )
```

```python
import functools
import math

import jax
import jax.numpy as jnp
from jax import lax
from jax.experimental import pallas as pl
from jax.experimental.pallas import tpu as pltpu
from jax.sharding import PartitionSpec as P

BLOCK = 128
QMAX = 448.0
EPS_NORM = 1e-06
EPS_SCALE = 1e-06
NEG = -1e30
LANES = 128
VMEM = 56 * 2**20

f32 = jnp.float32
bf16 = jnp.bfloat16
f8 = jnp.float8_e4m3fn


def params(limit=VMEM):
    return pltpu.CompilerParams(vmem_limit_bytes=limit)


def in_hbm(*arrays):
    return [pltpu.with_memory_space_constraint(x, pltpu.HBM) for x in arrays]


def in_vmem(*arrays):
    return [pltpu.with_memory_space_constraint(x, pltpu.VMEM) for x in arrays]


def cost(flops, read):
    return pl.CostEstimate(flops=int(flops), bytes_accessed=int(read), transcendentals=0)


def pick_tile(cols, most):
    tile = most
    while cols % tile:
        tile -= LANES
    return tile


def spread_lanes(tops):
    out = []
    for g in range(tops.shape[1] // LANES):
        top = jnp.max(tops[:, g * LANES : (g + 1) * LANES], axis=1, keepdims=True)
        out.append(jnp.broadcast_to(top, (tops.shape[0], LANES)))
    return jnp.concatenate(out, axis=1)


def rows_max(ref, start, size):
    return jnp.max(jnp.abs(ref[pl.ds(start, size), :]), axis=0, keepdims=True).astype(f32)


def fill_rows(rows):
    return jnp.concatenate(rows + [rows[0]] * (8 - len(rows)), axis=0)


def chunk_max(place, weights, cols, chunk, tile):
    rows = weights[0].shape[0]
    parts = rows // chunk
    count = len(weights)
    steps = cols // tile

    def kernel(place_ref, *refs):
        for a in range(count):
            tops = [rows_max(refs[a], j * chunk, chunk) for j in range(parts)]
            refs[count][a] = spread_lanes(fill_rows(tops))

    return pl.pallas_call(
        kernel,
        grid_spec=pltpu.PrefetchScalarGridSpec(
            num_scalar_prefetch=1,
            grid=(steps,),
            in_specs=[pl.BlockSpec((rows, tile), lambda i, p: (0, p[1] * steps + i))] * count,
            out_specs=pl.BlockSpec((count, 8, tile), lambda i, p: (0, 0, i)),
        ),
        out_shape=jax.ShapeDtypeStruct((count, 8, cols), f32),
        compiler_params=params(),
        cost_estimate=cost(2 * count * rows * cols, 2 * count * rows * cols),
        name="chunk_max",
    )(place, *in_hbm(*weights))


def edge_max(place, weights, cols, chunk, tile):
    parts = weights[0].shape[0] // chunk
    count = len(weights)
    steps = cols // tile

    def kernel(place_ref, *refs):
        refs[count][...] = spread_lanes(
            fill_rows([rows_max(refs[a], 0, chunk) for a in range(count)])
        )

    return pl.pallas_call(
        kernel,
        grid_spec=pltpu.PrefetchScalarGridSpec(
            num_scalar_prefetch=1,
            grid=(steps,),
            in_specs=[
                pl.BlockSpec(
                    (chunk, tile), lambda i, p: ((1 - p[0]) * (parts - 1), p[1] * steps + i)
                )
            ]
            * count,
            out_specs=pl.BlockSpec((8, tile), lambda i, p: (0, i)),
        ),
        out_shape=jax.ShapeDtypeStruct((8, cols), f32),
        compiler_params=params(),
        cost_estimate=cost(2 * count * chunk * cols, 2 * count * chunk * cols),
        name="edge_max",
    )(place, *in_hbm(*weights))


def join_pair(w_ref, other, odd, chunk, parts):
    mine = [rows_max(w_ref, j * chunk, chunk) for j in range(parts)]
    joined = []
    for j in range(parts):
        even = mine[j ^ 1] if j ^ 1 < parts else other
        back = j - 1 if j % 2 == 0 else j + 1
        near = other if back < 0 else mine[back]
        joined.append(jnp.maximum(mine[j], jnp.where(odd, near, even)))
    return fill_rows(joined)


def block_scales(w_ref, top_ref, place_ref, a, paired, chunk, parts):
    if paired:
        other = top_ref[pl.ds(a, 1), :]
        tops = spread_lanes(join_pair(w_ref, other, place_ref[0] == 1, chunk, parts))
    else:
        tops = top_ref[a]
    largest = tops + EPS_SCALE
    return QMAX / largest, largest * (1.0 / QMAX)


def rounded_chunk(w_ref, j, chunk, factor, scale):
    value = w_ref[pl.ds(j * chunk, chunk), :].astype(f32) * factor[j : j + 1]
    return (value.astype(f8).astype(f32) * scale[j : j + 1]).astype(bf16)


def top_spec_of(tops, paired, tile, at):
    if paired:
        return pl.BlockSpec((tops.shape[0], tile), lambda i, p: (0, at(i, p)))
    return pl.BlockSpec((tops.shape[0], 8, tile), lambda i, p: (0, 0, at(i, p)))


def rounded_weights(place, weights, tops, paired, first, flip, cols, chunk, tile):
    rows = weights[0].shape[0]
    parts = rows // chunk
    count = len(weights)
    taken = 1 if flip is None else 2
    steps = cols // (taken * tile)

    def columns(i, p):
        return i if flip is None else (p[0] ^ flip) * steps + i

    def kernel(place_ref, *refs):
        for a in range(count):
            factor, scale = block_scales(
                refs[a], refs[count], place_ref, first + a, paired, chunk, parts
            )
            for j in range(parts):
                refs[count + 1 + a][pl.ds(j * chunk, chunk), :] = rounded_chunk(
                    refs[a], j, chunk, factor, scale
                )

    return pl.pallas_call(
        kernel,
        grid_spec=pltpu.PrefetchScalarGridSpec(
            num_scalar_prefetch=1,
            grid=(steps,),
            in_specs=[
                pl.BlockSpec((rows, tile), lambda i, p: (0, taken * p[1] * steps + columns(i, p)))
            ]
            * count
            + [top_spec_of(tops, paired, tile, columns)],
            out_specs=[pl.BlockSpec((rows, tile), lambda i, p: (0, i))] * count,
        ),
        out_shape=[jax.ShapeDtypeStruct((rows, cols // taken), bf16)] * count,
        compiler_params=params(),
        cost_estimate=cost(
            6 * count * rows * cols // taken, 4 * count * rows * cols // taken
        ),
        name="rounded_weights",
    )(place, *in_hbm(*weights), *in_vmem(tops))


def join_group(parts, size, dim):
    count = lax.axis_size("wide")
    me = lax.axis_index("wide")
    share = parts.shape[dim]
    shape = list(parts.shape)
    shape[dim] = share * size
    out = jnp.zeros(shape, parts.dtype)
    out = lax.dynamic_update_slice_in_dim(out, parts, (me % size) * share, dim)
    for step in range(1, size):
        perm = [(i // size * size + (i + step) % size, i) for i in range(count)]
        got = lax.ppermute(parts, "wide", perm)
        out = lax.dynamic_update_slice_in_dim(out, got, ((me + step) % size) * share, dim)
    return out


def pair_shares_blocks(rows):
    return math.lcm(rows, BLOCK) == 2 * rows and math.gcd(rows, BLOCK) == BLOCK // 2


def joined_max(place, weights, cols, chunk, tile):
    rows = weights[0].shape[0]
    size = math.lcm(rows, BLOCK) // rows
    per = BLOCK // chunk
    parts = rows // chunk
    tops = chunk_max(place, weights, cols, chunk, tile)
    if size == 1:
        return tops
    joined = join_group(tops[:, :parts], size, 1)
    blocks = joined.reshape(joined.shape[0], -1, per, joined.shape[2])
    joined = jnp.broadcast_to(jnp.max(blocks, axis=2, keepdims=True), blocks.shape)
    joined = joined.reshape(joined.shape[0], size * parts, -1)
    own = lax.dynamic_slice_in_dim(joined, (lax.axis_index("wide") % size) * parts, parts, 1)
    return jnp.pad(own, ((0, 0), (0, 8 - parts), (0, 0)))


def out_levels_of(weight, tile):
    rows, cols = weight.shape
    parts = rows // BLOCK

    def kernel(w_ref, o_ref, s_ref):
        tops = spread_lanes(fill_rows([rows_max(w_ref, j * BLOCK, BLOCK) for j in range(parts)]))
        largest = tops + EPS_SCALE
        factor = QMAX / largest
        s_ref[...] = largest * (1.0 / QMAX)
        for j in range(parts):
            at = pl.ds(j * BLOCK, BLOCK)
            o_ref[at, :] = (w_ref[at, :].astype(f32) * factor[j : j + 1]).astype(f8)

    columns = lambda i: (0, i)
    return pl.pallas_call(
        kernel,
        grid=(cols // tile,),
        in_specs=[pl.BlockSpec((rows, tile), columns)],
        out_specs=[pl.BlockSpec((rows, tile), columns), pl.BlockSpec((8, tile), columns)],
        out_shape=[
            jax.ShapeDtypeStruct((rows, cols), f8),
            jax.ShapeDtypeStruct((8, cols), f32),
        ],
        compiler_params=params(),
        cost_estimate=cost(8 * rows * cols, 3 * rows * cols),
        name="out_levels_of",
    )(*in_hbm(weight))


def folded(count, width):
    if width % LANES != LANES // 2 or count % 16:
        return count, width
    return count * width // LANES, LANES


def fold(value):
    count, width = value.shape
    if folded(count, width) == (count, width):
        return value
    whole, half = width // LANES * LANES, count // 2
    pieces = [value[:, at : at + LANES] for at in range(0, whole, LANES)]
    rest = jnp.concatenate([value[:half, whole:], value[half:, whole:]], axis=1)
    return jnp.concatenate([*pieces, rest], axis=0)


def unfold(value, count, width):
    if value.shape == (count, width):
        return value
    whole = width // LANES
    rest = value[whole * count :]
    rest = jnp.concatenate([rest[:, : LANES // 2], rest[:, LANES // 2 :]], axis=0)
    pieces = [value[n * count : (n + 1) * count] for n in range(whole)]
    return jnp.concatenate([*pieces, rest], axis=1)


def out_product(left, levels, scale, owners):
    count, rows = left.shape
    cols = levels.shape[1]
    parts = rows // BLOCK
    share = cols // owners
    tile = pick_tile(cols, 4 * math.lcm(share, LANES))
    per = tile // share

    def kernel(x_ref, l_ref, s_ref, o_ref):
        total = None
        for j in range(parts):
            at = pl.ds(j * BLOCK, BLOCK)
            part = jnp.dot(x_ref[:, at], l_ref[at, :].astype(bf16), preferred_element_type=f32)
            part = part * s_ref[pl.ds(j, 1), :]
            total = part if total is None else total + part
        total = total.astype(bf16)
        for q in range(per):
            o_ref[q] = fold(total[:, q * share : (q + 1) * share])

    return pl.pallas_call(
        kernel,
        grid=(cols // tile,),
        in_specs=[
            pl.BlockSpec((count, rows), lambda i: (0, 0)),
            pl.BlockSpec((rows, tile), lambda i: (0, i)),
            pl.BlockSpec((8, tile), lambda i: (0, i)),
        ],
        out_specs=pl.BlockSpec((per, *folded(count, share)), lambda i: (i, 0, 0)),
        out_shape=jax.ShapeDtypeStruct((owners, *folded(count, share)), bf16),
        compiler_params=params(),
        cost_estimate=cost(2 * count * rows * cols, rows * cols),
        name="out_product",
    )(left, levels, scale)


def gate_up_product(place, hidden, gain, gate, up, tops, runs, chips, paired, cols):
    groups = len(hidden)
    rows = gate.shape[0]
    count = groups * hidden[0].shape[0]
    chunk = math.gcd(rows, BLOCK)
    parts = rows // chunk
    extra = -(-4 * chips // LANES) * LANES
    units = [run * BLOCK for run in runs]
    widths = (2 * units[0], 2 * units[1] + extra)
    together = 2 if sum(runs) % 2 == 0 else 1
    tile = together * chips * BLOCK

    def kernel(place_ref, *refs):
        h_refs = refs[:groups]
        gain_ref, g_ref, u_ref = refs[groups : groups + 3]
        o_refs, x_ref, p_ref = refs[-4:-2], refs[-2], refs[-1]
        step = pl.program_id(0)

        @pl.when(step == 0)
        def _():
            values = [ref[...].astype(f32) for ref in h_refs]
            if groups == 2:
                first = place_ref[1] == 0
                values = [
                    jnp.where(first, values[0], values[1]),
                    jnp.where(first, values[1], values[0]),
                ]
            states = jnp.concatenate(values, axis=0)
            x_ref[...] = (states * gain_ref[...]).astype(bf16)
            squares = jnp.sum(states * states, axis=1, keepdims=True)
            high = squares.astype(bf16).astype(f32)
            lane = lax.broadcasted_iota(jnp.int32, (count, extra), 1)
            at = 2 * place_ref[3]
            p_ref[...] = jnp.where(
                lane == at, high, jnp.where(lane == at + 1, squares - high, 0.0)
            )

        totals = []
        for a, ref in enumerate((g_ref, u_ref)):
            if tops is None:
                weight = ref[...]
            else:
                factor, scale = block_scales(
                    ref, refs[groups + 3], place_ref, a, paired, chunk, parts
                )
                weight = jnp.concatenate(
                    [rounded_chunk(ref, j, chunk, factor, scale) for j in range(parts)], axis=0
                )
            totals.append(jnp.dot(x_ref[...], weight, preferred_element_type=f32))

        def write(run, block, position, q):
            ref = o_refs[run]
            at = ((runs[0] * run + block) % together * chips + q) * BLOCK
            for a, total in enumerate(totals):
                lanes = pl.ds(a * units[run] + block * BLOCK, BLOCK)
                ref[position, :, lanes] = total[:, at : at + BLOCK].astype(bf16)
            if run == 1 and block == 0:
                ref[position, :, pl.ds(2 * units[1], extra)] = p_ref[...].astype(bf16)

        def write_first(block):
            for q in range(chips):
                position, rest = 0, q ^ place_ref[2]
                for _ in range(chips.bit_length() - 1):
                    position, rest = position * 2 + rest % 2, rest // 2
                write(0, block, position, q)

        def write_second(block):
            for q in range(chips):
                write(1, block, q ^ (place_ref[2] % 2), q)

        for block in range(runs[0]):
            pl.when(step == block // together)(functools.partial(write_first, block))
        for block in range(runs[1]):
            pl.when(step == (runs[0] + block) // together)(
                functools.partial(write_second, block)
            )

    steps = sum(runs) // together
    home = lambda i, p: p[0] * steps + i
    fixed = lambda i, p: (0, 0)
    out_shapes = [(chips, count, width) for width in widths]
    if tops is None:
        weight_spec = pl.BlockSpec((rows, tile), lambda i, p: (0, i))
    else:
        weight_spec = pl.BlockSpec((rows, tile), lambda i, p: (0, 2 * p[1] * steps + home(i, p)))
    in_specs = [pl.BlockSpec(x.shape, fixed) for x in hidden]
    in_specs += [pl.BlockSpec((1, rows), fixed), weight_spec, weight_spec]
    if tops is not None:
        in_specs.append(top_spec_of(tops, paired, tile, home))
    return pl.pallas_call(
        kernel,
        grid_spec=pltpu.PrefetchScalarGridSpec(
            num_scalar_prefetch=1,
            grid=(steps,),
            in_specs=in_specs,
            out_specs=[pl.BlockSpec(shape, lambda i, p: (0, 0, 0)) for shape in out_shapes],
            scratch_shapes=[pltpu.VMEM((count, rows), bf16), pltpu.VMEM((count, extra), f32)],
        ),
        out_shape=[jax.ShapeDtypeStruct(shape, bf16) for shape in out_shapes],
        compiler_params=params(),
        cost_estimate=cost(4 * count * rows * cols // 2, 2 * rows * cols),
        name="gate_up_product",
    )(place, *in_vmem(*hidden), gain, *in_hbm(gate, up), *([] if tops is None else in_vmem(tops)))


def packed(width):
    return (2 * (width // LANES) + 1, LANES) if width % LANES == LANES // 2 else (2, width)


def pack(pair):
    width = pair[0].shape[1]
    if packed(width)[1] == width:
        return pair
    whole = width // LANES * LANES
    pieces = [x[:, at : at + LANES] for x in pair for at in range(0, whole, LANES)]
    return [*pieces, jnp.concatenate([x[:, whole:] for x in pair], axis=1)]


def unpack(pieces, width):
    if packed(width)[1] == width:
        return pieces
    each, rest = width // LANES, width % LANES
    last = pieces[-1]
    return [
        jnp.concatenate(
            [*pieces[n * each : (n + 1) * each], last[..., n * rest : (n + 1) * rest]], axis=-1
        )
        for n in range(2)
    ]


def down_product(place, act, weight, added, states, mine):
    chips, count, units = act.shape
    width = weight.shape[0]
    together = 2 if units % (2 * BLOCK) == 0 else 1
    tile = together * chips * BLOCK
    steps = units // (together * BLOCK)
    last = added is not None

    def kernel(place_ref, a_ref, w_ref, *refs):
        step = pl.program_id(0)
        o_ref, total_ref = refs[-2:]
        total = lax.dot_general(
            jnp.concatenate(
                [
                    a_ref[q, :, pl.ds(t * BLOCK, BLOCK)]
                    for t in range(together)
                    for q in range(chips)
                ],
                axis=1,
            ),
            w_ref[...],
            (((1,), (1,)), ((), ())),
            preferred_element_type=f32,
        )

        @pl.when(step == 0)
        def _():
            total_ref[...] = refs[0][...] + total if last else total

        @pl.when(step > 0)
        def _():
            total_ref[...] += total

        @pl.when(step == steps - 1)
        def _():
            if not last:
                o_ref[...] = total_ref[...]
                return
            values = [ref[...].astype(f32) for ref in refs[1 : 1 + len(states)]]
            if len(states) == 2:
                first = place_ref[1] == 0
                values = [
                    jnp.where(first, values[0], values[1]),
                    jnp.where(first, values[1], values[0]),
                ]
            pieces = pack([total_ref[...], jnp.concatenate(values, axis=0)])
            for b in range(count // mine):
                at = slice(b * mine, (b + 1) * mine)
                o_ref[b] = jnp.concatenate([piece[at] for piece in pieces], axis=0).astype(bf16)

    fixed = lambda shape: pl.BlockSpec(shape, lambda i, p: (0,) * len(shape))
    more = [added, *states] if last else []
    pieces, lanes = packed(width)
    shape = (count // mine, pieces * mine, lanes) if last else (count, width)
    return pl.pallas_call(
        kernel,
        grid_spec=pltpu.PrefetchScalarGridSpec(
            num_scalar_prefetch=1,
            grid=(steps,),
            in_specs=[
                pl.BlockSpec((chips, count, together * BLOCK), lambda i, p: (0, 0, i)),
                pl.BlockSpec((width, tile), lambda i, p: (0, i)),
            ]
            + [fixed(x.shape) for x in more],
            out_specs=fixed(shape),
            scratch_shapes=[pltpu.VMEM((count, width), f32)],
        ),
        out_shape=jax.ShapeDtypeStruct(shape, bf16 if last else f32),
        compiler_params=params(16 * 2**20),
        cost_estimate=cost(2 * count * width * tile * steps, 2 * width * tile * steps),
        name="down_product",
    )(place, act, weight, *more)


def attention(cache_len, queries, kv_cache, new_kv, owners):
    steps, seqs, heads, per, size = queries.shape
    slots = kv_cache.shape[3]
    factor = size ** (-0.5)
    share = heads * per // owners
    splits = 2 if heads % 2 == 0 and owners % 2 == 0 else 1
    mine = heads // splits
    rows = steps * per
    pad = 8 - steps

    def kernel(len_ref, q_ref, kv_ref, new_ref, o_ref, h_ref):
        live = len_ref[lax.axis_index("wide") * seqs + pl.program_id(0)]
        valid = lax.broadcasted_iota(jnp.int32, (rows, slots), 1) < live
        step_of = lax.broadcasted_iota(jnp.int32, (rows, 8), 0) // per
        fresh = lax.broadcasted_iota(jnp.int32, (rows, 8), 1) <= step_of

        def product(left, right, dim):
            return lax.dot_general(
                left, right, (((1,), (dim,)), ((), ())), preferred_element_type=f32
            )

        new = []
        for n in range(2):
            value = new_ref[:, n, 0].astype(f32)
            if splits == 2:
                value = jnp.where(pl.program_id(1) == 0, value[:, :mine], value[:, mine:])
            new.append(value)
        at = range(mine)
        queries_of = [
            q_ref[:, 0, h].astype(f32).reshape(rows, size).astype(bf16) for h in at
        ]
        new_keys, new_values = [
            [
                jnp.concatenate([value[:, h], jnp.zeros((pad, size), f32)], axis=0).astype(bf16)
                for h in at
            ]
            for value in new
        ]
        cached = [product(queries_of[h], kv_ref[0, 0, h], 1) for h in at]
        recent = [product(queries_of[h], new_keys[h], 1) for h in at]
        cached = [jnp.where(valid, value * factor, NEG) for value in cached]
        recent = [jnp.where(fresh, value * factor, NEG) for value in recent]
        top = [
            jnp.maximum(
                jnp.max(cached[h], axis=1, keepdims=True), jnp.max(recent[h], axis=1, keepdims=True)
            )
            for h in at
        ]
        cached = [jnp.exp(cached[h] - top[h]) for h in at]
        recent = [jnp.exp(recent[h] - top[h]) for h in at]
        share_of = [
            1.0
            / (
                jnp.sum(cached[h], axis=1, keepdims=True)
                + jnp.sum(recent[h], axis=1, keepdims=True)
            )
            for h in at
        ]
        cached = [(cached[h] * share_of[h]).astype(bf16) for h in at]
        recent = [(recent[h] * share_of[h]).astype(bf16) for h in at]
        mixed = [
            product(cached[h], kv_ref[1, 0, h], 0) + product(recent[h], new_values[h], 0)
            for h in at
        ]
        for h in at:
            value = mixed[h].reshape(steps, per, size)
            o_ref[:, 0, h] = value.astype(bf16)
            for j in range(per):
                head = h * per + j
                h_ref[head // share, 0, :, pl.ds(head % share * size, size)] = value[:, j].astype(
                    bf16
                )

    return pl.pallas_call(
        kernel,
        grid_spec=pltpu.PrefetchScalarGridSpec(
            num_scalar_prefetch=1,
            grid=(seqs, splits),
            in_specs=[
                pl.BlockSpec((steps, 1, mine, per, size), lambda s, i, n: (0, s, i, 0, 0)),
                pl.BlockSpec((2, 1, mine, slots, size), lambda s, i, n: (0, s, i, 0, 0)),
                pl.BlockSpec((steps, 2, 1, heads, size), lambda s, i, n: (0, 0, s, 0, 0)),
            ],
            out_specs=[
                pl.BlockSpec((steps, 1, mine, per, size), lambda s, i, n: (0, s, i, 0, 0)),
                pl.BlockSpec(
                    (owners // splits, 1, steps, share * size), lambda s, i, n: (i, s, 0, 0)
                ),
            ],
        ),
        out_shape=[
            jax.ShapeDtypeStruct(queries.shape, bf16),
            jax.ShapeDtypeStruct((owners, seqs, steps, share * size), bf16),
        ],
        compiler_params=params(),
        cost_estimate=cost(4 * rows * heads * slots * size * seqs, 4 * heads * slots * size * seqs),
        name="attention",
    )(cache_len, queries, *in_hbm(kv_cache), new_kv)


def swap_cores(value):
    count = lax.axis_size("wide")
    return lax.ppermute(value, "wide", [(i, i ^ 1) for i in range(count)])


def exchange(value):
    return lax.all_to_all(value, "wide", split_axis=0, concat_axis=0, tiled=True)


def exchange_chips(value):
    count = lax.axis_size("wide")
    groups = [list(range(core, count, 2)) for core in range(2)]
    return lax.all_to_all(
        value, "wide", split_axis=0, concat_axis=0, tiled=True, axis_index_groups=groups
    )


def exchange_halves(kept, got, send, beside):
    count = lax.axis_size("wide")
    bit = 2
    while True:
        half = kept.shape[0] // 2
        received = lax.ppermute(send, "wide", [(i, i ^ bit) for i in range(count)])
        if bit == 2:
            received, beside = lax.optimization_barrier((received, beside))
        total = kept[:half].astype(f32) + received.astype(f32)
        if got is not None:
            total = total + got[:half].astype(f32)
        got = None
        bit *= 2
        if bit == count:
            return total[0], beside
        kept = total.astype(bf16)
        send = kept[half // 2 :]


def exchange_pairs(value):
    count = lax.axis_size("wide")
    groups = [[rest + 4 * k for k in range(count // 4)] for rest in range(4)]
    value = value.reshape(count // 4, 2, *value.shape[1:])
    value = lax.all_to_all(
        value, "wide", split_axis=0, concat_axis=0, tiled=True, axis_index_groups=groups
    )
    value = jnp.sum(value.astype(f32), axis=0)
    received = lax.ppermute(value[1].astype(bf16), "wide", [(i, i ^ 2) for i in range(count)])
    return value[0] + received.astype(f32)


def on_device(
    residual_in,
    norm_gain,
    gate_weight,
    up_weight,
    down_weight,
    out_weight,
    queries,
    kv_cache,
    new_kv,
    cache_len,
):
    owners = lax.axis_size("wide")
    groups = lax.axis_size("grp")
    me = lax.axis_index("wide")
    steps, seqs, width_dev = residual_in.shape
    seq_dev = seqs // owners
    tokens = steps * seqs
    mine = steps * seq_dev
    width = width_dev * owners
    chips = owners // 2
    hidden_units = gate_weight.shape[1]

    parts = groups if hidden_units % (groups * owners * 2 * BLOCK) == 0 else 1
    units = hidden_units // parts
    per_owner = units // (owners * BLOCK)
    runs = (per_owner - max(1, per_owner // 4), max(1, per_owner // 4))
    part = lax.axis_index("grp") if parts > 1 else jnp.zeros((), jnp.int32)
    place = jnp.stack([me % 2, part, me // 2, me]).astype(jnp.int32)

    attn_out, heads = attention(cache_len, queries, kv_cache, new_kv, owners)
    heads = exchange(heads)

    out_levels, out_scale = out_levels_of(out_weight, pick_tile(out_weight.shape[1], 2560))
    heads, out_levels, out_scale = lax.optimization_barrier((heads, out_levels, out_scale))
    heads = heads.reshape(tokens, -1)
    projected = exchange(out_product(heads, out_levels, out_scale, owners))

    down = down_weight.T
    rows = gate_weight.shape[0]
    chunk = math.gcd(rows, BLOCK)
    tile = pick_tile(units, 2048)
    paired = pair_shares_blocks(rows) and down.shape[0] == rows
    weights = [gate_weight, up_weight]
    if paired:
        tops = edge_max(place, [*weights, down], units, chunk, pick_tile(units, 4096))
        tops = swap_cores(tops)
    else:
        tops = joined_max(place, weights, units, chunk, tile)
    away = rounded_weights(
        place, weights, tops, paired, 0, 1, units, chunk, pick_tile(units // 2, 1024)
    )
    gain = lax.dynamic_slice_in_dim(norm_gain, me * width_dev, width_dev, 0).astype(f32)[None]
    residual = jnp.transpose(residual_in, (1, 0, 2)).reshape(tokens, width_dev).astype(f32)
    projected, away, gain, residual = lax.optimization_barrier(
        (projected, away, gain, residual)
    )
    projected = unfold(jnp.sum(projected.astype(f32), axis=0), tokens, width_dev)
    hidden = (residual + projected).astype(bf16)

    states = [hidden]
    if parts == 2:
        states.append(lax.ppermute(hidden, "grp", [(0, 1), (1, 0)]))
    elif parts > 1:
        states = [lax.all_gather(hidden, "grp", axis=0, tiled=True)]

    def product(weights, tops):
        return gate_up_product(place, states, gain, *weights, tops, runs, chips, paired, units)

    got = [swap_cores(value) for value in product(away, None)]
    kept = list(product(weights, tops))
    half = chips // 2
    send = (kept[0][half:].astype(f32) + got[0][half:].astype(f32)).astype(bf16)
    send, kept[1], got[1] = lax.optimization_barrier((send, kept[1], got[1]))
    second = (kept[1].astype(f32) + got[1].astype(f32)).astype(bf16)
    second, place = lax.optimization_barrier((second, place))

    down_chunk = math.gcd(down.shape[0], BLOCK)
    row = 2
    if not paired:
        tops, row = joined_max(place, [down], units, down_chunk, pick_tile(units, 4096)), 0
    home, away = [
        rounded_weights(
            place, [down], tops, paired, row, flip, units, down_chunk, pick_tile(units // 2, 4096)
        )[0]
        for flip in range(2)
    ]
    last = exchange_pairs(second)
    first, (home, away) = exchange_halves(kept[0], got[0], send, (home, away))

    squares = jnp.sum(last[:, 2 * runs[1] * BLOCK :], axis=1, keepdims=True)
    scale = lax.rsqrt(squares / width + EPS_NORM)

    def act_of(summed, run):
        size = run * BLOCK
        gate = summed[:, :size] * scale
        up = summed[:, size : 2 * size] * scale
        return (jax.nn.silu(gate) * up).astype(bf16)

    act = jnp.concatenate([act_of(first, runs[0]), act_of(last, runs[1])], axis=1)
    act = exchange_chips(jnp.broadcast_to(act[None], (chips,) + act.shape))
    other = swap_cores(act)
    ffn = down_product(place, act, home, None, states, mine)
    both = down_product(place, other, away, ffn, states, mine)

    axes = ("grp", "wide") if parts > 1 else "wide"
    both = lax.all_to_all(both, axes, split_axis=0, concat_axis=0, tiled=True)
    pieces, lanes = packed(width_dev)
    both = both.reshape(parts, owners, pieces, seq_dev, steps, lanes)
    ffn, hidden_out = unpack([both[:, :, n] for n in range(pieces)], width_dev)
    if parts > 1:
        ffn = jnp.sum(ffn.astype(f32), axis=0, keepdims=True).astype(bf16)
    ffn_out = jnp.transpose(ffn[0], (2, 1, 0, 3)).reshape(steps, seq_dev, width)
    hidden_out = jnp.transpose(hidden_out[0], (2, 1, 0, 3)).reshape(steps, seq_dev, width)
    return (ffn_out, attn_out, hidden_out)


def solution(mesh):
    placed = (
        P("grp", None, "wide"),
        P(),
        P("wide", None),
        P("wide", None),
        P(None, "wide"),
        P("wide", None),
        P("grp", "wide", None, None, None),
        P(None, ("grp", "wide"), None, None, None),
        P("grp", None, "wide", None, None),
        P("grp"),
    )
    return jax.shard_map(
        on_device,
        mesh=mesh,
        in_specs=placed,
        out_specs=(
            P("grp", "wide", None),
            P("grp", "wide", None, None, None),
            P("grp", "wide", None),
        ),
        check_vma=False,
    )
```
